32 devices in a mesh: dp: 4 (over z), ctx: 8 (over y, x, core).
Axes of the slice: x: 2, y: 2, z: 4, core: 2. Of those that a mesh axis runs over, the one named last changes fastest.
Arguments:
- hidden_in: bfloat16 [4, 4096, 2048], P('dp', 'ctx'), may hold values from -6 to 6
- in_gain: bfloat16 [2048], P(('dp', 'ctx')), may hold values from 0.5 to 1.5
- w_query: bfloat16 [2048, 2048], P(('dp', 'ctx')), may hold values from -0.125 to 0.125
- b_query: bfloat16 [2048], P(('dp', 'ctx')), may hold values from -1.796875 to 1.796875
- w_key: bfloat16 [2048, 2048], P(('dp', 'ctx')), may hold values from -0.125 to 0.125
- b_key: bfloat16 [2048], P(('dp', 'ctx')), may hold values from -1.796875 to 1.796875
- w_value: bfloat16 [2048, 2048], P(('dp', 'ctx')), may hold values from -0.125 to 0.125
- b_value: bfloat16 [2048], P(('dp', 'ctx')), may hold values from -1.796875 to 1.796875
- w_out: bfloat16 [2048, 2048], P(('dp', 'ctx')), may hold values from -0.375 to 0.375
- ffn_gain: bfloat16 [2048], P(('dp', 'ctx')), may hold values from 0.5 to 1.5
- w_router: bfloat16 [2048, 8], P(('dp', 'ctx')), may hold values from -0.0625 to 0.0625
- exp_gate: bfloat16 [8, 2048, 1408], P('ctx', 'dp'), may hold values from -0.125 to 0.125
- exp_up: bfloat16 [8, 2048, 1408], P('ctx', 'dp'), may hold values from -0.125 to 0.125
- exp_down: bfloat16 [8, 1408, 2048], P('ctx', None, 'dp'), may hold values from -0.3125 to 0.3125
- sh_gate: bfloat16 [2048, 5632], P(None, ('dp', 'ctx')), may hold values from -0.125 to 0.125
- sh_up: bfloat16 [2048, 5632], P(None, ('dp', 'ctx')), may hold values from -0.125 to 0.125
- sh_down: bfloat16 [5632, 2048], P(('dp', 'ctx')), may hold values from -0.15625 to 0.15625
- sh_mix: bfloat16 [2048], P(('dp', 'ctx')), may hold values from -0.125 to 0.125
- routes: int32 [4, 4096, 4], P('dp', 'ctx'), may hold values from 0 to 7, all different within a row
- priority: int32 [4, 8, 2048], P('dp', 'ctx'), may hold values from 0 to 2047, each once within a row
- blocks: int32 [4, 16], P('dp'), may hold values from 0 to 15, as said below
- cotangent: bfloat16 [4, 4096, 2048], P('dp', 'ctx'), may hold values from -6 to 6
Outputs:
- layer_out: bfloat16 [4, 4096, 2048], P('dp', 'ctx')
- grad_input: float32 [4, 4096, 2048], P('dp', 'ctx')
- grad_ingain: float32 [2048], P(('dp', 'ctx'))
- grad_wquery: float32 [2048, 2048], P(('dp', 'ctx'))
- grad_bquery: float32 [2048], P(('dp', 'ctx'))
- grad_wkey: float32 [2048, 2048], P(('dp', 'ctx'))
- grad_bkey: float32 [2048], P(('dp', 'ctx'))
- grad_wvalue: float32 [2048, 2048], P(('dp', 'ctx'))
- grad_bvalue: float32 [2048], P(('dp', 'ctx'))
- grad_wout: float32 [2048, 2048], P(('dp', 'ctx'))
- grad_ffngain: float32 [2048], P(('dp', 'ctx'))
- grad_router: float32 [2048, 8], P(('dp', 'ctx'))
- grad_expgate: float32 [8, 2048, 1408], P('ctx', 'dp')
- grad_expup: float32 [8, 2048, 1408], P('ctx', 'dp')
- grad_expdown: float32 [8, 1408, 2048], P('ctx', None, 'dp')
- grad_shgate: float32 [2048, 5632], P(None, ('dp', 'ctx'))
- grad_shup: float32 [2048, 5632], P(None, ('dp', 'ctx'))
- grad_shdown: float32 [5632, 2048], P(('dp', 'ctx'))
- grad_shmix: float32 [2048], P(('dp', 'ctx'))
The draws below stay inside these ranges and needn't reach their ends.
Inputs may be any that keep to these rules, and one draw needn't show every extreme that they name: `blocks`: in each row, entry 2c is a block below 16/2 (prompt) and entry 2c + 1 a block of 8 or more; each row names every block once.
All inputs are finite; a program needn't handle non-finite values.
Results may differ from the reference program's by a relative error of at most 0.03.
Values may be sent and summed in bfloat16 or wider, within the bound.
A program may use at most 512 MiB of HBM per device.

```python
from functools import partial
import jax
import jax.numpy as jnp
from jax import lax

D = 2048
HEADS = 16
HEAD_DIM = 128
EXP_FF = 1408
SHARED_FF = 5632
TOP_K = 4
CONT = 256
PROMPT = 2048
GROUP_LEN = 4096
GROUPS = 4
NBLK = 16
BLOCK = 256
TOK_DEV = 512
PAIRS = 2048
EXPERTS = 8
CAP = 320
N_CTX = 8


def draw_blocks(key, part):
    key = jax.random.fold_in(key, 7)
    middle = NBLK // 2

    def one_group(group_key):
        leading_key, trailing_key = jax.random.split(group_key)
        leading = jax.random.permutation(leading_key, middle)
        trailing = jax.random.permutation(trailing_key, middle) + middle
        return jnp.stack([leading, trailing], axis=1).reshape(NBLK).astype(jnp.int32)
    return jax.vmap(one_group)(jax.random.split(key, GROUPS))


def levels(stream_key, dims, pieces, smallest, high):
    def one(axis_at, parts):
        steps = jax.random.uniform(jax.random.fold_in(jax.random.fold_in(stream_key, 6), axis_at), (parts,), jnp.float32, smallest / len(pieces), high / len(pieces))
        return jnp.repeat(jnp.exp(steps), dims[axis_at] // parts).reshape((-1,) + (1,) * (len(dims) - axis_at - 1))

    gain = one(*pieces[0])
    for cut in pieces[1:]:
        gain = gain * one(*cut)
    return gain


def picks_of(stream_key, rows, amount, top, lift):
    sequence = jax.random.permutation(jax.random.fold_in(stream_key, 1), amount)
    boost = sequence
    for power in range(3):
        boost = boost * boost // amount
    boost = boost * lift // amount
    chance = jax.random.randint(jax.random.fold_in(stream_key, 2), (rows, amount), 0, 4096) + boost
    fixed_rows = jax.random.permutation(jax.random.fold_in(stream_key, 3), rows)[jnp.arange(amount) % rows]
    chance = jnp.where(jnp.arange(rows)[:, None] == fixed_rows[None, :], 1 << 14, chance)
    score = chance * amount + jnp.arange(amount)
    return lax.top_k(score.astype(jnp.int32), top)[1].astype(jnp.int32)


def bell_draw(key, dims, deviation, reach, cuts=(), held_as=jnp.bfloat16):
    entries = jax.random.normal(key, dims, jnp.float32) * deviation
    if len(cuts) > 0:
        entries = levels(key, dims, cuts, -0.22, 0.18) * entries
    return jnp.clip(entries, min=-reach, max=reach).astype(held_as)


def setup_inputs(seed: int = 0) -> dict:
    splits = jax.random.split(jax.random.key(seed), 23)
    return {
        "hidden_in": bell_draw(splits[0], (GROUPS, GROUP_LEN, D), 1.0, 6.0, ((0, 4), (1, 8))),
        "in_gain": jnp.clip(1.0 + 0.1 * jax.random.normal(splits[1], (D,), jnp.float32), 0.5, 1.5).astype(jnp.bfloat16),
        "w_query": bell_draw(splits[2], (D, D), D ** -0.5, 0.125, ((0, 32),)),
        "b_query": bell_draw(splits[3], (D,), 0.3, 1.796875, ((0, 32),)),
        "w_key": bell_draw(splits[4], (D, D), D ** -0.5, 0.125, ((0, 32),)),
        "b_key": bell_draw(splits[5], (D,), 0.3, 1.796875, ((0, 32),)),
        "w_value": bell_draw(splits[6], (D, D), D ** -0.5, 0.125, ((0, 32),)),
        "b_value": bell_draw(splits[7], (D,), 0.3, 1.796875, ((0, 32),)),
        "w_out": bell_draw(splits[8], (D, D), (D // 8) ** -0.5, 0.375, ((0, 32),)),
        "ffn_gain": jnp.clip(1.0 + 0.1 * jax.random.normal(splits[9], (D,), jnp.float32), 0.5, 1.5).astype(jnp.bfloat16),
        "w_router": bell_draw(splits[10], (D, EXPERTS), (4 * D) ** -0.5, 0.0625, ((0, 32),)),
        "exp_gate": bell_draw(splits[11], (EXPERTS, D, EXP_FF), D ** -0.5, 0.125, ((0, 8), (1, 4))),
        "exp_up": bell_draw(splits[12], (EXPERTS, D, EXP_FF), D ** -0.5, 0.125, ((0, 8), (1, 4))),
        "exp_down": bell_draw(splits[13], (EXPERTS, EXP_FF, D), (EXP_FF // 4) ** -0.5, 0.3125, ((0, 8), (2, 4))),
        "sh_gate": bell_draw(splits[14], (D, SHARED_FF), D ** -0.5, 0.125, ((1, 32),)),
        "sh_up": bell_draw(splits[15], (D, SHARED_FF), D ** -0.5, 0.125, ((1, 32),)),
        "sh_down": bell_draw(splits[16], (SHARED_FF, D), (SHARED_FF // 4) ** -0.5, 0.15625, ((0, 32),)),
        "sh_mix": bell_draw(splits[17], (D,), D ** -0.5, 0.125, ((0, 32),)),
        "routes": picks_of(splits[18], GROUPS * GROUP_LEN, EXPERTS, TOP_K, 4096).reshape((GROUPS, GROUP_LEN, TOP_K)),
        "priority": jax.vmap(lambda own: jax.random.permutation(own, PAIRS))(jax.random.split(splits[19], GROUPS * N_CTX)).reshape((GROUPS, N_CTX, PAIRS)).astype(jnp.int32),
        "blocks": draw_blocks(jax.random.fold_in(splits[22], 71), 0),
        "cotangent": bell_draw(splits[21], (GROUPS, GROUP_LEN, D), 1.0, 6.0, ((0, 4), (1, 8))),
    }


rope_base = 1000000.0
epsilon = 1e-06
masked_score = -1e+30

@jax.custom_vjp
def low(v):
    return lax.optimization_barrier(v.astype(jnp.bfloat16)).astype(jnp.float32)

@jax.custom_vjp
def low_back(v):
    return v

def low_keep(v):
    return (low(v), None)

def low_pass(kept, grad):
    return (grad,)

def back_keep(v):
    return (v, None)

def back_low(kept, grad):
    return (low(grad),)
low.defvjp(low_keep, low_pass)
low_back.defvjp(back_keep, back_low)

def matmul(left, right):
    return jnp.dot(left, right, precision=lax.Precision.HIGHEST)

def rms_scale(values):
    return lax.rsqrt(lax.optimization_barrier(jnp.mean(values * values, axis=-1, keepdims=True)) + epsilon)

def rotate(values, cosine, sine):
    middle = values.shape[-1] // 2
    leading = values[..., :middle]
    trailing = values[..., middle:]
    return jnp.concatenate([leading * cosine - trailing * sine, trailing * cosine + leading * sine], axis=-1)

def token_places(block_row):
    within = jnp.arange(BLOCK, dtype=jnp.int32)
    return (block_row[:, None] * BLOCK + within[None, :]).reshape(-1)

def rope_tables(places):
    turned = jnp.where(places < PROMPT, places, PROMPT + (places - PROMPT) % CONT)
    frequency = rope_base ** (-2.0 * jnp.arange(HEAD_DIM // 2, dtype=jnp.float32) / HEAD_DIM)
    angles = turned.astype(jnp.float32)[:, None] * frequency[None, :]
    return (jnp.cos(angles)[:, None, :], jnp.sin(angles)[:, None, :])

def segment_of(places):
    return jnp.where(places < PROMPT, 0, 1 + (places - PROMPT) // CONT)

def visible(query_places, key_places):
    query_segment = segment_of(query_places)
    key_segment = segment_of(key_places)
    causal = key_places[None, :] <= query_places[:, None]
    same_doc = (key_segment[None, :] == 0) | (key_segment[None, :] == query_segment[:, None])
    return causal & same_doc

def local_ranks(expert_ids, order):
    flat_ids = expert_ids.reshape(-1)
    arranged = jnp.zeros(flat_ids.shape, jnp.int32).at[order].set(flat_ids)
    member = (arranged[:, None] == jnp.arange(EXPERTS, dtype=jnp.int32)[None, :]).astype(jnp.int32)
    before = jnp.cumsum(member, axis=0) - member
    sorted_positions = lax.optimization_barrier(jnp.sum(before * member, axis=1))
    return sorted_positions[order].reshape(expert_ids.shape)

def head_attend(allowed, inputs):
    query_head, key_head, value_head = inputs
    scores = low_back(matmul(query_head, key_head.T) * HEAD_DIM ** (-0.5))
    scores = jnp.where(allowed, scores, masked_score)
    highest = lax.optimization_barrier(jnp.max(scores, axis=-1, keepdims=True))
    weight_collection = jnp.exp(scores - highest)
    probs_low = low(weight_collection / lax.optimization_barrier(jnp.sum(weight_collection, axis=-1, keepdims=True)))
    return low_back(matmul(probs_low, value_head))

def layer_group(weight_set, hidden, allowed, cosine, sine, routes_group, slots, table):
    in_gain, w_query, b_query, w_key, b_key, w_value, b_value, w_out, ffn_gain, w_router, exp_gate, exp_up, exp_down, sh_gate, sh_up, sh_down, sh_mix = weight_set
    head_shape = (GROUP_LEN, HEADS, HEAD_DIM)
    normed_one = low(hidden * rms_scale(hidden) * in_gain)
    query_rot = low(rotate(low_back(matmul(normed_one, w_query) + b_query).reshape(head_shape), cosine, sine))
    key_rot = low(rotate(low_back(matmul(normed_one, w_key) + b_key).reshape(head_shape), cosine, sine))
    value_rows = low(low_back(matmul(normed_one, w_value) + b_value)).reshape(head_shape)
    heads_out = lax.map(jax.checkpoint(partial(head_attend, allowed)), (query_rot.transpose(1, 0, 2), key_rot.transpose(1, 0, 2), value_rows.transpose(1, 0, 2)))
    attended = low(heads_out).transpose(1, 0, 2).reshape(GROUP_LEN, D)
    first_sum = hidden + low_back(matmul(attended, w_out))
    normed_two = low(first_sum * rms_scale(first_sum) * ffn_gain)
    logits = low_back(matmul(normed_two, w_router))
    chosen = jnp.take_along_axis(logits, routes_group, axis=1)
    gates = jax.nn.softmax(chosen, axis=-1)
    per_device = normed_two.reshape(N_CTX, TOK_DEV, D)
    sent = low_back(jnp.einsum('cst,ctd->csd', table, per_device, precision=lax.Precision.HIGHEST))
    slot_rows = sent.reshape(N_CTX, EXPERTS, CAP, D)
    gate_act = low_back(jnp.einsum('cerd,edf->cerf', slot_rows, exp_gate, precision=lax.Precision.HIGHEST))
    up_act = low_back(jnp.einsum('cerd,edf->cerf', slot_rows, exp_up, precision=lax.Precision.HIGHEST))
    hidden_act = low(jax.nn.silu(gate_act) * up_act)
    expert_out = low(low_back(jnp.einsum('cerf,efd->cerd', hidden_act, exp_down, precision=lax.Precision.HIGHEST)))
    expert_out = expert_out.reshape(N_CTX, EXPERTS * CAP, D)
    padded = jnp.concatenate([expert_out, jnp.zeros((N_CTX, 1, D), expert_out.dtype)], axis=1)
    picked = jnp.take_along_axis(padded, slots.reshape(N_CTX, PAIRS)[:, :, None], axis=1).reshape(GROUP_LEN, TOP_K, D)
    experts_sum = lax.optimization_barrier(jnp.sum(gates[:, :, None] * picked, axis=1))
    shared_g = low_back(matmul(normed_two, sh_gate))
    shared_u = low_back(matmul(normed_two, sh_up))
    shared_act = low(jax.nn.silu(shared_g) * shared_u)
    shared_sum = low_back(matmul(shared_act, sh_down))
    mixing = jax.nn.sigmoid(matmul(normed_two, sh_mix))
    return first_sum + experts_sum + mixing[:, None] * shared_sum

def reference(hidden_in, in_gain, w_query, b_query, w_key, b_key, w_value, b_value, w_out, ffn_gain, w_router, exp_gate, exp_up, exp_down, sh_gate, sh_up, sh_down, sh_mix, routes, priority, blocks, cotangent):
    weight_set = tuple((weight_item.astype(jnp.float32) for weight_item in (in_gain, w_query, b_query, w_key, b_key, w_value, b_value, w_out, ffn_gain, w_router, exp_gate, exp_up, exp_down, sh_gate, sh_up, sh_down, sh_mix)))

    def group_step(totals, inputs):
        hidden, routes_group, order_group, block_row, cot_group = inputs
        places = token_places(block_row)
        cosine, sine = rope_tables(places)
        allowed = visible(places, places)
        routes_dev = routes_group.reshape(N_CTX, TOK_DEV, TOP_K)
        ranks = jax.vmap(local_ranks)(routes_dev, order_group)
        slots = jnp.where(ranks < CAP, routes_dev * CAP + ranks, EXPERTS * CAP).astype(jnp.int32)
        slot_grid = jnp.arange(EXPERTS * CAP, dtype=jnp.int32)
        table = jnp.any(slots[:, None, :, :] == slot_grid[None, :, None, None], axis=3).astype(jnp.float32)

        def forward(weights_now, hidden_now):
            return layer_group(weights_now, hidden_now, allowed, cosine, sine, routes_group, slots, table)
        output, backward_function = jax.vjp(forward, weight_set, hidden.astype(jnp.float32))
        grad_weights, grad_hidden = backward_function(cot_group.astype(jnp.float32))
        totals = jax.tree.map(jnp.add, totals, grad_weights)
        return (totals, (output.astype(jnp.bfloat16), grad_hidden))
    zeros = tuple((jnp.zeros_like(weight_item) for weight_item in weight_set))
    totals, (outputs, grad_inputs) = lax.scan(group_step, zeros, (hidden_in, routes, priority, blocks, cotangent))
    return (outputs, grad_inputs, totals[0], totals[1], totals[2], totals[3], totals[4], totals[5], totals[6], totals[7], totals[8], totals[9], totals[10], totals[11], totals[12], totals[13], totals[14], totals[15], totals[16])
```

```python
import functools

import jax
import jax.numpy as jnp
from jax import lax
from jax.experimental import pallas as pl
from jax.experimental.pallas import tpu as pltpu
from jax.sharding import PartitionSpec as P

D = 2048
HEADS = 16
HEAD_DIM = 128
TOP_K = 4
CONT = 256
PROMPT = 2048

rope_base = 1000000.0
epsilon = 1e-06
masked_score = -1e30
log2_e = 1.4426950408889634
low = jnp.bfloat16
full = jnp.float32


def dot(left, right):
    return jnp.dot(left, right, preferred_element_type=full)


def dot_nt(left, right):
    return lax.dot_general(left, right, (((1,), (1,)), ((), ())), preferred_element_type=full)


def ein(spec, left, right):
    return jnp.einsum(spec, left, right, preferred_element_type=full)


def rotate(values, cosine, sine):
    middle = values.shape[-1] // 2
    leading = values[..., :middle]
    trailing = values[..., middle:]
    return jnp.concatenate(
        [leading * cosine - trailing * sine, trailing * cosine + leading * sine], axis=-1
    )


def rope_tables(places):
    turned = jnp.where(places < PROMPT, places, PROMPT + (places - PROMPT) % CONT)
    frequency = rope_base ** (-2.0 * jnp.arange(HEAD_DIM // 2, dtype=full) / HEAD_DIM)
    angles = turned.astype(full)[:, None] * frequency[None, :]
    return (jnp.cos(angles)[:, None, :], jnp.sin(angles)[:, None, :])


def rms_scale(values):
    return lax.rsqrt(jnp.mean(values * values, axis=-1, keepdims=True) + epsilon)


def norm_back(values, scale_rows, gain_row, upstream):
    weighted = upstream * gain_row
    grad_gain = jnp.sum(upstream * values * scale_rows, axis=0)
    grad_values = scale_rows * weighted - values * scale_rows**3 * jnp.mean(
        weighted * values, axis=-1, keepdims=True
    )
    return (grad_values, grad_gain)


def silu_parts(values):
    sig_value = jax.nn.sigmoid(values)
    return (values * sig_value, sig_value * (1.0 + values * (1.0 - sig_value)))


WIDE = 4


def attend_tiles(index, chunk, carry):
    whole = jnp.minimum(index, PROMPT // CONT)
    wide = whole // WIDE
    carry = lax.fori_loop(
        0, wide, lambda step, c: chunk(step * (WIDE * CONT), WIDE * CONT, False, c), carry
    )
    carry = lax.fori_loop(
        wide * WIDE, whole, lambda step, c: chunk(step * CONT, CONT, False, c), carry
    )
    return chunk(index * CONT, CONT, True, carry)


def forward_kernel(q_ref, k_ref, vt_ref, o_ref, lse_ref):
    index = pl.program_id(1)
    query = q_ref[...]
    score_scale = HEAD_DIM ** (-0.5) * log2_e

    def chunk(start, size, diagonal, carry):
        highest, total, acc = carry
        start = pl.multiple_of(start, CONT)
        scores = dot_nt(k_ref[pl.ds(start, size), :], query) * score_scale
        if diagonal:
            keys = lax.broadcasted_iota(jnp.int32, scores.shape, 0)
            queries = lax.broadcasted_iota(jnp.int32, scores.shape, 1)
            scores = jnp.where(keys <= queries, scores, masked_score)
        newest = jnp.maximum(highest, jnp.max(scores, axis=0, keepdims=True))
        weights = jnp.exp2(scores - newest)
        shrink = jnp.exp2(highest - newest)
        total = total * shrink + jnp.sum(weights, axis=0, keepdims=True)
        acc = acc * shrink + dot(vt_ref[:, pl.ds(start, size)], weights.astype(low))
        return (newest, total, acc)

    highest, total, acc = attend_tiles(
        index,
        chunk,
        (
            jnp.full((1, CONT), masked_score, full),
            jnp.zeros((1, CONT), full),
            jnp.zeros((HEAD_DIM, CONT), full),
        ),
    )
    o_ref[...] = (acc / total).T.astype(low)
    lse_ref[...] = (highest + jnp.log2(total))[None]


def attention_forward(query, key, value_t):
    rows, width = query.shape
    heads = width // HEAD_DIM
    tile = pl.BlockSpec((CONT, HEAD_DIM), lambda h, i: (i, h))
    return pl.pallas_call(
        forward_kernel,
        grid=(heads, rows // CONT),
        in_specs=[
            tile,
            pl.BlockSpec((rows, HEAD_DIM), lambda h, i: (0, h)),
            pl.BlockSpec((HEAD_DIM, rows), lambda h, i: (h, 0)),
        ],
        out_specs=[tile, pl.BlockSpec((1, 1, CONT), lambda h, i: (h, 0, i))],
        out_shape=[
            jax.ShapeDtypeStruct((rows, width), low),
            jax.ShapeDtypeStruct((heads, 1, rows), full),
        ],
        compiler_params=pltpu.CompilerParams(vmem_limit_bytes=48 * 2**20),
        name="attend_forward",
    )(query, key, value_t)


def backward_kernel(
    q_ref, do_ref, lse_ref, delta_ref, k_ref, kt_ref, v_ref, dq_ref, dk_ref, dv_ref
):
    index = pl.program_id(1)
    query = q_ref[...]
    upstream = do_ref[...]
    lse = lse_ref[0]
    delta = delta_ref[0]
    scale = HEAD_DIM ** (-0.5)

    @pl.when(index == 0)
    def _():
        dk_ref[...] = jnp.zeros_like(dk_ref)
        dv_ref[...] = jnp.zeros_like(dv_ref)

    def chunk(start, size, diagonal, acc):
        start = pl.multiple_of(start, CONT)
        span = pl.ds(start, size)
        scores = dot_nt(k_ref[span, :], query) * (scale * log2_e) - lse
        if diagonal:
            keys = lax.broadcasted_iota(jnp.int32, scores.shape, 0)
            queries = lax.broadcasted_iota(jnp.int32, scores.shape, 1)
            scores = jnp.where(keys <= queries, scores, masked_score)
        probs = jnp.exp2(scores)
        prob_grad = dot_nt(v_ref[span, :], upstream)
        score_grad = (probs * (prob_grad - delta)).astype(low)
        dv_ref[span, :] += dot(probs.astype(low), upstream)
        dk_ref[span, :] += dot(score_grad, query) * scale
        return acc + dot(kt_ref[:, span], score_grad)

    acc = attend_tiles(index, chunk, jnp.zeros((HEAD_DIM, CONT), full))
    dq_ref[...] = acc.T * scale


def attention_backward(query, upstream, lse, delta, key, key_t, value):
    rows, width = query.shape
    heads = width // HEAD_DIM
    tile = pl.BlockSpec((CONT, HEAD_DIM), lambda h, i: (i, h))
    line = pl.BlockSpec((1, 1, CONT), lambda h, i: (h, 0, i))
    whole = pl.BlockSpec((rows, HEAD_DIM), lambda h, i: (0, h))
    grad = jax.ShapeDtypeStruct((rows, width), full)
    return pl.pallas_call(
        backward_kernel,
        grid=(heads, rows // CONT),
        in_specs=[
            tile,
            tile,
            line,
            line,
            whole,
            pl.BlockSpec((HEAD_DIM, rows), lambda h, i: (h, 0)),
            whole,
        ],
        out_specs=[tile, whole, whole],
        out_shape=[grad, grad, grad],
        compiler_params=pltpu.CompilerParams(vmem_limit_bytes=48 * 2**20),
        name="attend_backward",
    )(query, upstream, lse, delta, key, key_t, value)


def take_blocks(rows, order):
    count = order.shape[0]
    blocked = rows.reshape(count, rows.shape[0] // count, *rows.shape[1:])
    return jnp.concatenate(
        [lax.dynamic_index_in_dim(blocked, order[i], 0, keepdims=False) for i in range(count)], axis=0
    )


def gather_ctx(values):
    return lax.all_gather(values, "ctx", axis=0, tiled=True)


def scatter_ctx(values):
    return lax.psum_scatter(values, "ctx", scatter_dimension=0, tiled=True)


def swap_ctx(values):
    return lax.all_to_all(values, "ctx", split_axis=0, concat_axis=0, tiled=True)


def on_device(
    hidden_in,
    in_gain,
    w_query,
    b_query,
    w_key,
    b_key,
    w_value,
    b_value,
    w_out,
    ffn_gain,
    w_router,
    exp_gate,
    exp_up,
    exp_down,
    sh_gate,
    sh_up,
    sh_down,
    sh_mix,
    routes,
    priority,
    blocks,
    cotangent,
):
    both = ("dp", "ctx")
    ctx_count = lax.axis_size("ctx")
    ctx_index = lax.axis_index("ctx")
    dp_count = lax.axis_size("dp")
    tokens_low = hidden_in[0]
    tokens = tokens_low.astype(full)
    cot_low = cotangent[0]
    cot_full = cot_low.astype(full)
    tok_count = tokens.shape[0]
    group_len = tok_count * ctx_count
    shard = w_query.shape[0]
    experts_total = ctx_count * exp_gate.shape[0]
    capacity = 5 * tok_count * TOP_K // (4 * experts_total)
    repeat = max(1, ctx_count // HEADS)
    heads = max(1, HEADS // ctx_count)
    width = heads * HEAD_DIM
    head_sets = HEADS // heads

    def by_heads(weight):
        parts = weight.reshape(shard, head_sets, width).transpose(1, 0, 2)
        return jnp.repeat(parts, repeat, axis=0) if repeat > 1 else parts

    qkv_parts = swap_ctx(
        jnp.concatenate([by_heads(w_query), by_heads(w_key), by_heads(w_value)], axis=2)
    )
    w_qkv = lax.all_gather(
        qkv_parts.reshape(ctx_count * shard, 3 * width), "dp", axis=0, tiled=True
    )
    x_all = gather_ctx(tokens_low)
    small = jnp.concatenate(
        [
            jnp.stack([in_gain, b_query, b_key, b_value, ffn_gain, sh_mix], axis=0),
            w_router.T,
        ],
        axis=0,
    )
    small_all = (
        lax.all_gather(small, both, axis=0)
        .transpose(1, 0, 2)
        .reshape(small.shape[0], shard * dp_count * ctx_count)
        .astype(full)
    )
    gain_one, gain_two, mix_row = small_all[0:1], small_all[4:5], small_all[5:6]
    mix_router = small_all[5:].astype(low)
    out_full = lax.all_gather(w_out, both, axis=0, tiled=True)
    cot_all = gather_ctx(cot_low)
    shared_gate, shared_up, shared_down = (
        lax.all_gather(sh_gate, "dp", axis=1, tiled=True),
        lax.all_gather(sh_up, "dp", axis=1, tiled=True),
        lax.all_gather(sh_down, "dp", axis=0, tiled=True),
    )
    expert_gate, expert_up, expert_down = (
        lax.all_gather(exp_gate[0], "dp", axis=0, tiled=True),
        lax.all_gather(exp_up[0], "dp", axis=0, tiled=True),
        lax.all_gather(exp_down[0], "dp", axis=1, tiled=True),
    )

    route_ids = routes[0]
    flat_ids = route_ids.reshape(-1)
    order = priority[0, 0]
    earlier = (flat_ids[:, None] == flat_ids[None, :]) & (order[None, :] < order[:, None])
    ranks = jnp.sum(earlier.astype(jnp.int32), axis=1).reshape(route_ids.shape)
    expert_grid = jnp.arange(experts_total, dtype=jnp.int32)
    route_hits = route_ids[None, :, :] == expert_grid[:, None, None]
    code = jnp.sum(jnp.where(route_hits, ranks[None] + 1, 0), axis=2) - 1
    code_all = lax.all_gather(code, "ctx", axis=0)

    stored_to_place = blocks[0]
    block_count = stored_to_place.shape[0]
    block_grid = jnp.arange(block_count, dtype=jnp.int32)
    place_to_stored = jnp.sum(
        jnp.where(stored_to_place[None, :] == block_grid[:, None], block_grid[None, :], 0), axis=1
    )
    cosine, sine = rope_tables(jnp.arange(group_len, dtype=jnp.int32))
    my_heads = (ctx_index // repeat) * width
    x_sorted = take_blocks(x_all, place_to_stored).astype(full)
    scale_sorted = rms_scale(x_sorted)
    normed_sorted = (x_sorted * scale_sorted * gain_one).astype(low)
    bias = lax.dynamic_slice_in_dim(small_all[1:4], my_heads, width, 1)
    head_shape = (group_len, heads, HEAD_DIM)
    projected = dot(normed_sorted, w_qkv)

    def part(index):
        return projected[:, index * width : (index + 1) * width] + bias[index : index + 1]

    query = rotate(part(0).reshape(head_shape), cosine, sine).reshape(group_len, width).astype(low)
    key = rotate(part(1).reshape(head_shape), cosine, sine).reshape(group_len, width).astype(low)
    value = part(2).astype(low)
    attended_heads, lse = attention_forward(query, key, value.T)
    attended_parts = swap_ctx(
        take_blocks(attended_heads, stored_to_place).reshape(ctx_count, tok_count, width)
    )[::repeat]
    attended = attended_parts.transpose(1, 0, 2).reshape(tok_count, D)
    first_sum = tokens + dot(attended, out_full)
    scale_two = rms_scale(first_sum)
    normed_two = (first_sum * scale_two * gain_two).astype(low)
    all_normed = gather_ctx(normed_two)

    logits_all = dot_nt(all_normed, mix_router)
    mix_all = jax.nn.sigmoid(logits_all[:, 0:1])
    chosen = code_all.transpose(0, 2, 1).reshape(group_len, experts_total) >= 0
    masked = jnp.where(chosen, logits_all[:, 1:], masked_score)
    raised = jnp.where(chosen, jnp.exp(masked - jnp.max(masked, axis=1, keepdims=True)), 0.0)
    gates_all = raised / jnp.sum(raised, axis=1, keepdims=True)
    is_mine = (expert_grid == ctx_index).astype(full)
    gate_mine = jnp.sum(gates_all * is_mine[None, :], axis=1).reshape(ctx_count, tok_count)
    code_mine = lax.dynamic_index_in_dim(code_all, ctx_index, 1, keepdims=False)
    slot_grid = jnp.arange(capacity, dtype=jnp.int32)
    hits = code_mine[:, None, :] == slot_grid[None, :, None]
    table = hits.astype(low)
    gated_table = jnp.where(hits, gate_mine[:, None, :], 0.0)
    slot_gates = jnp.sum(gated_table, axis=2)
    grouped = (ctx_count, tok_count, D)
    slots = ctx_count * capacity
    expert_rows = ein("crt,ctd->crd", table, all_normed.reshape(grouped)).astype(low)
    expert_rows = expert_rows.reshape(slots, D)
    slot_grads = (
        ein("crt,ctd->crd", table, cot_all.reshape(grouped)) * slot_gates[:, :, None]
    ).astype(low)
    slot_grads = slot_grads.reshape(slots, D)

    shared_g = dot(all_normed, shared_gate)
    shared_u = dot(all_normed, shared_up)
    shared_silu, shared_slope = silu_parts(shared_g)
    shared_low = (shared_silu * shared_u).astype(low)
    mix_cot = (mix_all * cot_all.astype(full)).astype(low)
    shared_hidden = dot_nt(mix_cot, shared_down)
    shared_dg = (shared_hidden * shared_u * shared_slope).astype(low)
    shared_du = (shared_hidden * shared_silu).astype(low)
    mix_share = jnp.sum(shared_hidden * shared_silu * shared_u, axis=1)
    grad_sgate = ein("td,tf->df", all_normed, shared_dg)
    grad_sup = ein("td,tf->df", all_normed, shared_du)
    grad_sdown = ein("tf,td->fd", shared_low, mix_cot)

    gate_act = dot(expert_rows, expert_gate)
    up_act = dot(expert_rows, expert_up)
    gate_silu, gate_slope = silu_parts(gate_act)
    hidden_low = (gate_silu * up_act).astype(low)
    hidden_grad = dot_nt(slot_grads, expert_down)
    gate_grad = (hidden_grad * up_act * gate_slope).astype(low)
    up_grad = (hidden_grad * gate_silu).astype(low)
    gate_share = jnp.sum(hidden_grad * gate_silu * up_act, axis=1).reshape(ctx_count, capacity)
    expert_dx = (dot_nt(gate_grad, expert_gate) + dot_nt(up_grad, expert_up)).astype(low)
    partial_dx = (
        dot_nt(shared_dg, shared_gate)
        + dot_nt(shared_du, shared_up)
        + ein("crt,crd->ctd", table, expert_dx.reshape(ctx_count, capacity, D)).reshape(
            group_len, D
        )
    )
    dx_mine = scatter_ctx(partial_dx.astype(low)).astype(full)
    expert_out = dot(hidden_low, expert_down).astype(low)
    partial_out = mix_all * dot(shared_low, shared_down) + ein(
        "crt,crd->ctd", gated_table.astype(low), expert_out.reshape(ctx_count, capacity, D)
    ).reshape(group_len, D)
    layer_out = first_sum + scatter_ctx(partial_out.astype(low)).astype(full)
    grad_edown = ein("rf,rd->fd", hidden_low, slot_grads)
    grad_egate = ein("rd,rf->df", expert_rows, gate_grad)
    grad_eup = ein("rd,rf->df", expert_rows, up_grad)

    share_of_token = jnp.sum(jnp.where(hits, gate_share[:, :, None], 0.0), axis=1)
    shares = swap_ctx(jnp.stack([share_of_token, mix_share.reshape(ctx_count, tok_count)], axis=1))
    gates_mine = lax.dynamic_slice_in_dim(gates_all, ctx_index * tok_count, tok_count)
    mix_mine = lax.dynamic_slice_in_dim(mix_all, ctx_index * tok_count, tok_count)
    gate_shares = shares[:, 0].T
    mix_grad = jnp.sum(shares[:, 1], axis=0)[:, None] * (1.0 - mix_mine)
    logit_grad = gate_shares - gates_mine * jnp.sum(gate_shares, axis=1, keepdims=True)
    narrow_grad = jnp.concatenate([mix_grad, logit_grad], axis=1)
    narrow_low = logit_grad.astype(low)
    grad_narrow = jnp.concatenate(
        [
            jnp.sum(mix_grad * normed_two.astype(full), axis=0, keepdims=True),
            ein("te,td->ed", narrow_low, normed_two),
        ],
        axis=0,
    )
    normed_grad = dx_mine + mix_grad * mix_row + dot(narrow_low, mix_router[1:])
    norm_grad_two, grad_gain_two = norm_back(first_sum, scale_two, gain_two, normed_grad)
    first_grad = cot_full + norm_grad_two
    first_low = first_grad.astype(low)
    attended_grad = dot_nt(first_low, out_full).astype(low)
    grad_out = ein("td,te->de", attended, first_low)

    upstream_parts = attended_grad.reshape(tok_count, head_sets, width).transpose(1, 0, 2)
    if repeat > 1:
        upstream_parts = jnp.repeat(upstream_parts, repeat, axis=0)
    upstream = take_blocks(swap_ctx(upstream_parts).reshape(group_len, width), place_to_stored)
    delta = jnp.sum(
        (upstream.astype(full) * attended_heads.astype(full)).reshape(head_shape), axis=2
    ).T.reshape(heads, 1, group_len)
    query_grad, key_grad, value_grad = attention_backward(
        query, upstream, lse, delta, key, key.T, value
    )
    qkv_grad = jnp.concatenate(
        [
            rotate(query_grad.reshape(head_shape), cosine, -sine).reshape(group_len, width),
            rotate(key_grad.reshape(head_shape), cosine, -sine).reshape(group_len, width),
            value_grad,
        ],
        axis=1,
    ).astype(low)
    if repeat > 1:
        qkv_grad = jnp.where(ctx_index % repeat == 0, qkv_grad, jnp.zeros_like(qkv_grad))
    partial_one = dot_nt(qkv_grad, w_qkv).astype(low)
    grad_qkv = ein("td,te->de", normed_sorted, qkv_grad)
    bias_sums = jnp.sum(qkv_grad.astype(full), axis=0).reshape(3, width)
    grad_bias = lax.dynamic_update_slice_in_dim(
        jnp.zeros((3, D), full), bias_sums, my_heads, 1
    )
    dx_one = scatter_ctx(take_blocks(partial_one, stored_to_place)).astype(full)
    norm_grad_one, grad_gain_one = norm_back(tokens, rms_scale(tokens), gain_one, dx_one)
    input_grad = first_grad + norm_grad_one

    qkv_rows = lax.psum_scatter(
        grad_qkv.astype(low).reshape(dp_count, ctx_count, shard, 3 * width),
        "dp",
        scatter_dimension=0,
        tiled=True,
    )[0]
    qkv_mine = swap_ctx(qkv_rows)[::repeat].astype(full)
    qkv_mine = qkv_mine.reshape(head_sets, shard, 3, width).transpose(2, 1, 0, 3).reshape(3, shard, D)
    grad_wout = lax.psum_scatter(
        grad_out.astype(low), both, scatter_dimension=0, tiled=True
    ).astype(full)
    small_grads = lax.psum_scatter(
        jnp.concatenate([grad_gain_one[None], grad_bias, grad_gain_two[None], grad_narrow], axis=0).T,
        both,
        scatter_dimension=0,
        tiled=True,
    )

    def over_dp(grad, dim):
        return lax.psum_scatter(
            grad.astype(low), "dp", scatter_dimension=dim, tiled=True
        ).astype(full)

    return (
        layer_out.astype(low)[None],
        input_grad[None],
        small_grads[:, 0],
        qkv_mine[0],
        small_grads[:, 1],
        qkv_mine[1],
        small_grads[:, 2],
        qkv_mine[2],
        small_grads[:, 3],
        grad_wout,
        small_grads[:, 4],
        small_grads[:, 6:],
        over_dp(grad_egate, 0)[None],
        over_dp(grad_eup, 0)[None],
        over_dp(grad_edown, 1)[None],
        over_dp(grad_sgate, 1),
        over_dp(grad_sup, 1),
        over_dp(grad_sdown, 0),
        small_grads[:, 5],
    )


def solution(mesh):
    rows = P("dp", "ctx", None)
    flat = P(("dp", "ctx"))
    lines = P(("dp", "ctx"), None)
    columns = P(None, ("dp", "ctx"))
    deep = P("ctx", "dp", None)
    down = P("ctx", None, "dp")
    in_specs = (
        (rows, flat, lines, flat, lines, flat, lines, flat, lines, flat, lines)
        + (deep, deep, down, columns, columns, lines, flat)
        + (rows, rows, P("dp", None), rows)
    )
    out_specs = (
        (rows, rows, flat, lines, flat, lines, flat, lines, flat, lines, flat, lines)
        + (deep, deep, down, columns, columns, lines, flat)
    )
    return jax.shard_map(
        on_device, mesh=mesh, in_specs=in_specs, out_specs=out_specs, check_vma=False
    )
```

```python
import functools

import jax
import jax.numpy as jnp
from jax import lax
from jax.experimental import pallas as pl
from jax.experimental.pallas import tpu as pltpu
from jax.sharding import PartitionSpec as P

D = 2048
HEADS = 16
HEAD_DIM = 128
TOP_K = 4
CONT = 256
PROMPT = 2048

rope_base = 1000000.0
epsilon = 1e-06
masked_score = -1e30
log2_e = 1.4426950408889634
low = jnp.bfloat16
full = jnp.float32


def dot(left, right):
    return jnp.dot(left, right, preferred_element_type=full)


def dot_nt(left, right):
    return lax.dot_general(left, right, (((1,), (1,)), ((), ())), preferred_element_type=full)


def ein(spec, left, right):
    return jnp.einsum(spec, left, right, preferred_element_type=full)


def rotate(values, cosine, sine):
    middle = values.shape[-1] // 2
    leading = values[..., :middle]
    trailing = values[..., middle:]
    return jnp.concatenate(
        [leading * cosine - trailing * sine, trailing * cosine + leading * sine], axis=-1
    )


def rope_tables(places):
    turned = jnp.where(places < PROMPT, places, PROMPT + (places - PROMPT) % CONT)
    frequency = rope_base ** (-2.0 * jnp.arange(HEAD_DIM // 2, dtype=full) / HEAD_DIM)
    angles = turned.astype(full)[:, None] * frequency[None, :]
    return (jnp.cos(angles)[:, None, :], jnp.sin(angles)[:, None, :])


def rms_scale(values):
    return lax.rsqrt(jnp.mean(values * values, axis=-1, keepdims=True) + epsilon)


def norm_back(values, scale_rows, gain_row, upstream):
    weighted = upstream * gain_row
    grad_gain = jnp.sum(upstream * values * scale_rows, axis=0)
    grad_values = scale_rows * weighted - values * scale_rows**3 * jnp.mean(
        weighted * values, axis=-1, keepdims=True
    )
    return (grad_values, grad_gain)


def silu_parts(values):
    sig_value = jax.nn.sigmoid(values)
    return (values * sig_value, sig_value * (1.0 + values * (1.0 - sig_value)))


WIDE = 4


def attend_tiles(index, chunk, carry):
    whole = jnp.minimum(index, PROMPT // CONT)
    wide = whole // WIDE
    carry = lax.fori_loop(
        0, wide, lambda step, c: chunk(step * (WIDE * CONT), WIDE * CONT, False, c), carry
    )
    carry = lax.fori_loop(
        wide * WIDE, whole, lambda step, c: chunk(step * CONT, CONT, False, c), carry
    )
    return chunk(index * CONT, CONT, True, carry)


def turn(values, cosine, sine):
    half = HEAD_DIM // 2
    swapped = jnp.concatenate([values[:, half:], values[:, :half]], axis=1)
    return values * cosine + swapped * sine


def project_kernel(
    place_ref, x_ref, gain_ref, w_ref, bias_ref, cos_ref, sin_ref, normed_ref, q_ref, k_ref, v_ref
):
    values = x_ref[0].astype(full)
    scale = lax.rsqrt(jnp.mean(values * values, axis=1, keepdims=True) + epsilon)
    normed = (values * scale * gain_ref[...]).astype(low)
    normed_ref[...] = normed
    width = q_ref.shape[1]
    projected = dot(normed, w_ref[...]) + bias_ref[...]
    cosine, sine = cos_ref[...], sin_ref[...]
    for start in range(0, width, HEAD_DIM):
        for kind, out in ((0, q_ref), (1, k_ref)):
            column = kind * width + start
            head = projected[:, column : column + HEAD_DIM]
            out[:, start : start + HEAD_DIM] = turn(head, cosine, sine).astype(low)
    v_ref[...] = projected[:, 2 * width :].astype(low)


def project(x_blocks, places, gain, weight, bias, cosine, sine):
    count, rows, _ = x_blocks.shape
    width = weight.shape[1] // 3
    at_place = lambda g, place: (place[g], 0)
    whole = lambda g, place: (0, 0)
    tile = pl.BlockSpec((rows, width), at_place)
    head = jax.ShapeDtypeStruct((count * rows, width), low)
    return pl.pallas_call(
        project_kernel,
        grid_spec=pltpu.PrefetchScalarGridSpec(
            num_scalar_prefetch=1,
            grid=(count,),
            in_specs=[
                pl.BlockSpec((1, rows, D), lambda g, place: (g, 0, 0)),
                pl.BlockSpec((1, D), whole),
                pl.BlockSpec((D, 3 * width), whole),
                pl.BlockSpec((1, 3 * width), whole),
                pl.BlockSpec((rows, HEAD_DIM), at_place),
                pl.BlockSpec((rows, HEAD_DIM), at_place),
            ],
            out_specs=[pl.BlockSpec((rows, D), at_place), tile, tile, tile],
        ),
        out_shape=[jax.ShapeDtypeStruct((count * rows, D), low), head, head, head],
        compiler_params=pltpu.CompilerParams(vmem_limit_bytes=40 * 2**20),
        name="project",
    )(places, x_blocks, gain, weight, bias, cosine, sine)


def unproject_kernel(place_ref, dq_ref, dk_ref, dv_ref, w_ref, odd_ref, even_ref):
    step = pl.program_id(0)
    middle = pl.num_programs(0) // 2
    width = dq_ref.shape[1]
    total = dot_nt(dq_ref[...], w_ref[:, :width])
    total += dot_nt(dk_ref[...], w_ref[:, width : 2 * width])
    total += dot_nt(dv_ref[...], w_ref[:, 2 * width :])

    @pl.when(step < middle)
    def _():
        odd_ref[...] = total.astype(low)

    @pl.when(step >= middle)
    def _():
        even_ref[...] = total.astype(low)


def unproject(grads, places, weight, per_device):
    count = places.shape[0]
    rows = grads[0].shape[0] // count
    width = weight.shape[1] // 3
    middle = count // 2

    def block_of(g):
        return odd_first(g // per_device, count // per_device) * per_device + g % per_device

    tile = pl.BlockSpec((rows, width), lambda g, place: (place[block_of(g)], 0))
    shape = jax.ShapeDtypeStruct((middle * rows, D), low)
    return pl.pallas_call(
        unproject_kernel,
        grid_spec=pltpu.PrefetchScalarGridSpec(
            num_scalar_prefetch=1,
            grid=(count,),
            in_specs=[tile, tile, tile, pl.BlockSpec((D, 3 * width), lambda g, place: (0, 0))],
            out_specs=[
                pl.BlockSpec((rows, D), lambda g, place: (jnp.minimum(g, middle - 1), 0)),
                pl.BlockSpec((rows, D), lambda g, place: (jnp.maximum(g - middle, 0), 0)),
            ],
        ),
        out_shape=[shape, shape],
        compiler_params=pltpu.CompilerParams(vmem_limit_bytes=40 * 2**20),
        name="unproject",
    )(places, *grads, weight)


def dot_tn(left, right):
    return lax.dot_general(left, right, (((0,), (0,)), ((), ())), preferred_element_type=full)


def expert_kernel(
    normed_ref, cot_ref, code_ref, gate_ref, wg_ref, wu_ref, wd_ref,
    rows_ref, sg_ref, act_ref, dg_ref, du_ref, share_ref, dx_ref, out_ref,
):
    slots = rows_ref.shape[1]
    tok = normed_ref.shape[0]
    hits = code_ref[0] == lax.broadcasted_iota(jnp.int32, (slots, tok), 0)
    table_full = jnp.where(hits, 1.0, 0.0)
    gated = jnp.where(hits, gate_ref[0], 0.0)
    table = table_full.astype(low)
    rows = dot(table, normed_ref[...]).astype(low)
    rows_ref[0] = rows
    slot_gate = jnp.sum(gated, axis=1, keepdims=True)
    slot_grad = (dot(table, cot_ref[...]) * slot_gate).astype(low)
    sg_ref[0] = slot_grad
    gate = dot(rows, wg_ref[...])
    up = dot(rows, wu_ref[...])
    hidden = dot_nt(slot_grad, wd_ref[...])
    silu, slope = silu_parts(gate)
    act_full = silu * up
    act = act_full.astype(low)
    act_ref[0] = act
    dg = (hidden * up * slope).astype(low)
    du = (hidden * silu).astype(low)
    dg_ref[0] = dg
    du_ref[0] = du
    slot_share = jnp.sum(hidden * act_full, axis=1, keepdims=True)
    share_ref[0] = jnp.sum(table_full * slot_share, axis=0, keepdims=True)
    slot_dx = (dot_nt(dg, wg_ref[...]) + dot_nt(du, wu_ref[...])).astype(low)
    dx_ref[...] = dot_tn(table, slot_dx).astype(low)
    expert_y = dot(act, wd_ref[...]).astype(low)
    out_ref[...] = dot_tn(gated.astype(low), expert_y).astype(low)


def routed_expert(all_normed, cot_all, code, gate, w_gate, w_up, w_down, slots):
    count, tok = code.shape
    ff = w_gate.shape[1]
    chunk = pl.BlockSpec((tok, D), lambda m: (m, 0))
    line = pl.BlockSpec((1, 1, tok), lambda m: (m, 0, 0))

    def fixed(array):
        return pl.BlockSpec(array.shape, lambda m: (0, 0), pipeline_mode=pl.Buffered(1))

    def per_slot(last):
        return pl.BlockSpec((1, slots, last), lambda m: (m, 0, 0))

    def shape(*dims, dtype=low):
        return jax.ShapeDtypeStruct(dims, dtype)

    return pl.pallas_call(
        expert_kernel,
        grid=(count,),
        in_specs=[chunk, chunk, line, line, fixed(w_gate), fixed(w_up), fixed(w_down)],
        out_specs=[per_slot(D), per_slot(D), per_slot(ff), per_slot(ff), per_slot(ff), line, chunk, chunk],
        out_shape=[
            shape(count, slots, D),
            shape(count, slots, D),
            shape(count, slots, ff),
            shape(count, slots, ff),
            shape(count, slots, ff),
            shape(count, 1, tok, dtype=full),
            shape(count * tok, D),
            shape(count * tok, D),
        ],
        compiler_params=pltpu.CompilerParams(vmem_limit_bytes=60 * 2**20),
        name="routed_expert",
    )(all_normed, cot_all, code[:, None, :], gate[:, None, :], w_gate, w_up, w_down)


def shared_kernel(
    normed_ref, cot_ref, mix_ref, wg_ref, wu_ref, wd_ref, dxe_ref, oute_ref,
    mixcot_ref, act_ref, dg_ref, du_ref, share_ref, dx_odd, dx_even, out_odd, out_even,
):
    step = pl.program_id(0)
    middle = pl.num_programs(0) // 2
    normed = normed_ref[...]
    mix = mix_ref[...]
    mix_cot = (mix * cot_ref[...].astype(full)).astype(low)
    mixcot_ref[...] = mix_cot
    gate = dot_nt(normed, wg_ref[...])
    up = dot_nt(normed, wu_ref[...])
    hidden = dot_nt(mix_cot, wd_ref[...])
    silu, slope = silu_parts(gate)
    act_full = silu * up
    act = act_full.astype(low)
    act_ref[...] = act
    dg = (hidden * up * slope).astype(low)
    du = (hidden * silu).astype(low)
    dg_ref[...] = dg
    du_ref[...] = du
    share_ref[...] = jnp.sum(hidden * act_full, axis=1, keepdims=True)
    dx = dot(dg, wg_ref[...]) + dot(du, wu_ref[...]) + dxe_ref[...].astype(full)
    out = mix * dot(act, wd_ref[...]) + oute_ref[...].astype(full)

    @pl.when(step < middle)
    def _():
        dx_odd[...] = dx.astype(low)
        out_odd[...] = out.astype(low)

    @pl.when(step >= middle)
    def _():
        dx_even[...] = dx.astype(low)
        out_even[...] = out.astype(low)


def shared_expert(all_normed, cot_all, mix, w_gate_t, w_up_t, w_down, dx_routed, out_routed, tok):
    rows = all_normed.shape[0]
    ff = w_down.shape[0]
    count = rows // tok
    middle = count // 2
    chunk = pl.BlockSpec((tok, D), lambda g: (odd_first(g, count), 0))
    narrow = pl.BlockSpec((tok, ff), lambda g: (odd_first(g, count), 0))
    column = pl.BlockSpec((tok, 1), lambda g: (odd_first(g, count), 0))
    odd = pl.BlockSpec((tok, D), lambda g: (jnp.minimum(g, middle - 1), 0))
    even = pl.BlockSpec((tok, D), lambda g: (jnp.maximum(g - middle, 0), 0))
    fixed = pl.BlockSpec((ff, D), lambda g: (0, 0), pipeline_mode=pl.Buffered(1))
    narrow_shape = jax.ShapeDtypeStruct((rows, ff), low)
    half_shape = jax.ShapeDtypeStruct((rows // 2, D), low)
    return pl.pallas_call(
        shared_kernel,
        grid=(count,),
        in_specs=[chunk, chunk, column, fixed, fixed, fixed, chunk, chunk],
        out_specs=[chunk, narrow, narrow, narrow, column, odd, even, odd, even],
        out_shape=[
            jax.ShapeDtypeStruct((rows, D), low),
            narrow_shape,
            narrow_shape,
            narrow_shape,
            jax.ShapeDtypeStruct((rows, 1), full),
            half_shape,
            half_shape,
            half_shape,
            half_shape,
        ],
        compiler_params=pltpu.CompilerParams(vmem_limit_bytes=60 * 2**20),
        name="shared_expert",
    )(all_normed, cot_all, mix, w_gate_t, w_up_t, w_down, dx_routed, out_routed)


def forward_kernel(at_ref, q_ref, k_ref, vt_ref, o_ref, lse_ref):
    index = pl.program_id(1)
    query = q_ref[...]
    score_scale = HEAD_DIM ** (-0.5) * log2_e

    def chunk(start, size, diagonal, carry):
        highest, total, acc = carry
        start = pl.multiple_of(start, CONT)
        scores = dot_nt(k_ref[pl.ds(start, size), :], query) * score_scale
        if diagonal:
            keys = lax.broadcasted_iota(jnp.int32, scores.shape, 0)
            queries = lax.broadcasted_iota(jnp.int32, scores.shape, 1)
            scores = jnp.where(keys <= queries, scores, masked_score)
        newest = jnp.maximum(highest, jnp.max(scores, axis=0, keepdims=True))
        weights = jnp.exp2(scores - newest)
        shrink = jnp.exp2(highest - newest)
        total = total * shrink + jnp.sum(weights, axis=0, keepdims=True)
        acc = acc * shrink + dot(vt_ref[:, pl.ds(start, size)], weights.astype(low))
        return (newest, total, acc)

    highest, total, acc = attend_tiles(
        index,
        chunk,
        (
            jnp.full((1, CONT), masked_score, full),
            jnp.zeros((1, CONT), full),
            jnp.zeros((HEAD_DIM, CONT), full),
        ),
    )
    o_ref[...] = (acc / total).T.astype(low)
    lse_ref[...] = (highest + jnp.log2(total))[None]


def attention_forward(query, key, value_t, at):
    rows, width = query.shape
    heads = width // HEAD_DIM
    return pl.pallas_call(
        forward_kernel,
        grid_spec=pltpu.PrefetchScalarGridSpec(
            num_scalar_prefetch=1,
            grid=(heads, rows // CONT),
            in_specs=[
                pl.BlockSpec((CONT, HEAD_DIM), lambda h, i, at: (i, h)),
                pl.BlockSpec((rows, HEAD_DIM), lambda h, i, at: (0, h)),
                pl.BlockSpec((HEAD_DIM, rows), lambda h, i, at: (h, 0)),
            ],
            out_specs=[
                pl.BlockSpec((CONT, HEAD_DIM), lambda h, i, at: (at[i], h)),
                pl.BlockSpec((1, 1, CONT), lambda h, i, at: (h, 0, i)),
            ],
        ),
        out_shape=[
            jax.ShapeDtypeStruct((rows, width), low),
            jax.ShapeDtypeStruct((heads, 1, rows), full),
        ],
        compiler_params=pltpu.CompilerParams(vmem_limit_bytes=48 * 2**20),
        name="attend_forward",
    )(at, query, key, value_t)


def backward_kernel(
    at_ref, q_ref, do_ref, o_ref, lse_ref, k_ref, kt_ref, v_ref, cos_ref, sin_ref,
    dq_ref, dk_ref, dv_ref, dk_sum, dv_sum,
):
    index = pl.program_id(1)
    query = q_ref[...]
    upstream = do_ref[...]
    lse = lse_ref[0]
    product = upstream.astype(full) * o_ref[...].astype(full)
    delta = jnp.sum(product.T, axis=0, keepdims=True)
    scale = HEAD_DIM ** (-0.5)
    span_now = pl.ds(pl.multiple_of(index * CONT, CONT), CONT)

    @pl.when(index == 0)
    def _():
        dk_sum[...] = jnp.zeros_like(dk_sum)
        dv_sum[...] = jnp.zeros_like(dv_sum)

    def chunk(start, size, diagonal, acc):
        start = pl.multiple_of(start, CONT)
        span = pl.ds(start, size)
        scores = dot_nt(k_ref[span, :], query) * (scale * log2_e) - lse
        if diagonal:
            keys = lax.broadcasted_iota(jnp.int32, scores.shape, 0)
            queries = lax.broadcasted_iota(jnp.int32, scores.shape, 1)
            scores = jnp.where(keys <= queries, scores, masked_score)
        probs = jnp.exp2(scores)
        prob_grad = dot_nt(v_ref[span, :], upstream)
        score_grad = (probs * (prob_grad - delta)).astype(low)
        dv_sum[span, :] += dot(probs.astype(low), upstream)
        dk_sum[span, :] += dot(score_grad, query)
        return acc + dot(kt_ref[:, span], score_grad)

    acc = attend_tiles(index, chunk, jnp.zeros((HEAD_DIM, CONT), full))
    dq_ref[...] = turn(acc.T * scale, cos_ref[span_now, :], -sin_ref[span_now, :]).astype(low)

    @pl.when(index == pl.num_programs(1) - 1)
    def _():
        def finish(step, carry):
            span = pl.ds(pl.multiple_of(step * CONT, CONT), CONT)
            dk_ref[span, :] = turn(
                dk_sum[span, :] * scale, cos_ref[span, :], -sin_ref[span, :]
            ).astype(low)
            dv_ref[span, :] = dv_sum[span, :].astype(low)
            return carry

        lax.fori_loop(0, pl.num_programs(1), finish, 0)


def attention_backward(query, upstream, attended, lse, key, key_t, value, cosine, sine, at):
    rows, width = query.shape
    heads = width // HEAD_DIM
    tile = pl.BlockSpec((CONT, HEAD_DIM), lambda h, i, at: (i, h))
    stored = pl.BlockSpec((CONT, HEAD_DIM), lambda h, i, at: (at[i], h))
    whole = pl.BlockSpec((rows, HEAD_DIM), lambda h, i, at: (0, h))
    table = pl.BlockSpec((rows, HEAD_DIM), lambda h, i, at: (0, 0))
    grad = jax.ShapeDtypeStruct((rows, width), low)
    return pl.pallas_call(
        backward_kernel,
        grid_spec=pltpu.PrefetchScalarGridSpec(
            num_scalar_prefetch=1,
            grid=(heads, rows // CONT),
            in_specs=[
                tile,
                stored,
                stored,
                pl.BlockSpec((1, 1, CONT), lambda h, i, at: (h, 0, i)),
                whole,
                pl.BlockSpec((HEAD_DIM, rows), lambda h, i, at: (h, 0)),
                whole,
                table,
                table,
            ],
            out_specs=[tile, whole, whole],
            scratch_shapes=[
                pltpu.VMEM((rows, HEAD_DIM), full),
                pltpu.VMEM((rows, HEAD_DIM), full),
            ],
        ),
        out_shape=[grad, grad, grad],
        compiler_params=pltpu.CompilerParams(vmem_limit_bytes=48 * 2**20),
        name="attend_backward",
    )(at, query, upstream, attended, lse, key, key_t, value, cosine, sine)


def take_blocks(rows, order):
    count = order.shape[0]
    blocked = rows.reshape(count, rows.shape[0] // count, *rows.shape[1:])
    return jnp.concatenate(
        [lax.dynamic_index_in_dim(blocked, order[i], 0, keepdims=False) for i in range(count)], axis=0
    )


def bit_orders(count):
    bits = [1 << i for i in range(1, count.bit_length() - 1)]
    return bits, bits[::-1]


def exchange(values, bit, count):
    return lax.ppermute(values, "ctx", [(i, i ^ bit) for i in range(count)])


def gather_plan(count):
    plan = []
    orders = bit_orders(count)
    held = [[0], [0]]
    for depth in range(len(orders[0])):
        sends = [[(half, m, orders[half][depth]) for m in held[half]] for half in (0, 1)]
        plan += [send for pair in zip(*sends) for send in pair]
        for half in (0, 1):
            held[half] = held[half] + [m ^ orders[half][depth] for m in held[half]]
    return plan, [(half, m, 1) for m in held[0] for half in (0, 1)]


def gather_kernel(count, with_small, *refs):
    if with_small:
        x_ref, small_ref, out_ref, small_out, send_sems, recv_sems, own_sems = refs
    else:
        x_ref, out_ref, send_sems, recv_sems, own_sems = refs
    me = lax.axis_index("ctx")
    dp = lax.axis_index("dp")
    bits = bit_orders(count)[0] + [1]
    rows = x_ref.shape[0] // 2
    barrier = pltpu.get_barrier_semaphore()
    for bit in bits:
        pl.semaphore_signal(
            barrier, inc=1, device_id=(dp, me ^ bit), device_id_type=pl.DeviceIdType.MESH
        )
    pl.semaphore_wait(barrier, len(bits))
    spots = [out_ref.at[i] for i in range(2 * count)]
    if with_small:
        spots += [small_out.at[m] for m in range(count)]
    own = [x_ref.at[pl.ds(0, rows)], x_ref.at[pl.ds(rows, rows)]]
    local = [pltpu.make_async_copy(own[h], spots[h], own_sems.at[h]) for h in (0, 1)]
    if with_small:
        own.append(small_ref)
        local.append(pltpu.make_async_copy(small_ref, spots[2 * count], own_sems.at[2]))
    for copy in local:
        copy.start()

    def spot(half, m):
        return 2 * count + m if half == 2 else 2 * m + half

    copies = {}
    waited = set()

    def send(half, m, bit):
        if m and (half, m) not in waited:
            copies[(half, m)].wait_recv()
            waited.add((half, m))
        lands = spot(half, m ^ bit)
        copy = pltpu.make_async_remote_copy(
            src_ref=spots[spot(half, m)] if m else own[half],
            dst_ref=spots[lands],
            send_sem=send_sems.at[lands],
            recv_sem=recv_sems.at[lands],
            device_id=(dp, me ^ bit),
            device_id_type=pl.DeviceIdType.MESH,
        )
        copy.start()
        copies[(half, m ^ bit)] = copy

    far, near = gather_plan(count)
    if with_small:
        small_far = [(2, m, bit) for half, m, bit in far if half == 0]
        small_near = [(2, m, bit) for half, m, bit in near if half == 0]
        far, near = far + small_far, near + small_near
    done = set()
    for entry in far:
        send(*entry)
        for other in near:
            if other not in done and (other[1] == 0 or (other[0], other[1]) in waited):
                done.add(other)
                send(*other)
    for other in near:
        if other not in done:
            send(*other)
    for key, copy in copies.items():
        if key not in waited:
            copy.wait_recv()
    for copy in copies.values():
        copy.wait_send()
    for copy in local:
        copy.wait()


def gather_now(values, small=None, collective_id=0):
    count = lax.axis_size("ctx")
    rows, width = values.shape
    arrays = [values] if small is None else [values, small]
    shapes = [jax.ShapeDtypeStruct((2 * count, rows // 2, width), values.dtype)]
    places = 2 * count
    if small is not None:
        shapes.append(jax.ShapeDtypeStruct((count, *small.shape), small.dtype))
        places += count
    return pl.pallas_call(
        functools.partial(gather_kernel, count, small is not None),
        in_specs=[pl.BlockSpec(memory_space=pl.ANY)] * len(arrays),
        out_specs=[pl.BlockSpec(memory_space=pl.ANY)] * len(arrays),
        out_shape=shapes,
        scratch_shapes=[
            pltpu.SemaphoreType.DMA((places,)),
            pltpu.SemaphoreType.DMA((places,)),
            pltpu.SemaphoreType.DMA((3,)),
        ],
        compiler_params=pltpu.CompilerParams(
            collective_id=collective_id, has_side_effects=True, vmem_limit_bytes=4 * 2**20
        ),
        name="gather_rows",
    )(*arrays)


def split_rows(values, parts):
    rows = values.shape[0] // parts
    return [values[i * rows : (i + 1) * rows] for i in range(parts)]


def pin(arrays, *others):
    held = lax.optimization_barrier((tuple(arrays), *others))
    return (list(held[0]), *held[1:])


def gather_steps(values):
    count = lax.axis_size("ctx")
    orders = bit_orders(count)
    names, held = [[0], [0]], [[piece] for piece in split_rows(values, 2)]
    for depth in range(len(orders[0])):
        came = []
        for half in (0, 1):
            sent = jnp.concatenate(held[half], axis=0) if depth else held[half][0]
            came.append(exchange(sent, orders[half][depth], count))
        came = yield came
        for half in (0, 1):
            held[half] = held[half] + split_rows(came[half], len(held[half]))
            names[half] = names[half] + [m ^ orders[half][depth] for m in names[half]]
    halves = [dict(zip(names[half], held[half])) for half in (0, 1)]
    own = jnp.stack(
        [jnp.concatenate([half[m] for half in halves], axis=0) for m in range(0, count, 2)]
    )
    (other,) = yield [exchange(own, 1, count)]
    return jnp.stack([own, other], axis=1).reshape(count * values.shape[0], *values.shape[1:])


def add_low(left, right):
    return (left.astype(full) + right.astype(full)).astype(low)


def scatter_steps(odd, even):
    count = lax.axis_size("ctx")
    parts = count // 2
    (came,) = yield [exchange(odd, 1, count)]
    pairs = list(zip(split_rows(even, parts), split_rows(came, parts)))
    orders = bit_orders(count)
    held = [
        {
            2 * n: add_low(split_rows(left, 2)[half], split_rows(right, 2)[half])
            for n, (left, right) in enumerate(pairs)
        }
        for half in (0, 1)
    ]
    for depth in range(len(orders[0])):
        names, came = [], []
        for half in (0, 1):
            bit = orders[half][depth]
            names.append([m for m in held[half] if m & bit])
            sent = [held[half][m] for m in names[half]]
            sent = jnp.concatenate(sent, axis=0) if len(sent) > 1 else sent[0]
            came.append(exchange(sent, bit, count))
        came = yield came
        for half in (0, 1):
            bit = orders[half][depth]
            pieces = split_rows(came[half], len(names[half]))
            held[half] = {
                m ^ bit: add_low(held[half][m ^ bit], x) for m, x in zip(names[half], pieces)
            }
    return jnp.concatenate([half[0] for half in held], axis=0)


def advance(steps, came):
    try:
        return (steps.send(came), None)
    except StopIteration as stop:
        return (None, stop.value)


def finish(steps, came):
    value = None
    while value is None:
        came, value = advance(steps, came)
    return value


def odd_first(step, count):
    return lax.rem(2 * step + 1, count + 1)


def swap_ctx(values):
    return lax.all_to_all(values, "ctx", split_axis=0, concat_axis=0, tiled=True)


def on_device(
    hidden_in,
    in_gain,
    w_query,
    b_query,
    w_key,
    b_key,
    w_value,
    b_value,
    w_out,
    ffn_gain,
    w_router,
    exp_gate,
    exp_up,
    exp_down,
    sh_gate,
    sh_up,
    sh_down,
    sh_mix,
    routes,
    priority,
    blocks,
    cotangent,
):
    both = ("dp", "ctx")
    ctx_count = lax.axis_size("ctx")
    ctx_index = lax.axis_index("ctx")
    dp_count = lax.axis_size("dp")
    dp_index = lax.axis_index("dp")
    tokens_low = hidden_in[0]
    tokens = tokens_low.astype(full)
    cot_low = cotangent[0]
    cot_full = cotangent[0].astype(full)
    tok_count = tokens.shape[0]
    group_len = tok_count * ctx_count
    shard = w_query.shape[0]
    experts_total = ctx_count * exp_gate.shape[0]
    capacity = 5 * tok_count * TOP_K // (4 * experts_total)
    repeat = max(1, ctx_count // HEADS)
    heads = max(1, HEADS // ctx_count)
    width = heads * HEAD_DIM
    head_sets = HEADS // heads

    def by_heads(weight):
        parts = weight.reshape(shard, head_sets, width).transpose(1, 0, 2)
        return jnp.repeat(parts, repeat, axis=0) if repeat > 1 else parts

    qkv_parts = swap_ctx(
        jnp.concatenate([by_heads(w_query), by_heads(w_key), by_heads(w_value)], axis=2)
    )
    w_qkv = lax.all_gather(
        qkv_parts.reshape(ctx_count * shard, 3 * width), "dp", axis=0, tiled=True
    )
    partners = jnp.arange(ctx_count, dtype=jnp.int32) ^ ctx_index
    small = jnp.concatenate(
        [
            jnp.stack([in_gain, b_query, b_key, b_value, ffn_gain, sh_mix], axis=0),
            w_router.T,
        ],
        axis=0,
    ).astype(full)
    small_count = small.shape[0]
    small_rows = -(-dp_count * small_count * shard // HEAD_DIM // 8) * 8
    around = [small] + [
        lax.ppermute(small, "dp", [(i, (i + k) % dp_count) for i in range(dp_count)])
        for k in range(1, dp_count)
    ]
    origin = (dp_index - jnp.arange(dp_count, dtype=jnp.int32)) % dp_count
    small = jnp.take(jnp.stack(around), origin, axis=0).reshape(-1)
    small = jnp.pad(small, (0, small_rows * HEAD_DIM - small.shape[0])).reshape(small_rows, HEAD_DIM)
    x_blocks, small_all = gather_now(tokens_low, small, 0)
    small_all = small_all.reshape(ctx_count, -1)[:, : dp_count * small_count * shard]
    small_all = jnp.take(small_all, partners, axis=0)
    small_all = (
        small_all.reshape(ctx_count, dp_count, small_count, shard)
        .transpose(2, 1, 0, 3)
        .reshape(small_count, shard * dp_count * ctx_count)
    )
    gain_one, gain_two, mix_row = small_all[0:1], small_all[4:5], small_all[5:6]
    mix_router = small_all[5:].astype(low)
    w_out, qkv_parts = lax.optimization_barrier((w_out, qkv_parts))
    out_mine = lax.all_gather(w_out, "dp", axis=0, tiled=True)
    (cot_low, out_mine), x_blocks = pin([cot_low, out_mine], x_blocks)
    cot_steps, out_steps = gather_steps(cot_low), gather_steps(out_mine)
    came = next(cot_steps) + next(out_steps)
    shared_gate, shared_up, shared_down = (
        lax.all_gather(sh_gate.T, "dp", axis=0, tiled=True),
        lax.all_gather(sh_up.T, "dp", axis=0, tiled=True),
        lax.all_gather(sh_down, "dp", axis=0, tiled=True),
    )
    expert_gate, expert_up, expert_down = (
        lax.all_gather(exp_gate[0], "dp", axis=0, tiled=True),
        lax.all_gather(exp_up[0], "dp", axis=0, tiled=True),
        lax.all_gather(exp_down[0], "dp", axis=1, tiled=True),
    )

    route_ids = routes[0]
    flat_ids = route_ids.reshape(-1)
    order = priority[0, 0]
    earlier = (flat_ids[:, None] == flat_ids[None, :]) & (order[None, :] < order[:, None])
    ranks = jnp.sum(earlier.astype(jnp.int32), axis=1).reshape(route_ids.shape)
    expert_grid = jnp.arange(experts_total, dtype=jnp.int32)
    route_hits = route_ids[None, :, :] == expert_grid[:, None, None]
    code = jnp.sum(jnp.where(route_hits, ranks[None] + 1, 0), axis=2) - 1

    stored_to_place = blocks[0]
    block_count = stored_to_place.shape[0]
    block_grid = jnp.arange(block_count, dtype=jnp.int32)
    place_to_stored = jnp.sum(
        jnp.where(stored_to_place[None, :] == block_grid[:, None], block_grid[None, :], 0), axis=1
    )
    per_device = block_count // ctx_count
    near = partners * per_device
    stored_near = jnp.concatenate(
        [
            lax.dynamic_slice_in_dim(stored_to_place, near[m], per_device)
            for m in range(ctx_count)
        ]
    )
    place_to_near = (place_to_stored // per_device ^ ctx_index) * per_device + (
        place_to_stored % per_device
    )
    cosine, sine = rope_tables(jnp.arange(group_len, dtype=jnp.int32))
    my_heads = (ctx_index // repeat) * width
    scale_one = rms_scale(tokens)
    bias = lax.dynamic_slice_in_dim(small_all[1:4], my_heads, width, 1).reshape(1, 3 * width)
    cosine_wide = jnp.concatenate([cosine[:, 0], cosine[:, 0]], axis=1)
    sine_wide = jnp.concatenate([-sine[:, 0], sine[:, 0]], axis=1)
    normed_sorted, query, key, value = project(
        x_blocks, stored_near, gain_one, w_qkv, bias, cosine_wide, sine_wide
    )
    tiles = group_len // CONT
    direct = block_count == tiles
    at = place_to_stored if direct else jnp.arange(tiles, dtype=jnp.int32)
    (*came, value), query = pin([*came, value], query)
    cot_came, cot_all = advance(cot_steps, came[:2])
    out_came, out_parts = advance(out_steps, came[2:])
    came = cot_came + out_came
    attended_heads, lse = attention_forward(query, key, value.T, at)
    came, attended_heads = pin(came, attended_heads)
    split = len(came) // 2
    attended_stored = attended_heads if direct else take_blocks(attended_heads, stored_to_place)
    attended_parts = swap_ctx(attended_stored.reshape(ctx_count, tok_count, width))[::repeat]
    out_parts = finish(out_steps, came[split:])
    cot_all = finish(cot_steps, came[:split])
    out_parts = out_parts.reshape(ctx_count, dp_count, shard, D)
    out_full = (
        jnp.stack(
            [lax.dynamic_index_in_dim(out_parts, partners[i], 0, False) for i in range(ctx_count)],
            axis=1,
        )
    ).reshape(D, D)
    attended = attended_parts.transpose(1, 0, 2).reshape(tok_count, D)
    first_sum = tokens + dot(attended, out_full)
    scale_two = rms_scale(first_sum)
    normed_two = (first_sum * scale_two * gain_two).astype(low)
    logits = dot_nt(normed_two, mix_router)
    mix_mine = jax.nn.sigmoid(logits[:, 0:1])
    chosen = code.T >= 0
    masked = jnp.where(chosen, logits[:, 1:], masked_score)
    raised = jnp.where(chosen, jnp.exp(masked - jnp.max(masked, axis=1, keepdims=True)), 0.0)
    gates_mine = raised / jnp.sum(raised, axis=1, keepdims=True)
    narrow = jnp.concatenate([mix_mine.T, gates_mine.T, code.astype(full)], axis=0)
    narrow = jnp.pad(narrow, ((0, -narrow.shape[0] % 8), (0, 0)))
    all_normed, narrow_all = gather_now(normed_two, narrow, 1)
    all_normed = all_normed.reshape(group_len, D)
    mix_all = narrow_all[:, 0].reshape(group_len, 1)
    gate_mine = lax.dynamic_index_in_dim(narrow_all, ctx_index + 1, 1, keepdims=False)
    code_mine = lax.dynamic_index_in_dim(
        narrow_all, ctx_index + 1 + experts_total, 1, keepdims=False
    ).astype(jnp.int32)
    code_mine = jnp.where(code_mine < capacity, code_mine, -1)
    slot_rows = -(-capacity // 32) * 32
    expert_rows, slot_grads, hidden_low, gate_grad, up_grad, gate_share, dx_routed, out_routed = (
        routed_expert(
            all_normed, cot_all, code_mine, gate_mine, expert_gate, expert_up, expert_down, slot_rows
        )
    )
    grad_egate = ein("crd,crf->df", expert_rows, gate_grad).astype(low)
    dx_routed, grad_egate = lax.optimization_barrier((dx_routed, grad_egate))
    mix_cot, shared_low, shared_dg, shared_du, mix_share, dx_odd, dx_even, out_odd, out_even = (
        shared_expert(
            all_normed, cot_all, mix_all, shared_gate, shared_up, shared_down,
            dx_routed, out_routed, tok_count,
        )
    )
    dx_steps = scatter_steps(dx_odd, dx_even)
    came = next(dx_steps)
    grad_eup = ein("crd,crf->df", expert_rows, up_grad).astype(low)
    came, grad_eup, hidden_low, shared_low, shared_dg, shared_du = pin(
        came, grad_eup, hidden_low, shared_low, shared_dg, shared_du
    )
    came, dx_mine = advance(dx_steps, came)
    grad_edown = ein("crf,crd->fd", hidden_low, slot_grads).astype(low)
    grad_sdown = ein("tf,td->fd", shared_low, mix_cot).astype(low)
    came, grad_edown, grad_sdown, shared_dg, shared_du = pin(
        came, grad_edown, grad_sdown, shared_dg, shared_du
    )
    came, dx_mine = advance(dx_steps, came)
    grad_sgate = ein("tf,td->fd", shared_dg, all_normed).astype(low)
    grad_sup = ein("tf,td->fd", shared_du, all_normed).astype(low)
    came, grad_sgate, grad_sup = pin(came, grad_sgate, grad_sup)
    dx_mine = finish(dx_steps, came).astype(full)

    shares = jnp.stack([gate_share[:, 0], mix_share.reshape(ctx_count, tok_count)], axis=1)
    shares = swap_ctx(jnp.take(shares, partners, axis=0))
    gate_shares = shares[:, 0].T
    mix_grad = jnp.sum(shares[:, 1], axis=0)[:, None] * (1.0 - mix_mine)
    logit_grad = gate_shares - gates_mine * jnp.sum(gate_shares, axis=1, keepdims=True)
    narrow_low = logit_grad.astype(low)
    grad_narrow = jnp.concatenate(
        [
            jnp.sum(mix_grad * normed_two.astype(full), axis=0, keepdims=True),
            ein("te,td->ed", narrow_low, normed_two),
        ],
        axis=0,
    )
    (out_odd,), dx_mine = pin([out_odd], dx_mine)
    add_steps = scatter_steps(out_odd, out_even)
    came = next(add_steps)
    normed_grad = dx_mine + mix_grad * mix_row + dot(narrow_low, mix_router[1:])
    norm_grad_two, grad_gain_two = norm_back(first_sum, scale_two, gain_two, normed_grad)
    first_grad = cot_full + norm_grad_two
    first_low = first_grad.astype(low)
    attended_grad = dot_nt(first_low, out_full).astype(low)
    grad_out = ein("td,te->de", attended, first_low)

    upstream_parts = attended_grad.reshape(tok_count, head_sets, width).transpose(1, 0, 2)
    if repeat > 1:
        upstream_parts = jnp.repeat(upstream_parts, repeat, axis=0)
    came, upstream_parts = pin(came, upstream_parts)
    came, added = advance(add_steps, came)
    upstream = swap_ctx(upstream_parts).reshape(group_len, width)
    if not direct:
        upstream = take_blocks(upstream, place_to_stored)
    qkv_grads = attention_backward(
        query, upstream, attended_heads, lse, key, key.T, value, cosine_wide, sine_wide, at
    )
    (*came, value_grad), key_grad, query_grad = pin([*came, qkv_grads[2]], qkv_grads[1], qkv_grads[0])
    qkv_grads = [query_grad, key_grad, value_grad]
    came, added = advance(add_steps, came)
    if repeat > 1:
        qkv_grads = [jnp.where(ctx_index % repeat == 0, g, jnp.zeros_like(g)) for g in qkv_grads]
    grad_qkv = jnp.concatenate(
        [ein("td,te->de", normed_sorted, g).astype(low) for g in qkv_grads], axis=1
    )
    bias_sums = jnp.stack([jnp.sum(g.astype(full), axis=0) for g in qkv_grads])
    grad_bias = lax.dynamic_update_slice_in_dim(
        jnp.zeros((3, D), full), bias_sums, my_heads, 1
    )
    grad_qkv, first_grads = lax.optimization_barrier((grad_qkv, qkv_grads[0]))
    odd_one, even_one = unproject([first_grads, *qkv_grads[1:]], stored_near, w_qkv, per_device)
    came, odd_one = pin(came, odd_one)
    added = finish(add_steps, came)
    layer_out = first_sum + added.astype(full)
    one_steps = scatter_steps(odd_one, even_one)
    dx_one = finish(one_steps, next(one_steps)).astype(full)
    norm_grad_one, grad_gain_one = norm_back(tokens, scale_one, gain_one, dx_one)
    input_grad = first_grad + norm_grad_one

    qkv_rows = lax.psum_scatter(
        grad_qkv.reshape(dp_count, ctx_count, shard, 3 * width),
        "dp",
        scatter_dimension=0,
        tiled=True,
    )[0]
    qkv_mine = swap_ctx(qkv_rows)[::repeat].astype(full)
    qkv_mine = qkv_mine.reshape(head_sets, shard, 3, width).transpose(2, 1, 0, 3).reshape(3, shard, D)
    out_rows = swap_ctx(
        grad_out.astype(low).reshape(dp_count, ctx_count, shard, D).transpose(1, 0, 2, 3)
    )
    out_rows = jnp.sum(out_rows.astype(full), axis=0).astype(low)
    grad_wout = lax.psum_scatter(out_rows, "dp", scatter_dimension=0, tiled=True)[0].astype(full)
    small_grads = jnp.concatenate(
        [grad_gain_one[None], grad_bias, grad_gain_two[None], grad_narrow], axis=0
    )
    small_grads = small_grads.reshape(-1, dp_count, ctx_count, shard).transpose(2, 1, 0, 3)
    small_grads = jnp.sum(swap_ctx(small_grads), axis=0)
    small_grads = jnp.sum(
        lax.all_to_all(small_grads, "dp", split_axis=0, concat_axis=0, tiled=True), axis=0
    ).T

    def over_dp(grad, dim):
        return lax.psum_scatter(
            grad.astype(low), "dp", scatter_dimension=dim, tiled=True
        ).astype(full)

    return (
        layer_out.astype(low)[None],
        input_grad[None],
        small_grads[:, 0],
        qkv_mine[0],
        small_grads[:, 1],
        qkv_mine[1],
        small_grads[:, 2],
        qkv_mine[2],
        small_grads[:, 3],
        grad_wout,
        small_grads[:, 4],
        small_grads[:, 6:],
        over_dp(grad_egate, 0)[None],
        over_dp(grad_eup, 0)[None],
        over_dp(grad_edown, 1)[None],
        over_dp(grad_sgate, 0).T,
        over_dp(grad_sup, 0).T,
        over_dp(grad_sdown, 0),
        small_grads[:, 5],
    )


def solution(mesh):
    rows = P("dp", "ctx", None)
    flat = P(("dp", "ctx"))
    lines = P(("dp", "ctx"), None)
    columns = P(None, ("dp", "ctx"))
    deep = P("ctx", "dp", None)
    down = P("ctx", None, "dp")
    in_specs = (
        (rows, flat, lines, flat, lines, flat, lines, flat, lines, flat, lines)
        + (deep, deep, down, columns, columns, lines, flat)
        + (rows, rows, P("dp", None), rows)
    )
    out_specs = (
        (rows, rows, flat, lines, flat, lines, flat, lines, flat, lines, flat, lines)
        + (deep, deep, down, columns, columns, lines, flat)
    )
    return jax.shard_map(
        on_device, mesh=mesh, in_specs=in_specs, out_specs=out_specs, check_vma=False
    )
```

```python
import functools

import jax
import jax.numpy as jnp
import numpy as np
from jax import lax
from jax.experimental import pallas as pl
from jax.experimental.pallas import tpu as pltpu
from jax.sharding import PartitionSpec as P

D = 2048
HEADS = 16
HEAD_DIM = 128
TOP_K = 4
CONT = 256
PROMPT = 2048

rope_base = 1000000.0
epsilon = 1e-06
masked_score = -1e30
log2_e = 1.4426950408889634
low = jnp.bfloat16
full = jnp.float32


def dot(left, right):
    return jnp.dot(left, right, preferred_element_type=full)


def dot_nt(left, right):
    return lax.dot_general(left, right, (((1,), (1,)), ((), ())), preferred_element_type=full)


def ein(spec, left, right):
    return jnp.einsum(spec, left, right, preferred_element_type=full)


def rotate(values, cosine, sine):
    middle = values.shape[-1] // 2
    leading = values[..., :middle]
    trailing = values[..., middle:]
    return jnp.concatenate(
        [leading * cosine - trailing * sine, trailing * cosine + leading * sine], axis=-1
    )


def rope_tables(rows):
    places = np.arange(rows)
    turned = np.where(places < PROMPT, places, PROMPT + (places - PROMPT) % CONT)
    frequency = rope_base ** (-2.0 * np.arange(HEAD_DIM // 2, dtype=np.float64) / HEAD_DIM)
    angles = turned.astype(np.float64)[:, None] * frequency[None, :]
    cosine, sine = np.cos(angles), np.sin(angles)
    wide = np.concatenate([cosine, cosine], axis=1), np.concatenate([-sine, sine], axis=1)
    return tuple(jnp.asarray(table.astype(np.float32)) for table in wide)


def rms_scale(values):
    return lax.rsqrt(jnp.mean(values * values, axis=-1, keepdims=True) + epsilon)


def norm_back(values, scale_rows, gain_row, upstream):
    weighted = upstream * gain_row
    grad_gain = jnp.sum(upstream * values * scale_rows, axis=0)
    grad_values = scale_rows * weighted - values * scale_rows**3 * jnp.mean(
        weighted * values, axis=-1, keepdims=True
    )
    return (grad_values, grad_gain)


def silu_parts(values):
    sig_value = jax.nn.sigmoid(values)
    return (values * sig_value, sig_value * (1.0 + values * (1.0 - sig_value)))


def cost(microseconds):
    return pl.CostEstimate(
        flops=int(microseconds * 1.1e9),
        bytes_accessed=int(microseconds * 3.3e6),
        transcendentals=0,
    )


WIDE = 4


def attend_tiles(index, chunk, carry):
    whole = jnp.minimum(index, PROMPT // CONT)
    wide = whole // WIDE
    carry = lax.fori_loop(
        0, wide, lambda step, c: chunk(step * (WIDE * CONT), WIDE * CONT, False, c), carry
    )
    carry = lax.fori_loop(
        wide * WIDE, whole, lambda step, c: chunk(step * CONT, CONT, False, c), carry
    )
    return chunk(index * CONT, CONT, True, carry)


def turn(values, cosine, sine):
    half = HEAD_DIM // 2
    swapped = jnp.concatenate([values[:, half:], values[:, :half]], axis=1)
    return values * cosine + swapped * sine


def project_kernel(
    place_ref, x_ref, gain_ref, w_ref, bias_ref, cos_ref, sin_ref, normed_ref, q_ref, k_ref, v_ref
):
    values = x_ref[0].astype(full)
    scale = lax.rsqrt(jnp.mean(values * values, axis=1, keepdims=True) + epsilon)
    normed = (values * scale * gain_ref[...]).astype(low)
    normed_ref[...] = normed
    width = q_ref.shape[1]
    projected = dot(normed, w_ref[...]) + bias_ref[...]
    cosine, sine = cos_ref[...], sin_ref[...]
    for start in range(0, width, HEAD_DIM):
        for kind, out in ((0, q_ref), (1, k_ref)):
            column = kind * width + start
            head = projected[:, column : column + HEAD_DIM]
            out[:, start : start + HEAD_DIM] = turn(head, cosine, sine).astype(low)
    v_ref[...] = projected[:, 2 * width :].astype(low)


def project(x_blocks, places, gain, weight, bias, cosine, sine):
    count, rows, _ = x_blocks.shape
    width = weight.shape[1] // 3
    at_place = lambda g, place: (place[g], 0)
    whole = lambda g, place: (0, 0)
    tile = pl.BlockSpec((rows, width), at_place)
    head = jax.ShapeDtypeStruct((count * rows, width), low)
    return pl.pallas_call(
        project_kernel,
        grid_spec=pltpu.PrefetchScalarGridSpec(
            num_scalar_prefetch=1,
            grid=(count,),
            in_specs=[
                pl.BlockSpec((1, rows, D), lambda g, place: (g, 0, 0)),
                pl.BlockSpec((1, D), whole),
                pl.BlockSpec((D, 3 * width), whole),
                pl.BlockSpec((1, 3 * width), whole),
                pl.BlockSpec((rows, HEAD_DIM), at_place),
                pl.BlockSpec((rows, HEAD_DIM), at_place),
            ],
            out_specs=[pl.BlockSpec((rows, D), at_place), tile, tile, tile],
        ),
        out_shape=[jax.ShapeDtypeStruct((count * rows, D), low), head, head, head],
        compiler_params=pltpu.CompilerParams(vmem_limit_bytes=40 * 2**20),
        cost_estimate=cost(24),
        name="project",
    )(places, x_blocks, gain, weight, bias, cosine, sine)


def unproject_kernel(place_ref, grad_ref, w_ref, normed_ref, odd_ref, even_ref, gain_ref):
    step = pl.program_id(0)
    middle = pl.num_programs(0) // 2
    total = dot_nt(grad_ref[...], w_ref[...])
    gain_part = jnp.sum(total * normed_ref[...].astype(full), axis=0, keepdims=True)

    @pl.when(step == 0)
    def _():
        gain_ref[...] = jnp.zeros_like(gain_ref)

    gain_ref[...] += gain_part

    @pl.when(step < middle)
    def _():
        odd_ref[...] = total.astype(low)

    @pl.when(step >= middle)
    def _():
        even_ref[...] = total.astype(low)


def unproject(grads, places, weight, normed, per_device):
    count = places.shape[0]
    rows = grads.shape[0] // count
    width = weight.shape[1]
    middle = count // 2

    def at_place(g, place):
        block = odd_first(g // per_device, count // per_device) * per_device + g % per_device
        return (place[block], 0)

    shape = jax.ShapeDtypeStruct((middle * rows, D), low)
    return pl.pallas_call(
        unproject_kernel,
        grid_spec=pltpu.PrefetchScalarGridSpec(
            num_scalar_prefetch=1,
            grid=(count,),
            in_specs=[
                pl.BlockSpec((rows, width), at_place),
                pl.BlockSpec((D, width), lambda g, place: (0, 0)),
                pl.BlockSpec((rows, D), at_place),
            ],
            out_specs=[
                pl.BlockSpec((rows, D), lambda g, place: (jnp.minimum(g, middle - 1), 0)),
                pl.BlockSpec((rows, D), lambda g, place: (jnp.maximum(g - middle, 0), 0)),
                pl.BlockSpec((1, D), lambda g, place: (0, 0)),
            ],
        ),
        out_shape=[shape, shape, jax.ShapeDtypeStruct((1, D), full)],
        compiler_params=pltpu.CompilerParams(vmem_limit_bytes=40 * 2**20),
        cost_estimate=cost(20),
        name="unproject",
    )(places, grads, weight, normed)


def dot_tn(left, right):
    return lax.dot_general(left, right, (((0,), (0,)), ((), ())), preferred_element_type=full)


def expert_kernel(
    normed_ref, cot_ref, code_ref, gate_ref, wg_ref, wu_ref, wd_ref,
    rows_ref, sg_ref, act_ref, dg_ref, du_ref, share_ref, dx_ref, out_ref,
):
    slots = rows_ref.shape[1]
    tok = normed_ref.shape[0]
    hits = code_ref[0] == lax.broadcasted_iota(jnp.int32, (slots, tok), 0)
    table_full = jnp.where(hits, 1.0, 0.0)
    gated = jnp.where(hits, gate_ref[0], 0.0)
    table = table_full.astype(low)
    rows = dot(table, normed_ref[...]).astype(low)
    rows_ref[0] = rows
    slot_gate = jnp.sum(gated, axis=1, keepdims=True)
    slot_grad = (dot(table, cot_ref[...]) * slot_gate).astype(low)
    sg_ref[0] = slot_grad
    gate = dot(rows, wg_ref[...])
    up = dot(rows, wu_ref[...])
    hidden = dot_nt(slot_grad, wd_ref[...])
    silu, slope = silu_parts(gate)
    act_full = silu * up
    act = act_full.astype(low)
    act_ref[0] = act
    dg = (hidden * up * slope).astype(low)
    du = (hidden * silu).astype(low)
    dg_ref[0] = dg
    du_ref[0] = du
    slot_share = jnp.sum(hidden * act_full, axis=1, keepdims=True)
    share_ref[0] = jnp.sum(table_full * slot_share, axis=0, keepdims=True)
    slot_dx = (dot_nt(dg, wg_ref[...]) + dot_nt(du, wu_ref[...])).astype(low)
    dx_ref[...] = dot_tn(table, slot_dx).astype(low)
    expert_y = dot(act, wd_ref[...]).astype(low)
    out_ref[...] = dot_tn(gated.astype(low), expert_y).astype(low)


def routed_expert(all_normed, cot_all, code, gate, w_gate, w_up, w_down, slots):
    count, tok = code.shape
    ff = w_gate.shape[1]
    chunk = pl.BlockSpec((tok, D), lambda m: (m, 0))
    line = pl.BlockSpec((1, 1, tok), lambda m: (m, 0, 0))

    def fixed(array):
        return pl.BlockSpec(array.shape, lambda m: (0, 0), pipeline_mode=pl.Buffered(1))

    def per_slot(last):
        return pl.BlockSpec((1, slots, last), lambda m: (m, 0, 0))

    def shape(*dims, dtype=low):
        return jax.ShapeDtypeStruct(dims, dtype)

    return pl.pallas_call(
        expert_kernel,
        grid=(count,),
        in_specs=[chunk, chunk, line, line, fixed(w_gate), fixed(w_up), fixed(w_down)],
        out_specs=[per_slot(D), per_slot(D), per_slot(ff), per_slot(ff), per_slot(ff), line, chunk, chunk],
        out_shape=[
            shape(count, slots, D),
            shape(count, slots, D),
            shape(count, slots, ff),
            shape(count, slots, ff),
            shape(count, slots, ff),
            shape(count, 1, tok, dtype=full),
            shape(count * tok, D),
            shape(count * tok, D),
        ],
        compiler_params=pltpu.CompilerParams(vmem_limit_bytes=60 * 2**20),
        cost_estimate=cost(140),
        name="routed_expert",
    )(all_normed, cot_all, code[:, None, :], gate[:, None, :], w_gate, w_up, w_down)


def shared_kernel(
    normed_ref, cot_ref, mix_ref, wg_ref, wu_ref, wd_ref, dxe_ref, oute_ref,
    mixcot_ref, act_ref, dg_ref, du_ref, share_ref, dx_odd, dx_even, out_odd, out_even,
):
    step = pl.program_id(0)
    middle = pl.num_programs(0) // 2
    normed = normed_ref[...]
    mix = mix_ref[...]
    mix_cot = (mix * cot_ref[...].astype(full)).astype(low)
    mixcot_ref[...] = mix_cot
    gate = dot_nt(normed, wg_ref[...])
    up = dot_nt(normed, wu_ref[...])
    hidden = dot_nt(mix_cot, wd_ref[...])
    silu, slope = silu_parts(gate)
    act_full = silu * up
    act = act_full.astype(low)
    act_ref[...] = act
    dg = (hidden * up * slope).astype(low)
    du = (hidden * silu).astype(low)
    dg_ref[...] = dg
    du_ref[...] = du
    share_ref[...] = jnp.sum(hidden * act_full, axis=1, keepdims=True)
    dx = dot(dg, wg_ref[...]) + dot(du, wu_ref[...]) + dxe_ref[...].astype(full)
    out = mix * dot(act, wd_ref[...]) + oute_ref[...].astype(full)

    @pl.when(step < middle)
    def _():
        dx_odd[...] = dx.astype(low)
        out_odd[...] = out.astype(low)

    @pl.when(step >= middle)
    def _():
        dx_even[...] = dx.astype(low)
        out_even[...] = out.astype(low)


def shared_expert(all_normed, cot_all, mix, w_gate_t, w_up_t, w_down, dx_routed, out_routed, tok):
    rows = all_normed.shape[0]
    ff = w_down.shape[0]
    count = rows // tok
    middle = count // 2
    chunk = pl.BlockSpec((tok, D), lambda g: (odd_first(g, count), 0))
    narrow = pl.BlockSpec((tok, ff), lambda g: (odd_first(g, count), 0))
    column = pl.BlockSpec((tok, 1), lambda g: (odd_first(g, count), 0))
    odd = pl.BlockSpec((tok, D), lambda g: (jnp.minimum(g, middle - 1), 0))
    even = pl.BlockSpec((tok, D), lambda g: (jnp.maximum(g - middle, 0), 0))
    fixed = pl.BlockSpec((ff, D), lambda g: (0, 0), pipeline_mode=pl.Buffered(1))
    narrow_shape = jax.ShapeDtypeStruct((rows, ff), low)
    half_shape = jax.ShapeDtypeStruct((rows // 2, D), low)
    return pl.pallas_call(
        shared_kernel,
        grid=(count,),
        in_specs=[chunk, chunk, column, fixed, fixed, fixed, chunk, chunk],
        out_specs=[chunk, narrow, narrow, narrow, column, odd, even, odd, even],
        out_shape=[
            jax.ShapeDtypeStruct((rows, D), low),
            narrow_shape,
            narrow_shape,
            narrow_shape,
            jax.ShapeDtypeStruct((rows, 1), full),
            half_shape,
            half_shape,
            half_shape,
            half_shape,
        ],
        compiler_params=pltpu.CompilerParams(vmem_limit_bytes=60 * 2**20),
        cost_estimate=cost(103),
        name="shared_expert",
    )(all_normed, cot_all, mix, w_gate_t, w_up_t, w_down, dx_routed, out_routed)


def forward_kernel(at_ref, q_ref, k_ref, vt_ref, o_ref, lse_ref):
    index = pl.program_id(0)
    query = q_ref[...]
    score_scale = HEAD_DIM ** (-0.5) * log2_e

    def chunk(start, size, diagonal, carry):
        highest, total, acc = carry
        start = pl.multiple_of(start, CONT)
        scores = dot_nt(k_ref[pl.ds(start, size), :], query) * score_scale
        if diagonal:
            keys = lax.broadcasted_iota(jnp.int32, scores.shape, 0)
            queries = lax.broadcasted_iota(jnp.int32, scores.shape, 1)
            scores = jnp.where(keys <= queries, scores, masked_score)
        newest = jnp.maximum(highest, jnp.max(scores, axis=0, keepdims=True))
        weights = jnp.exp2(scores - newest)
        shrink = jnp.exp2(highest - newest)
        total = total * shrink + jnp.sum(weights, axis=0, keepdims=True)
        acc = acc * shrink + dot(vt_ref[:, pl.ds(start, size)], weights.astype(low))
        return (newest, total, acc)

    highest, total, acc = attend_tiles(
        index,
        chunk,
        (
            jnp.full((1, CONT), masked_score, full),
            jnp.zeros((1, CONT), full),
            jnp.zeros((HEAD_DIM, CONT), full),
        ),
    )
    o_ref[...] = (acc / total).T.astype(low)
    lse_ref[...] = highest + jnp.log2(total)


def attention_forward(query, key, value_t, at, head):
    rows = query.shape[0]
    return pl.pallas_call(
        forward_kernel,
        grid_spec=pltpu.PrefetchScalarGridSpec(
            num_scalar_prefetch=1,
            grid=(rows // CONT,),
            in_specs=[
                pl.BlockSpec((CONT, HEAD_DIM), lambda i, at: (i, head)),
                pl.BlockSpec((rows, HEAD_DIM), lambda i, at: (0, head)),
                pl.BlockSpec((HEAD_DIM, rows), lambda i, at: (head, 0)),
            ],
            out_specs=[
                pl.BlockSpec((CONT, HEAD_DIM), lambda i, at: (at[i], 0)),
                pl.BlockSpec((1, CONT), lambda i, at: (0, i)),
            ],
        ),
        out_shape=[
            jax.ShapeDtypeStruct((rows, HEAD_DIM), low),
            jax.ShapeDtypeStruct((1, rows), full),
        ],
        compiler_params=pltpu.CompilerParams(vmem_limit_bytes=32 * 2**20),
        cost_estimate=cost(30),
        name="attend_forward",
    )(at, query, key, value_t)


def backward_kernel(
    at_ref, q_ref, do_ref, o_ref, lse_ref, k_ref, kt_ref, v_ref, cos_ref, sin_ref,
    dq_ref, dk_ref, dv_ref, dk_sum, dv_sum,
):
    index = pl.program_id(0)
    query = q_ref[...]
    upstream = do_ref[...]
    lse = lse_ref[...]
    product = upstream.astype(full) * o_ref[...].astype(full)
    delta = jnp.sum(product.T, axis=0, keepdims=True)
    scale = HEAD_DIM ** (-0.5)
    span_now = pl.ds(pl.multiple_of(index * CONT, CONT), CONT)

    @pl.when(index == 0)
    def _():
        dk_sum[...] = jnp.zeros_like(dk_sum)
        dv_sum[...] = jnp.zeros_like(dv_sum)

    def chunk(start, size, diagonal, acc):
        start = pl.multiple_of(start, CONT)
        span = pl.ds(start, size)
        scores = dot_nt(k_ref[span, :], query) * (scale * log2_e) - lse
        if diagonal:
            keys = lax.broadcasted_iota(jnp.int32, scores.shape, 0)
            queries = lax.broadcasted_iota(jnp.int32, scores.shape, 1)
            scores = jnp.where(keys <= queries, scores, masked_score)
        probs = jnp.exp2(scores)
        prob_grad = dot_nt(v_ref[span, :], upstream)
        score_grad = (probs * (prob_grad - delta)).astype(low)
        dv_sum[span, :] += dot(probs.astype(low), upstream)
        dk_sum[span, :] += dot(score_grad, query)
        return acc + dot(kt_ref[:, span], score_grad)

    acc = attend_tiles(index, chunk, jnp.zeros((HEAD_DIM, CONT), full))
    dq_ref[...] = turn(acc.T * scale, cos_ref[span_now, :], -sin_ref[span_now, :]).astype(low)

    @pl.when(index == pl.num_programs(0) - 1)
    def _():
        def finish(step, carry):
            span = pl.ds(pl.multiple_of(step * CONT, CONT), CONT)
            dk_ref[span, :] = turn(
                dk_sum[span, :] * scale, cos_ref[span, :], -sin_ref[span, :]
            ).astype(low)
            dv_ref[span, :] = dv_sum[span, :].astype(low)
            return carry

        lax.fori_loop(0, pl.num_programs(0), finish, 0)


def attention_backward(query, upstream, attended, lse, key, key_t, value, cosine, sine, at, head):
    rows = query.shape[0]
    tile = pl.BlockSpec((CONT, HEAD_DIM), lambda i, at: (i, head))
    stored = pl.BlockSpec((CONT, HEAD_DIM), lambda i, at: (at[i], 0))
    whole = pl.BlockSpec((rows, HEAD_DIM), lambda i, at: (0, head))
    table = pl.BlockSpec((rows, HEAD_DIM), lambda i, at: (0, 0))
    grad = jax.ShapeDtypeStruct((rows, HEAD_DIM), low)
    return pl.pallas_call(
        backward_kernel,
        grid_spec=pltpu.PrefetchScalarGridSpec(
            num_scalar_prefetch=1,
            grid=(rows // CONT,),
            in_specs=[
                tile,
                stored,
                stored,
                pl.BlockSpec((1, CONT), lambda i, at: (0, i)),
                whole,
                pl.BlockSpec((HEAD_DIM, rows), lambda i, at: (head, 0)),
                whole,
                table,
                table,
            ],
            out_specs=[pl.BlockSpec((CONT, HEAD_DIM), lambda i, at: (i, 0)), table, table],
            scratch_shapes=[
                pltpu.VMEM((rows, HEAD_DIM), full),
                pltpu.VMEM((rows, HEAD_DIM), full),
            ],
        ),
        out_shape=[grad, grad, grad],
        compiler_params=pltpu.CompilerParams(vmem_limit_bytes=48 * 2**20),
        cost_estimate=cost(38),
        name="attend_backward",
    )(at, query, upstream, attended, lse, key, key_t, value, cosine, sine)


def take_blocks(rows, order):
    count = order.shape[0]
    blocked = rows.reshape(count, rows.shape[0] // count, *rows.shape[1:])
    return jnp.concatenate(
        [lax.dynamic_index_in_dim(blocked, order[i], 0, keepdims=False) for i in range(count)], axis=0
    )


def bit_orders(count):
    bits = [1 << i for i in range(1, count.bit_length() - 1)]
    return bits, bits[::-1]


def exchange(values, bit, count):
    return lax.ppermute(values, "ctx", [(i, i ^ bit) for i in range(count)])


def gather_plan(count):
    plan = []
    orders = bit_orders(count)
    held = [[0], [0]]
    for depth in range(len(orders[0])):
        sends = [[(half, m, orders[half][depth]) for m in held[half]] for half in (0, 1)]
        plan += [send for pair in zip(*sends) for send in pair]
        for half in (0, 1):
            held[half] = held[half] + [m ^ orders[half][depth] for m in held[half]]
    return plan, [(half, m, 1) for m in held[0] for half in (0, 1)]


def gather_kernel(count, big, with_small, *refs):
    ins = refs[: big + with_small]
    outs = refs[big + with_small : 2 * (big + with_small)]
    send_sems, recv_sems, own_sems = refs[2 * (big + with_small) :]
    me = lax.axis_index("ctx")
    dp = lax.axis_index("dp")
    bits = bit_orders(count)[0] + [1]
    rows = ins[0].shape[0] // 2
    barrier = pltpu.get_barrier_semaphore()
    for bit in bits:
        pl.semaphore_signal(
            barrier, inc=1, device_id=(dp, me ^ bit), device_id_type=pl.DeviceIdType.MESH
        )
    pl.semaphore_wait(barrier, len(bits))
    own, spots = [], []
    for a in range(big):
        for half in (0, 1):
            own.append(ins[a].at[pl.ds(half * rows, rows)])
            spots.append([outs[a].at[2 * m + half] for m in range(count)])
    if with_small:
        own.append(ins[big])
        spots.append([outs[big].at[m] for m in range(count)])
    local = [
        pltpu.make_async_copy(own[t], spots[t][0], own_sems.at[t]) for t in range(len(own))
    ]
    for copy in local:
        copy.start()
    copies = {}
    waited = set()

    def send(track, m, bit):
        if m and (track, m) not in waited:
            copies[(track, m)].wait_recv()
            waited.add((track, m))
        lands = track * count + (m ^ bit)
        copy = pltpu.make_async_remote_copy(
            src_ref=spots[track][m] if m else own[track],
            dst_ref=spots[track][m ^ bit],
            send_sem=send_sems.at[lands],
            recv_sem=recv_sems.at[lands],
            device_id=(dp, me ^ bit),
            device_id_type=pl.DeviceIdType.MESH,
        )
        copy.start()
        copies[(track, m ^ bit)] = copy

    plan_far, plan_near = gather_plan(count)
    far, near = [], []
    if with_small:
        far += [(2 * big, m, bit) for half, m, bit in plan_far if half == 0]
        near += [(2 * big, m, bit) for half, m, bit in plan_near if half == 0]
    for half, m, bit in plan_far:
        far += [(2 * a + half, m, bit) for a in range(big)]
    for half, m, bit in plan_near:
        near += [(2 * a + half, m, bit) for a in range(big)]
    done = set()
    for entry in far:
        send(*entry)
        for other in near:
            if other not in done and (other[1] == 0 or (other[0], other[1]) in waited):
                done.add(other)
                send(*other)
    for other in near:
        if other not in done:
            send(*other)
    for key, copy in copies.items():
        if key not in waited:
            copy.wait_recv()
    for copy in copies.values():
        copy.wait_send()
    for copy in local:
        copy.wait()


def gather_now(arrays, small, collective_id, microseconds):
    count = lax.axis_size("ctx")
    shapes = [
        jax.ShapeDtypeStruct((2 * count, x.shape[0] // 2, x.shape[1]), x.dtype) for x in arrays
    ]
    shapes.append(jax.ShapeDtypeStruct((count, *small.shape), small.dtype))
    tracks = 2 * len(arrays) + 1
    return pl.pallas_call(
        functools.partial(gather_kernel, count, len(arrays), 1),
        in_specs=[pl.BlockSpec(memory_space=pl.ANY)] * len(shapes),
        out_specs=[pl.BlockSpec(memory_space=pltpu.HBM)] * len(arrays)
        + [pl.BlockSpec(memory_space=pl.ANY)],
        out_shape=shapes,
        scratch_shapes=[
            pltpu.SemaphoreType.DMA((tracks * count,)),
            pltpu.SemaphoreType.DMA((tracks * count,)),
            pltpu.SemaphoreType.DMA((tracks,)),
        ],
        compiler_params=pltpu.CompilerParams(
            collective_id=collective_id, has_side_effects=True, vmem_limit_bytes=4 * 2**20
        ),
        cost_estimate=cost(microseconds),
        name="gather_rows",
    )(*arrays, small)


def split_rows(values, parts):
    rows = values.shape[0] // parts
    return [values[i * rows : (i + 1) * rows] for i in range(parts)]


def pin(arrays, *others):
    held = lax.optimization_barrier((tuple(arrays), *others))
    return (list(held[0]), *held[1:])


def gather_steps(values):
    count = lax.axis_size("ctx")
    orders = bit_orders(count)
    names, held = [[0], [0]], [[piece] for piece in split_rows(values, 2)]
    for depth in range(len(orders[0])):
        came = []
        for half in (0, 1):
            sent = jnp.concatenate(held[half], axis=0) if depth else held[half][0]
            came.append(exchange(sent, orders[half][depth], count))
        came = yield came
        for half in (0, 1):
            held[half] = held[half] + split_rows(came[half], len(held[half]))
            names[half] = names[half] + [m ^ orders[half][depth] for m in names[half]]
    halves = [dict(zip(names[half], held[half])) for half in (0, 1)]
    own = jnp.stack(
        [jnp.concatenate([half[m] for half in halves], axis=0) for m in range(0, count, 2)]
    )
    (other,) = yield [exchange(own, 1, count)]
    return jnp.stack([own, other], axis=1).reshape(count * values.shape[0], *values.shape[1:])


def add_low(left, right):
    return (left.astype(full) + right.astype(full)).astype(low)


def scatter_steps(odd, even):
    count = lax.axis_size("ctx")
    parts = count // 2
    (came,) = yield [exchange(odd, 1, count)]
    pairs = list(zip(split_rows(even, parts), split_rows(came, parts)))
    orders = bit_orders(count)
    held = [
        {
            2 * n: add_low(split_rows(left, 2)[half], split_rows(right, 2)[half])
            for n, (left, right) in enumerate(pairs)
        }
        for half in (0, 1)
    ]
    for depth in range(len(orders[0])):
        names, came = [], []
        for half in (0, 1):
            bit = orders[half][depth]
            names.append([m for m in held[half] if m & bit])
            sent = [held[half][m] for m in names[half]]
            sent = jnp.concatenate(sent, axis=0) if len(sent) > 1 else sent[0]
            came.append(exchange(sent, bit, count))
        came = yield came
        for half in (0, 1):
            bit = orders[half][depth]
            pieces = split_rows(came[half], len(names[half]))
            held[half] = {
                m ^ bit: add_low(held[half][m ^ bit], x) for m, x in zip(names[half], pieces)
            }
    return jnp.concatenate([half[0] for half in held], axis=0)


def scatter_kernel(count, odd_ref, even_ref, out_ref, sums, came, near_sems, far_send, far_recv):
    me = lax.axis_index("ctx")
    dp = lax.axis_index("dp")
    orders = bit_orders(count)
    bits = orders[0] + [1]
    parts = count // 2
    rows = even_ref.shape[2]
    tile = min(32, rows)
    barrier = pltpu.get_barrier_semaphore()
    for bit in bits:
        pl.semaphore_signal(
            barrier, inc=1, device_id=(dp, me ^ bit), device_id_type=pl.DeviceIdType.MESH
        )
    pl.semaphore_wait(barrier, len(bits))
    first = sorted(range(parts), key=lambda n: -bin(n).count("1"))
    near = {}
    for n in first:
        near[n] = pltpu.make_async_remote_copy(
            src_ref=odd_ref.at[n],
            dst_ref=sums.at[n],
            send_sem=near_sems.at[0, n],
            recv_sem=near_sems.at[1, n],
            device_id=(dp, me ^ 1),
            device_id_type=pl.DeviceIdType.MESH,
        )
        near[n].start()

    def add(into, left, right):
        def body(step, carry):
            span = pl.ds(pl.multiple_of(step * tile, tile), tile)
            total = left[span, :].astype(full) + right[span, :].astype(full)
            into[span, :] = total.astype(into.dtype)
            return carry

        lax.fori_loop(0, rows // tile, body, 0)

    far = []
    used = [0, 0]

    def send(half, n, bit):
        place = used[half]
        used[half] += 1
        copy = pltpu.make_async_remote_copy(
            src_ref=sums.at[n, half],
            dst_ref=came.at[half, place],
            send_sem=far_send.at[half, place],
            recv_sem=far_recv.at[half, place],
            device_id=(dp, me ^ bit),
            device_id_type=pl.DeviceIdType.MESH,
        )
        copy.start()
        far.append(copy)
        return copy, place

    pending = [{}, {}]
    for n in first:
        near[n].wait_recv()
        for half in (0, 1):
            add(sums.at[n, half], sums.at[n, half], even_ref.at[n, half])
            bit = orders[half][0]
            if 2 * n & bit:
                pending[half][n] = send(half, n, bit)
    depth_count = len(orders[0])
    for depth in range(depth_count):
        later = [{}, {}]
        waiting = [(half, n) for k in range(parts) for half in (0, 1) for n in list(pending[half])[k : k + 1]]
        for half, n in waiting:
            copy, place = pending[half][n]
            keep = n ^ (orders[half][depth] >> 1)
            copy.wait_recv()
            if depth + 1 == depth_count:
                add(out_ref.at[half], sums.at[keep, half], came.at[half, place])
            else:
                add(sums.at[keep, half], sums.at[keep, half], came.at[half, place])
                bit = orders[half][depth + 1]
                if 2 * keep & bit:
                    later[half][keep] = send(half, keep, bit)
        pending = later
    for n in first:
        near[n].wait_send()
    for copy in far:
        copy.wait_send()


def scatter_now(odd, even, collective_id):
    count = lax.axis_size("ctx")
    parts = count // 2
    rows = odd.shape[0] // parts // 2
    shape = (parts, 2, rows, odd.shape[1])
    out = pl.pallas_call(
        functools.partial(scatter_kernel, count),
        in_specs=[pl.BlockSpec(memory_space=pl.ANY), pl.BlockSpec(memory_space=pltpu.VMEM)],
        out_specs=pl.BlockSpec(memory_space=pltpu.VMEM),
        out_shape=jax.ShapeDtypeStruct((2, rows, odd.shape[1]), full),
        scratch_shapes=[
            pltpu.VMEM(shape, low),
            pltpu.VMEM((2, parts - 1, rows, odd.shape[1]), low),
            pltpu.SemaphoreType.DMA((2, parts)),
            pltpu.SemaphoreType.DMA((2, parts - 1)),
            pltpu.SemaphoreType.DMA((2, parts - 1)),
        ],
        compiler_params=pltpu.CompilerParams(
            collective_id=collective_id, has_side_effects=True, vmem_limit_bytes=40 * 2**20
        ),
        cost_estimate=cost(90),
        name="scatter_rows",
    )(odd.reshape(shape), even.reshape(shape))
    return out.reshape(2 * rows, odd.shape[1])


def advance(steps, came):
    try:
        return (steps.send(came), None)
    except StopIteration as stop:
        return (None, stop.value)


def finish(steps, came):
    value = None
    while value is None:
        came, value = advance(steps, came)
    return value


def over_dp(grad, dim):
    return lax.psum_scatter(grad, "dp", scatter_dimension=dim, tiled=True)


def odd_first(step, count):
    return lax.rem(2 * step + 1, count + 1)


def swap_ctx(values):
    return lax.all_to_all(values, "ctx", split_axis=0, concat_axis=0, tiled=True)


def on_device(
    hidden_in,
    in_gain,
    w_query,
    b_query,
    w_key,
    b_key,
    w_value,
    b_value,
    w_out,
    ffn_gain,
    w_router,
    exp_gate,
    exp_up,
    exp_down,
    sh_gate,
    sh_up,
    sh_down,
    sh_mix,
    routes,
    priority,
    blocks,
    cotangent,
):
    both = ("dp", "ctx")
    ctx_count = lax.axis_size("ctx")
    ctx_index = lax.axis_index("ctx")
    dp_count = lax.axis_size("dp")
    dp_index = lax.axis_index("dp")
    tokens_low = hidden_in[0]
    tokens = tokens_low.astype(full)
    cot_low = cotangent[0]
    cot_full = cotangent[0].astype(full)
    tok_count = tokens.shape[0]
    group_len = tok_count * ctx_count
    shard = w_query.shape[0]
    experts_total = ctx_count * exp_gate.shape[0]
    capacity = 5 * tok_count * TOP_K // (4 * experts_total)
    repeat = max(1, ctx_count // HEADS)
    heads = max(1, HEADS // ctx_count)
    width = heads * HEAD_DIM
    head_sets = HEADS // heads

    def by_heads(weight):
        parts = weight.reshape(shard, head_sets, width).transpose(1, 0, 2)
        return jnp.repeat(parts, repeat, axis=0) if repeat > 1 else parts

    qkv_parts = swap_ctx(
        jnp.concatenate([by_heads(w_query), by_heads(w_key), by_heads(w_value)], axis=2)
    )
    w_qkv = lax.all_gather(
        qkv_parts.reshape(ctx_count * shard, 3 * width), "dp", axis=0, tiled=True
    )
    partners = jnp.arange(ctx_count, dtype=jnp.int32) ^ ctx_index
    small = jnp.concatenate(
        [
            jnp.stack([in_gain, b_query, b_key, b_value, ffn_gain, sh_mix], axis=0),
            w_router.T,
        ],
        axis=0,
    ).astype(full)
    small_count = small.shape[0]
    small_rows = -(-dp_count * small_count * shard // HEAD_DIM // 8) * 8
    around = [small] + [
        lax.ppermute(small, "dp", [(i, (i + k) % dp_count) for i in range(dp_count)])
        for k in range(1, dp_count)
    ]
    origin = (dp_index - jnp.arange(dp_count, dtype=jnp.int32)) % dp_count
    small = jnp.take(jnp.stack(around), origin, axis=0).reshape(-1)
    small = jnp.pad(small, (0, small_rows * HEAD_DIM - small.shape[0])).reshape(small_rows, HEAD_DIM)
    w_out, small = lax.optimization_barrier((w_out, small))
    out_around = jnp.stack(
        [w_out]
        + [
            lax.ppermute(w_out, "dp", [(i, (i + k) % dp_count) for i in range(dp_count)])
            for k in range(1, dp_count)
        ]
    )
    x_blocks, cot_all, small_all = gather_now([tokens_low, cot_low], small, 0, 145)
    cot_all = cot_all.reshape(group_len, D)
    small_all = small_all.reshape(ctx_count, -1)[:, : dp_count * small_count * shard]
    small_all = jnp.take(small_all, partners, axis=0)
    small_all = (
        small_all.reshape(ctx_count, dp_count, small_count, shard)
        .transpose(2, 1, 0, 3)
        .reshape(small_count, shard * dp_count * ctx_count)
    )
    gain_one, gain_two, mix_row = small_all[0:1], small_all[4:5], small_all[5:6]
    mix_router = small_all[5:].astype(low)
    out_mine = jnp.concatenate(
        [lax.dynamic_index_in_dim(out_around, origin[p], 0, False) for p in range(dp_count)], axis=0
    )
    (out_mine,), x_blocks = pin([out_mine], x_blocks)
    out_steps = gather_steps(out_mine)
    out_came = next(out_steps)
    shared_gate, shared_up, shared_down = (
        lax.all_gather(sh_gate.T, "dp", axis=0, tiled=True),
        lax.all_gather(sh_up.T, "dp", axis=0, tiled=True),
        lax.all_gather(sh_down, "dp", axis=0, tiled=True),
    )
    expert_gate, expert_up, expert_down = (
        lax.all_gather(exp_gate[0], "dp", axis=0, tiled=True),
        lax.all_gather(exp_up[0], "dp", axis=0, tiled=True),
        lax.all_gather(exp_down[0], "dp", axis=1, tiled=True),
    )

    route_ids = routes[0]
    flat_ids = route_ids.reshape(-1)
    order = priority[0, 0]
    earlier = (flat_ids[:, None] == flat_ids[None, :]) & (order[None, :] < order[:, None])
    ranks = jnp.sum(earlier.astype(jnp.int32), axis=1).reshape(route_ids.shape)
    expert_grid = jnp.arange(experts_total, dtype=jnp.int32)
    route_hits = route_ids[None, :, :] == expert_grid[:, None, None]
    code = jnp.sum(jnp.where(route_hits, ranks[None] + 1, 0), axis=2) - 1

    stored_to_place = blocks[0]
    block_count = stored_to_place.shape[0]
    block_grid = jnp.arange(block_count, dtype=jnp.int32)
    place_to_stored = jnp.sum(
        jnp.where(stored_to_place[None, :] == block_grid[:, None], block_grid[None, :], 0), axis=1
    )
    per_device = block_count // ctx_count
    near = partners * per_device
    stored_near = jnp.concatenate(
        [
            lax.dynamic_slice_in_dim(stored_to_place, near[m], per_device)
            for m in range(ctx_count)
        ]
    )
    place_to_near = (place_to_stored // per_device ^ ctx_index) * per_device + (
        place_to_stored % per_device
    )
    cosine_wide, sine_wide = rope_tables(group_len)
    my_heads = (ctx_index // repeat) * width
    scale_one = rms_scale(tokens)
    bias = lax.dynamic_slice_in_dim(small_all[1:4], my_heads, width, 1).reshape(1, 3 * width)
    normed_sorted, query, key, value = project(
        x_blocks, stored_near, gain_one, w_qkv, bias, cosine_wide, sine_wide
    )
    tiles = group_len // CONT
    direct = block_count == tiles
    at = place_to_stored if direct else jnp.arange(tiles, dtype=jnp.int32)
    out_came, query = pin(out_came, query)
    out_came, out_parts = advance(out_steps, out_came)
    attended_heads, lses, parts = [], [], []
    value_t = value.T
    for head in range(heads):
        one_head, lse = attention_forward(query, key, value_t, at, head)
        if head == 0:
            (*out_came, query), one_head = pin([*out_came, query], one_head)
            out_came, out_parts = advance(out_steps, out_came)
        attended_heads.append(one_head)
        lses.append(lse)
        stored_head = one_head if direct else take_blocks(one_head, stored_to_place)
        parts.append(swap_ctx(stored_head.reshape(ctx_count, tok_count, HEAD_DIM))[::repeat])
    if out_parts is None:
        out_came, parts[-1] = pin(out_came, parts[-1]) if heads == 1 else (out_came, parts[-1])
        out_parts = finish(out_steps, out_came)
    out_parts = out_parts.reshape(ctx_count, dp_count, shard, D)
    out_full = (
        jnp.stack(
            [lax.dynamic_index_in_dim(out_parts, partners[i], 0, False) for i in range(ctx_count)],
            axis=1,
        )
    ).reshape(D, D)
    attended_parts = jnp.stack(parts, axis=2).reshape(head_sets, tok_count, width)
    attended = attended_parts.transpose(1, 0, 2).reshape(tok_count, D)
    first_sum = tokens + dot(attended, out_full)
    scale_two = rms_scale(first_sum)
    normed_two = (first_sum * scale_two * gain_two).astype(low)
    logits = dot_nt(normed_two, mix_router)
    mix_mine = jax.nn.sigmoid(logits[:, 0:1])
    chosen = code.T >= 0
    masked = jnp.where(chosen, logits[:, 1:], masked_score)
    raised = jnp.where(chosen, jnp.exp(masked - jnp.max(masked, axis=1, keepdims=True)), 0.0)
    gates_mine = raised / jnp.sum(raised, axis=1, keepdims=True)
    narrow = jnp.concatenate([mix_mine.T, gates_mine.T, code.astype(full)], axis=0)
    narrow = jnp.pad(narrow, ((0, -narrow.shape[0] % 8), (0, 0)))
    all_normed, narrow_all = gather_now([normed_two], narrow, 1, 75)
    all_normed = all_normed.reshape(group_len, D)
    mix_all = narrow_all[:, 0].reshape(group_len, 1)
    gate_mine = lax.dynamic_index_in_dim(narrow_all, ctx_index + 1, 1, keepdims=False)
    code_mine = lax.dynamic_index_in_dim(
        narrow_all, ctx_index + 1 + experts_total, 1, keepdims=False
    ).astype(jnp.int32)
    code_mine = jnp.where(code_mine < capacity, code_mine, -1)
    slot_rows = -(-capacity // 32) * 32
    expert_rows, slot_grads, hidden_low, gate_grad, up_grad, gate_share, dx_routed, out_routed = (
        routed_expert(
            all_normed, cot_all, code_mine, gate_mine, expert_gate, expert_up, expert_down, slot_rows
        )
    )
    grad_egate = ein("crd,crf->df", expert_rows, gate_grad).astype(low)
    grad_eup = ein("crd,crf->df", expert_rows, up_grad).astype(low)
    dx_routed, grad_egate, grad_eup = lax.optimization_barrier((dx_routed, grad_egate, grad_eup))
    sum_egate, sum_eup = over_dp(grad_egate, 0), over_dp(grad_eup, 0)
    mix_cot, shared_low, shared_dg, shared_du, mix_share, dx_odd, dx_even, out_odd, out_even = (
        shared_expert(
            all_normed, cot_all, mix_all, shared_gate, shared_up, shared_down,
            dx_routed, out_routed, tok_count,
        )
    )
    dx_steps = scatter_steps(dx_odd, dx_even)
    came = next(dx_steps)
    grad_edown = ein("crf,crd->fd", hidden_low, slot_grads).astype(low)
    came, grad_edown, sum_egate, shared_low, shared_dg, shared_du = pin(
        came, grad_edown, sum_egate, shared_low, shared_dg, shared_du
    )
    sum_edown = over_dp(grad_edown, 1)
    came, dx_mine = advance(dx_steps, came)
    grad_sdown = ein("tf,td->fd", shared_low, mix_cot).astype(low)
    grad_sgate = ein("tf,td->fd", shared_dg, all_normed).astype(low)
    came, grad_sdown, grad_sgate, shared_du = pin(came, grad_sdown, grad_sgate, shared_du)
    sum_sdown, sum_sgate = over_dp(grad_sdown, 0), over_dp(grad_sgate, 0)
    came, dx_mine = advance(dx_steps, came)
    grad_sup = ein("tf,td->fd", shared_du, all_normed).astype(low)
    came, grad_sup = pin(came, grad_sup)
    sum_sup = over_dp(grad_sup, 0)
    dx_mine = finish(dx_steps, came).astype(full)

    shares = jnp.stack([gate_share[:, 0], mix_share.reshape(ctx_count, tok_count)], axis=1)
    shares = swap_ctx(jnp.take(shares, partners, axis=0))
    gate_shares = shares[:, 0].T
    mix_grad = jnp.sum(shares[:, 1], axis=0)[:, None] * (1.0 - mix_mine)
    logit_grad = gate_shares - gates_mine * jnp.sum(gate_shares, axis=1, keepdims=True)
    narrow_low = logit_grad.astype(low)
    grad_narrow = jnp.concatenate(
        [
            jnp.sum(mix_grad * normed_two.astype(full), axis=0, keepdims=True),
            ein("te,td->ed", narrow_low, normed_two),
        ],
        axis=0,
    )
    (out_odd,), dx_mine = pin([out_odd], dx_mine)
    add_steps = scatter_steps(out_odd, out_even)
    came = next(add_steps)
    normed_grad = dx_mine + mix_grad * mix_row + dot(narrow_low, mix_router[1:])
    norm_grad_two, grad_gain_two = norm_back(first_sum, scale_two, gain_two, normed_grad)
    first_grad = cot_full + norm_grad_two
    first_low = first_grad.astype(low)
    attended_grad = dot_nt(first_low, out_full).astype(low)
    grad_out = ein("td,te->de", attended, first_low).astype(low)

    upstream_parts = attended_grad.reshape(tok_count, head_sets, heads, HEAD_DIM)
    upstream_parts = [upstream_parts[:, :, head].transpose(1, 0, 2) for head in range(heads)]
    if repeat > 1:
        upstream_parts = [jnp.repeat(part, repeat, axis=0) for part in upstream_parts]
    came, upstream_parts[0], sum_eup = pin(came, upstream_parts[0], sum_eup)
    came, added = advance(add_steps, came)
    upstreams = [swap_ctx(part).reshape(group_len, HEAD_DIM) for part in upstream_parts]
    (grad_out,), upstreams[0] = pin([grad_out], upstreams[0])
    grad_out = grad_out.reshape(dp_count, ctx_count, shard, D)

    def out_rows_of(first):
        return jnp.concatenate(
            [
                lax.dynamic_index_in_dim(grad_out, partners[m], 1, False).reshape(-1, D)
                for m in range(first, ctx_count, 2)
            ],
            axis=0,
        )

    wout_steps = scatter_steps(out_rows_of(1), out_rows_of(0))
    wout_came = next(wout_steps)
    key_t = key.T
    head_grads = []
    for head in range(heads):
        upstream = upstreams[head] if direct else take_blocks(upstreams[head], place_to_stored)
        grads = attention_backward(
            query, upstream, attended_heads[head], lses[head], key, key_t, value,
            cosine_wide, sine_wide, at, head,
        )
        grads = list(grads)
        if head == 0:
            wout_came, grads[0] = pin(wout_came, grads[0])
            wout_came, wout = advance(wout_steps, wout_came)
        head_grads.append(grads)
    came, last, sum_edown = pin(came, head_grads[-1][0], sum_edown)
    head_grads[-1][0] = last
    came, added = advance(add_steps, came)
    qkv_grads = jnp.concatenate(
        [head_grads[head][kind] for kind in range(3) for head in range(heads)], axis=1
    )
    if repeat > 1:
        qkv_grads = jnp.where(ctx_index % repeat == 0, qkv_grads, jnp.zeros_like(qkv_grads))
    wout_came, qkv_grads = pin(wout_came, qkv_grads)
    wout_came, wout = advance(wout_steps, wout_came)
    grad_qkv = ein("td,te->de", normed_sorted, qkv_grads).astype(low)
    bias_sums = jnp.sum(qkv_grads.astype(full), axis=0).reshape(3, width)
    grad_bias = lax.dynamic_update_slice_in_dim(
        jnp.zeros((3, D), full), bias_sums, my_heads, 1
    )
    came, grad_qkv, qkv_grads = pin(came, grad_qkv, qkv_grads)
    odd_one, even_one, gain_sums = unproject(
        qkv_grads, stored_near, w_qkv, normed_sorted, per_device
    )
    grad_gain_one = gain_sums[0] / gain_one[0]
    added = finish(add_steps, came)
    layer_out = first_sum + added.astype(full)
    wout_came, odd_one = pin(wout_came, odd_one)
    wout = finish(wout_steps, wout_came)
    (wout,), odd_one, sum_sdown = pin([wout], odd_one, sum_sdown)
    qkv_rows = lax.psum_scatter(
        grad_qkv.reshape(dp_count, ctx_count, shard, 3 * width),
        "dp",
        scatter_dimension=0,
        tiled=True,
    )[0]
    wout_rows = lax.psum_scatter(
        wout.reshape(dp_count, shard, D), "dp", scatter_dimension=0, tiled=True
    )[0]
    dx_one = scatter_now(odd_one, even_one, 2)
    (sum_sgate, sum_sup, qkv_rows, wout_rows), dx_one = pin(
        [sum_sgate, sum_sup, qkv_rows, wout_rows], dx_one
    )
    norm_grad_one, _ = norm_back(tokens, scale_one, gain_one, dx_one)
    input_grad = first_grad + norm_grad_one

    qkv_mine = swap_ctx(qkv_rows)[::repeat].astype(full)
    qkv_mine = qkv_mine.reshape(head_sets, shard, 3, width).transpose(2, 1, 0, 3).reshape(3, shard, D)
    grad_wout = wout_rows.astype(full)
    small_grads = jnp.concatenate(
        [grad_gain_one[None], grad_bias, grad_gain_two[None], grad_narrow], axis=0
    )
    small_grads = small_grads.reshape(-1, dp_count, ctx_count, shard).transpose(2, 1, 0, 3)
    small_grads = jnp.sum(swap_ctx(small_grads), axis=0)
    small_grads = jnp.sum(
        lax.all_to_all(small_grads, "dp", split_axis=0, concat_axis=0, tiled=True), axis=0
    ).T

    return (
        layer_out.astype(low)[None],
        input_grad[None],
        small_grads[:, 0],
        qkv_mine[0],
        small_grads[:, 1],
        qkv_mine[1],
        small_grads[:, 2],
        qkv_mine[2],
        small_grads[:, 3],
        grad_wout,
        small_grads[:, 4],
        small_grads[:, 6:],
        sum_egate.astype(full)[None],
        sum_eup.astype(full)[None],
        sum_edown.astype(full)[None],
        sum_sgate.astype(full).T,
        sum_sup.astype(full).T,
        sum_sdown.astype(full),
        small_grads[:, 5],
    )


def solution(mesh):
    rows = P("dp", "ctx", None)
    flat = P(("dp", "ctx"))
    lines = P(("dp", "ctx"), None)
    columns = P(None, ("dp", "ctx"))
    deep = P("ctx", "dp", None)
    down = P("ctx", None, "dp")
    in_specs = (
        (rows, flat, lines, flat, lines, flat, lines, flat, lines, flat, lines)
        + (deep, deep, down, columns, columns, lines, flat)
        + (rows, rows, P("dp", None), rows)
    )
    out_specs = (
        (rows, rows, flat, lines, flat, lines, flat, lines, flat, lines, flat, lines)
        + (deep, deep, down, columns, columns, lines, flat)
    )
    return jax.shard_map(
        on_device, mesh=mesh, in_specs=in_specs, out_specs=out_specs, check_vma=False
    )
```

```python
import functools

import jax
import jax.numpy as jnp
import numpy as np
from jax import lax
from jax.experimental import pallas as pl
from jax.experimental.pallas import tpu as pltpu
from jax.sharding import PartitionSpec as P

D = 2048
HEADS = 16
HEAD_DIM = 128
TOP_K = 4
CONT = 256
PROMPT = 2048

rope_base = 1000000.0
epsilon = 1e-06
masked_score = -1e30
log2_e = 1.4426950408889634
low = jnp.bfloat16
full = jnp.float32


def dot(left, right):
    return jnp.dot(left, right, preferred_element_type=full)


def dot_nt(left, right):
    return lax.dot_general(left, right, (((1,), (1,)), ((), ())), preferred_element_type=full)


def ein(spec, left, right):
    return jnp.einsum(spec, left, right, preferred_element_type=full)


def rotate(values, cosine, sine):
    middle = values.shape[-1] // 2
    leading = values[..., :middle]
    trailing = values[..., middle:]
    return jnp.concatenate(
        [leading * cosine - trailing * sine, trailing * cosine + leading * sine], axis=-1
    )


def rope_tables(rows):
    places = np.arange(rows)
    turned = np.where(places < PROMPT, places, PROMPT + (places - PROMPT) % CONT)
    frequency = rope_base ** (-2.0 * np.arange(HEAD_DIM // 2, dtype=np.float64) / HEAD_DIM)
    angles = turned.astype(np.float64)[:, None] * frequency[None, :]
    cosine, sine = np.cos(angles), np.sin(angles)
    wide = np.concatenate([cosine, cosine], axis=1), np.concatenate([-sine, sine], axis=1)
    return tuple(jnp.asarray(table.astype(np.float32)) for table in wide)


def rms_scale(values):
    return lax.rsqrt(jnp.mean(values * values, axis=-1, keepdims=True) + epsilon)


def norm_back(values, scale_rows, gain_row, upstream):
    weighted = upstream * gain_row
    grad_gain = jnp.sum(upstream * values * scale_rows, axis=0)
    grad_values = scale_rows * weighted - values * scale_rows**3 * jnp.mean(
        weighted * values, axis=-1, keepdims=True
    )
    return (grad_values, grad_gain)


def silu_parts(values):
    sig_value = jax.nn.sigmoid(values)
    return (values * sig_value, sig_value * (1.0 + values * (1.0 - sig_value)))


def cost(microseconds):
    return pl.CostEstimate(
        flops=int(microseconds * 1.1e9),
        bytes_accessed=int(microseconds * 3.3e6),
        transcendentals=0,
    )


WIDE = 4


def attend_tiles(index, chunk, carry):
    whole = jnp.minimum(index, PROMPT // CONT)
    wide = whole // WIDE
    carry = lax.fori_loop(
        0, wide, lambda step, c: chunk(step * (WIDE * CONT), WIDE * CONT, False, c), carry
    )
    carry = lax.fori_loop(
        wide * WIDE, whole, lambda step, c: chunk(step * CONT, CONT, False, c), carry
    )
    return chunk(index * CONT, CONT, True, carry)


def turn(values, cosine, sine):
    half = HEAD_DIM // 2
    swapped = jnp.concatenate([values[:, half:], values[:, :half]], axis=1)
    return values * cosine + swapped * sine


def project_kernel(
    place_ref, x_ref, gain_ref, w_ref, bias_ref, cos_ref, sin_ref, normed_ref, q_ref, k_ref, v_ref
):
    values = x_ref[0].astype(full)
    scale = lax.rsqrt(jnp.mean(values * values, axis=1, keepdims=True) + epsilon)
    normed = (values * scale * gain_ref[...]).astype(low)
    normed_ref[...] = normed
    width = q_ref.shape[1]
    projected = dot(normed, w_ref[...]) + bias_ref[...]
    cosine, sine = cos_ref[...], sin_ref[...]
    for start in range(0, width, HEAD_DIM):
        for kind, out in ((0, q_ref), (1, k_ref)):
            column = kind * width + start
            head = projected[:, column : column + HEAD_DIM]
            out[:, start : start + HEAD_DIM] = turn(head, cosine, sine).astype(low)
    v_ref[...] = projected[:, 2 * width :].astype(low)


def project(x_blocks, places, gain, weight, bias, cosine, sine):
    count, rows, _ = x_blocks.shape
    width = bias.shape[1] // 3
    at_place = lambda g, place: (place[g], 0)
    whole = lambda g, place: (0, 0)
    tile = pl.BlockSpec((rows, width), at_place)
    head = jax.ShapeDtypeStruct((count * rows, width), low)
    return pl.pallas_call(
        project_kernel,
        grid_spec=pltpu.PrefetchScalarGridSpec(
            num_scalar_prefetch=1,
            grid=(count,),
            in_specs=[
                pl.BlockSpec((1, rows, D), lambda g, place: (g, 0, 0)),
                pl.BlockSpec((1, D), whole),
                pl.BlockSpec((D, 3 * width), whole),
                pl.BlockSpec((1, 3 * width), whole),
                pl.BlockSpec((rows, HEAD_DIM), at_place),
                pl.BlockSpec((rows, HEAD_DIM), at_place),
            ],
            out_specs=[pl.BlockSpec((rows, D), at_place), tile, tile, tile],
        ),
        out_shape=[jax.ShapeDtypeStruct((count * rows, D), low), head, head, head],
        compiler_params=pltpu.CompilerParams(vmem_limit_bytes=40 * 2**20),
        cost_estimate=cost(24),
        name="project",
    )(places, x_blocks, gain, weight, bias, cosine, sine)


def unproject_kernel(place_ref, grad_ref, w_ref, normed_ref, odd_ref, even_ref, gain_ref):
    step = pl.program_id(0)
    middle = pl.num_programs(0) // 2
    total = dot_nt(grad_ref[...], w_ref[...])
    gain_part = jnp.sum(total * normed_ref[...].astype(full), axis=0, keepdims=True)

    @pl.when(step == 0)
    def _():
        gain_ref[...] = jnp.zeros_like(gain_ref)

    gain_ref[...] += gain_part

    @pl.when(step < middle)
    def _():
        odd_ref[...] = total.astype(low)

    @pl.when(step >= middle)
    def _():
        even_ref[...] = total.astype(low)


def unproject(grads, places, weight, normed, per_device):
    count = places.shape[0]
    rows = grads.shape[0] // count
    width = grads.shape[1]
    middle = count // 2

    def at_place(g, place):
        block = odd_first(g // per_device, count // per_device) * per_device + g % per_device
        return (place[block], 0)

    shape = jax.ShapeDtypeStruct((middle * rows, D), low)
    return pl.pallas_call(
        unproject_kernel,
        grid_spec=pltpu.PrefetchScalarGridSpec(
            num_scalar_prefetch=1,
            grid=(count,),
            in_specs=[
                pl.BlockSpec((rows, width), at_place),
                pl.BlockSpec((D, width), lambda g, place: (0, 0)),
                pl.BlockSpec((rows, D), at_place),
            ],
            out_specs=[
                pl.BlockSpec((rows, D), lambda g, place: (jnp.minimum(g, middle - 1), 0)),
                pl.BlockSpec((rows, D), lambda g, place: (jnp.maximum(g - middle, 0), 0)),
                pl.BlockSpec((1, D), lambda g, place: (0, 0)),
            ],
        ),
        out_shape=[shape, shape, jax.ShapeDtypeStruct((1, D), full)],
        compiler_params=pltpu.CompilerParams(vmem_limit_bytes=40 * 2**20),
        cost_estimate=cost(20),
        name="unproject",
    )(places, grads, weight, normed)


def dot_tn(left, right):
    return lax.dot_general(left, right, (((0,), (0,)), ((), ())), preferred_element_type=full)


def expert_kernel(
    normed_ref, cot_ref, code_ref, gate_ref, wg_ref, wu_ref, wd_ref,
    rows_ref, sg_ref, act_ref, dg_ref, du_ref, share_ref, dx_ref, out_ref,
):
    slots = rows_ref.shape[1]
    tok = normed_ref.shape[0]
    hits = code_ref[0] == lax.broadcasted_iota(jnp.int32, (slots, tok), 0)
    table_full = jnp.where(hits, 1.0, 0.0)
    gated = jnp.where(hits, gate_ref[0], 0.0)
    table = table_full.astype(low)
    rows = dot(table, normed_ref[...]).astype(low)
    rows_ref[0] = rows
    slot_gate = jnp.sum(gated, axis=1, keepdims=True)
    slot_grad = (dot(table, cot_ref[...]) * slot_gate).astype(low)
    sg_ref[0] = slot_grad
    gate = dot(rows, wg_ref[...])
    up = dot(rows, wu_ref[...])
    hidden = dot_nt(slot_grad, wd_ref[...])
    silu, slope = silu_parts(gate)
    act_full = silu * up
    act = act_full.astype(low)
    act_ref[0] = act
    dg = (hidden * up * slope).astype(low)
    du = (hidden * silu).astype(low)
    dg_ref[0] = dg
    du_ref[0] = du
    slot_share = jnp.sum(hidden * act_full, axis=1, keepdims=True)
    share_ref[0] = jnp.sum(table_full * slot_share, axis=0, keepdims=True)
    slot_dx = (dot_nt(dg, wg_ref[...]) + dot_nt(du, wu_ref[...])).astype(low)
    dx_ref[...] = dot_tn(table, slot_dx).astype(low)
    expert_y = dot(act, wd_ref[...]).astype(low)
    out_ref[...] = dot_tn(gated.astype(low), expert_y).astype(low)


def routed_expert(all_normed, cot_all, code, gate, w_gate, w_up, w_down, slots):
    count, tok = code.shape
    ff = w_gate.shape[1]
    chunk = pl.BlockSpec((tok, D), lambda m: (m, 0))
    line = pl.BlockSpec((1, 1, tok), lambda m: (m, 0, 0))

    def fixed(array):
        return pl.BlockSpec(array.shape, lambda m: (0, 0), pipeline_mode=pl.Buffered(1))

    def per_slot(last):
        return pl.BlockSpec((1, slots, last), lambda m: (m, 0, 0))

    def shape(*dims, dtype=low):
        return jax.ShapeDtypeStruct(dims, dtype)

    return pl.pallas_call(
        expert_kernel,
        grid=(count,),
        in_specs=[chunk, chunk, line, line, fixed(w_gate), fixed(w_up), fixed(w_down)],
        out_specs=[per_slot(D), per_slot(D), per_slot(ff), per_slot(ff), per_slot(ff), line, chunk, chunk],
        out_shape=[
            shape(count, slots, D),
            shape(count, slots, D),
            shape(count, slots, ff),
            shape(count, slots, ff),
            shape(count, slots, ff),
            shape(count, 1, tok, dtype=full),
            shape(count * tok, D),
            shape(count * tok, D),
        ],
        compiler_params=pltpu.CompilerParams(vmem_limit_bytes=60 * 2**20),
        cost_estimate=cost(140),
        name="routed_expert",
    )(all_normed, cot_all, code[:, None, :], gate[:, None, :], w_gate, w_up, w_down)


def shared_kernel(
    normed_ref, cot_ref, mix_ref, wg_ref, wu_ref, wd_ref, dxe_ref, oute_ref,
    mixcot_ref, act_ref, dg_ref, du_ref, share_ref, dx_odd, dx_even, out_odd, out_even,
):
    step = pl.program_id(0)
    middle = pl.num_programs(0) // 2
    normed = normed_ref[...]
    mix = mix_ref[...]
    mix_cot = (mix * cot_ref[...].astype(full)).astype(low)
    mixcot_ref[...] = mix_cot
    gate = dot_nt(normed, wg_ref[...])
    up = dot_nt(normed, wu_ref[...])
    hidden = dot_nt(mix_cot, wd_ref[...])
    silu, slope = silu_parts(gate)
    act_full = silu * up
    act = act_full.astype(low)
    act_ref[...] = act
    dg = (hidden * up * slope).astype(low)
    du = (hidden * silu).astype(low)
    dg_ref[...] = dg
    du_ref[...] = du
    share_ref[...] = jnp.sum(hidden * act_full, axis=1, keepdims=True)
    dx = dot(dg, wg_ref[...]) + dot(du, wu_ref[...]) + dxe_ref[...].astype(full)
    out = mix * dot(act, wd_ref[...]) + oute_ref[...].astype(full)

    @pl.when(step < middle)
    def _():
        dx_odd[...] = dx.astype(low)
        out_odd[...] = out.astype(low)

    @pl.when(step >= middle)
    def _():
        dx_even[...] = dx.astype(low)
        out_even[...] = out.astype(low)


def shared_expert(all_normed, cot_all, mix, w_gate_t, w_up_t, w_down, dx_routed, out_routed, tok):
    rows = all_normed.shape[0]
    ff = w_down.shape[0]
    count = rows // tok
    middle = count // 2
    chunk = pl.BlockSpec((tok, D), lambda g: (odd_first(g, count), 0))
    narrow = pl.BlockSpec((tok, ff), lambda g: (odd_first(g, count), 0))
    column = pl.BlockSpec((tok, 1), lambda g: (odd_first(g, count), 0))
    odd = pl.BlockSpec((tok, D), lambda g: (jnp.minimum(g, middle - 1), 0))
    even = pl.BlockSpec((tok, D), lambda g: (jnp.maximum(g - middle, 0), 0))
    fixed = pl.BlockSpec((ff, D), lambda g: (0, 0), pipeline_mode=pl.Buffered(1))
    narrow_shape = jax.ShapeDtypeStruct((rows, ff), low)
    half_shape = jax.ShapeDtypeStruct((rows // 2, D), low)
    return pl.pallas_call(
        shared_kernel,
        grid=(count,),
        in_specs=[chunk, chunk, column, fixed, fixed, fixed, chunk, chunk],
        out_specs=[chunk, narrow, narrow, narrow, column, odd, even, odd, even],
        out_shape=[
            jax.ShapeDtypeStruct((rows, D), low),
            narrow_shape,
            narrow_shape,
            narrow_shape,
            jax.ShapeDtypeStruct((rows, 1), full),
            half_shape,
            half_shape,
            half_shape,
            half_shape,
        ],
        compiler_params=pltpu.CompilerParams(vmem_limit_bytes=60 * 2**20),
        cost_estimate=cost(103),
        name="shared_expert",
    )(all_normed, cot_all, mix, w_gate_t, w_up_t, w_down, dx_routed, out_routed)


def forward_kernel(at_ref, q_ref, k_ref, vt_ref, o_ref, lse_ref):
    index = pl.program_id(0)
    query = q_ref[...]
    score_scale = HEAD_DIM ** (-0.5) * log2_e

    def chunk(start, size, diagonal, carry):
        highest, total, acc = carry
        start = pl.multiple_of(start, CONT)
        scores = dot_nt(k_ref[pl.ds(start, size), :], query) * score_scale
        if diagonal:
            keys = lax.broadcasted_iota(jnp.int32, scores.shape, 0)
            queries = lax.broadcasted_iota(jnp.int32, scores.shape, 1)
            scores = jnp.where(keys <= queries, scores, masked_score)
        newest = jnp.maximum(highest, jnp.max(scores, axis=0, keepdims=True))
        weights = jnp.exp2(scores - newest)
        shrink = jnp.exp2(highest - newest)
        total = total * shrink + jnp.sum(weights, axis=0, keepdims=True)
        acc = acc * shrink + dot(vt_ref[:, pl.ds(start, size)], weights.astype(low))
        return (newest, total, acc)

    highest, total, acc = attend_tiles(
        index,
        chunk,
        (
            jnp.full((1, CONT), masked_score, full),
            jnp.zeros((1, CONT), full),
            jnp.zeros((HEAD_DIM, CONT), full),
        ),
    )
    o_ref[...] = (acc / total).T.astype(low)
    lse_ref[...] = highest + jnp.log2(total)


def attention_forward(query, key, value_t, at, head):
    rows = query.shape[0]
    return pl.pallas_call(
        forward_kernel,
        grid_spec=pltpu.PrefetchScalarGridSpec(
            num_scalar_prefetch=1,
            grid=(rows // CONT,),
            in_specs=[
                pl.BlockSpec((CONT, HEAD_DIM), lambda i, at: (i, head)),
                pl.BlockSpec((rows, HEAD_DIM), lambda i, at: (0, head)),
                pl.BlockSpec((HEAD_DIM, rows), lambda i, at: (head, 0)),
            ],
            out_specs=[
                pl.BlockSpec((CONT, HEAD_DIM), lambda i, at: (at[i], 0)),
                pl.BlockSpec((1, CONT), lambda i, at: (0, i)),
            ],
        ),
        out_shape=[
            jax.ShapeDtypeStruct((rows, HEAD_DIM), low),
            jax.ShapeDtypeStruct((1, rows), full),
        ],
        compiler_params=pltpu.CompilerParams(vmem_limit_bytes=32 * 2**20),
        cost_estimate=cost(30),
        name="attend_forward",
    )(at, query, key, value_t)


def backward_kernel(
    at_ref, q_ref, do_ref, o_ref, lse_ref, k_ref, kt_ref, v_ref, cos_ref, sin_ref,
    dq_ref, dk_ref, dv_ref, dk_sum, dv_sum,
):
    index = pl.program_id(0)
    query = q_ref[...]
    upstream = do_ref[...]
    lse = lse_ref[...]
    product = upstream.astype(full) * o_ref[...].astype(full)
    delta = jnp.sum(product.T, axis=0, keepdims=True)
    scale = HEAD_DIM ** (-0.5)
    span_now = pl.ds(pl.multiple_of(index * CONT, CONT), CONT)

    @pl.when(index == 0)
    def _():
        dk_sum[...] = jnp.zeros_like(dk_sum)
        dv_sum[...] = jnp.zeros_like(dv_sum)

    def chunk(start, size, diagonal, acc):
        start = pl.multiple_of(start, CONT)
        span = pl.ds(start, size)
        scores = dot_nt(k_ref[span, :], query) * (scale * log2_e) - lse
        if diagonal:
            keys = lax.broadcasted_iota(jnp.int32, scores.shape, 0)
            queries = lax.broadcasted_iota(jnp.int32, scores.shape, 1)
            scores = jnp.where(keys <= queries, scores, masked_score)
        probs = jnp.exp2(scores)
        prob_grad = dot_nt(v_ref[span, :], upstream)
        score_grad = (probs * (prob_grad - delta)).astype(low)
        dv_sum[span, :] += dot(probs.astype(low), upstream)
        dk_sum[span, :] += dot(score_grad, query)
        return acc + dot(kt_ref[:, span], score_grad)

    acc = attend_tiles(index, chunk, jnp.zeros((HEAD_DIM, CONT), full))
    dq_ref[...] = turn(acc.T * scale, cos_ref[span_now, :], -sin_ref[span_now, :]).astype(low)

    @pl.when(index == pl.num_programs(0) - 1)
    def _():
        def finish(step, carry):
            span = pl.ds(pl.multiple_of(step * CONT, CONT), CONT)
            dk_ref[span, :] = turn(
                dk_sum[span, :] * scale, cos_ref[span, :], -sin_ref[span, :]
            ).astype(low)
            dv_ref[span, :] = dv_sum[span, :].astype(low)
            return carry

        lax.fori_loop(0, pl.num_programs(0), finish, 0)


def attention_backward(query, upstream, attended, lse, key, key_t, value, cosine, sine, at, head):
    rows = query.shape[0]
    tile = pl.BlockSpec((CONT, HEAD_DIM), lambda i, at: (i, head))
    stored = pl.BlockSpec((CONT, HEAD_DIM), lambda i, at: (at[i], 0))
    whole = pl.BlockSpec((rows, HEAD_DIM), lambda i, at: (0, head))
    table = pl.BlockSpec((rows, HEAD_DIM), lambda i, at: (0, 0))
    grad = jax.ShapeDtypeStruct((rows, HEAD_DIM), low)
    return pl.pallas_call(
        backward_kernel,
        grid_spec=pltpu.PrefetchScalarGridSpec(
            num_scalar_prefetch=1,
            grid=(rows // CONT,),
            in_specs=[
                tile,
                stored,
                stored,
                pl.BlockSpec((1, CONT), lambda i, at: (0, i)),
                whole,
                pl.BlockSpec((HEAD_DIM, rows), lambda i, at: (head, 0)),
                whole,
                table,
                table,
            ],
            out_specs=[pl.BlockSpec((CONT, HEAD_DIM), lambda i, at: (i, 0)), table, table],
            scratch_shapes=[
                pltpu.VMEM((rows, HEAD_DIM), full),
                pltpu.VMEM((rows, HEAD_DIM), full),
            ],
        ),
        out_shape=[grad, grad, grad],
        compiler_params=pltpu.CompilerParams(vmem_limit_bytes=48 * 2**20),
        cost_estimate=cost(38),
        name="attend_backward",
    )(at, query, upstream, attended, lse, key, key_t, value, cosine, sine)


def take_blocks(rows, order):
    count = order.shape[0]
    blocked = rows.reshape(count, rows.shape[0] // count, *rows.shape[1:])
    return jnp.concatenate(
        [lax.dynamic_index_in_dim(blocked, order[i], 0, keepdims=False) for i in range(count)], axis=0
    )


def bit_orders(count):
    bits = [1 << i for i in range(1, count.bit_length() - 1)]
    return bits, bits[::-1]


def exchange(values, bit, count):
    return lax.ppermute(values, "ctx", [(i, i ^ bit) for i in range(count)])


def gather_plan(count):
    plan = []
    orders = bit_orders(count)
    held = [[0], [0]]
    for depth in range(len(orders[0])):
        sends = [[(half, m, orders[half][depth]) for m in held[half]] for half in (0, 1)]
        plan += [send for pair in zip(*sends) for send in pair]
        for half in (0, 1):
            held[half] = held[half] + [m ^ orders[half][depth] for m in held[half]]
    return plan, [(half, m, 1) for m in held[0] for half in (0, 1)]


def gather_kernel(count, big, with_small, *refs):
    ins = refs[: big + with_small]
    outs = refs[big + with_small : 2 * (big + with_small)]
    send_sems, recv_sems, own_sems = refs[2 * (big + with_small) :]
    me = lax.axis_index("ctx")
    dp = lax.axis_index("dp")
    bits = bit_orders(count)[0] + [1]
    rows = ins[0].shape[0] // 2
    barrier = pltpu.get_barrier_semaphore()
    for bit in bits:
        pl.semaphore_signal(
            barrier, inc=1, device_id=(dp, me ^ bit), device_id_type=pl.DeviceIdType.MESH
        )
    pl.semaphore_wait(barrier, len(bits))
    own, spots = [], []
    for a in range(big):
        for half in (0, 1):
            own.append(ins[a].at[pl.ds(half * rows, rows)])
            spots.append([outs[a].at[2 * m + half] for m in range(count)])
    if with_small:
        own.append(ins[big])
        spots.append([outs[big].at[m] for m in range(count)])
    local = [
        pltpu.make_async_copy(own[t], spots[t][0], own_sems.at[t]) for t in range(len(own))
    ]
    for copy in local:
        copy.start()
    copies = {}
    waited = set()

    def send(track, m, bit):
        if m and (track, m) not in waited:
            copies[(track, m)].wait_recv()
            waited.add((track, m))
        lands = track * count + (m ^ bit)
        copy = pltpu.make_async_remote_copy(
            src_ref=spots[track][m] if m else own[track],
            dst_ref=spots[track][m ^ bit],
            send_sem=send_sems.at[lands],
            recv_sem=recv_sems.at[lands],
            device_id=(dp, me ^ bit),
            device_id_type=pl.DeviceIdType.MESH,
        )
        copy.start()
        copies[(track, m ^ bit)] = copy

    plan_far, plan_near = gather_plan(count)
    far, near = [], []
    if with_small:
        far += [(2 * big, m, bit) for half, m, bit in plan_far if half == 0]
        near += [(2 * big, m, bit) for half, m, bit in plan_near if half == 0]
    for half, m, bit in plan_far:
        far += [(2 * a + half, m, bit) for a in range(big)]
    for half, m, bit in plan_near:
        near += [(2 * a + half, m, bit) for a in range(big)]
    done = set()
    for entry in far:
        send(*entry)
        for other in near:
            if other not in done and (other[1] == 0 or (other[0], other[1]) in waited):
                done.add(other)
                send(*other)
    for other in near:
        if other not in done:
            send(*other)
    for key, copy in copies.items():
        if key not in waited:
            copy.wait_recv()
    for copy in copies.values():
        copy.wait_send()
    for copy in local:
        copy.wait()


def gather_now(arrays, small, collective_id, microseconds):
    count = lax.axis_size("ctx")
    shapes = [
        jax.ShapeDtypeStruct((2 * count, x.shape[0] // 2, x.shape[1]), x.dtype) for x in arrays
    ]
    inputs = list(arrays)
    if small is not None:
        inputs.append(small)
        shapes.append(jax.ShapeDtypeStruct((count, *small.shape), small.dtype))
    tracks = len(arrays) + len(inputs)
    return pl.pallas_call(
        functools.partial(gather_kernel, count, len(arrays), len(inputs) - len(arrays)),
        in_specs=[pl.BlockSpec(memory_space=pl.ANY)] * len(shapes),
        out_specs=[pl.BlockSpec(memory_space=pltpu.HBM)] * len(arrays)
        + [pl.BlockSpec(memory_space=pl.ANY)] * (len(inputs) - len(arrays)),
        out_shape=shapes,
        scratch_shapes=[
            pltpu.SemaphoreType.DMA((tracks * count,)),
            pltpu.SemaphoreType.DMA((tracks * count,)),
            pltpu.SemaphoreType.DMA((tracks,)),
        ],
        compiler_params=pltpu.CompilerParams(
            collective_id=collective_id, has_side_effects=True, vmem_limit_bytes=58 * 2**20
        ),
        cost_estimate=cost(microseconds),
        name="gather_rows",
    )(*inputs)


def split_rows(values, parts):
    rows = values.shape[0] // parts
    return [values[i * rows : (i + 1) * rows] for i in range(parts)]


def pin(arrays, *others):
    held = lax.optimization_barrier((tuple(arrays), *others))
    return (list(held[0]), *held[1:])


def gather_steps(values):
    count = lax.axis_size("ctx")
    orders = bit_orders(count)
    names, held = [[0], [0]], [[piece] for piece in split_rows(values, 2)]
    for depth in range(len(orders[0])):
        came = []
        for half in (0, 1):
            sent = jnp.concatenate(held[half], axis=0) if depth else held[half][0]
            came.append(exchange(sent, orders[half][depth], count))
        came = yield came
        for half in (0, 1):
            held[half] = held[half] + split_rows(came[half], len(held[half]))
            names[half] = names[half] + [m ^ orders[half][depth] for m in names[half]]
    halves = [dict(zip(names[half], held[half])) for half in (0, 1)]
    own = jnp.stack(
        [jnp.concatenate([half[m] for half in halves], axis=0) for m in range(0, count, 2)]
    )
    (other,) = yield [exchange(own, 1, count)]
    return jnp.stack([own, other], axis=1).reshape(count * values.shape[0], *values.shape[1:])


def add_low(left, right):
    return (left.astype(full) + right.astype(full)).astype(low)


def scatter_steps(odd, even):
    count = lax.axis_size("ctx")
    parts = count // 2
    (came,) = yield [exchange(odd, 1, count)]
    pairs = list(zip(split_rows(even, parts), split_rows(came, parts)))
    orders = bit_orders(count)
    held = [
        {
            2 * n: add_low(split_rows(left, 2)[half], split_rows(right, 2)[half])
            for n, (left, right) in enumerate(pairs)
        }
        for half in (0, 1)
    ]
    for depth in range(len(orders[0])):
        names, came = [], []
        for half in (0, 1):
            bit = orders[half][depth]
            names.append([m for m in held[half] if m & bit])
            sent = [held[half][m] for m in names[half]]
            sent = jnp.concatenate(sent, axis=0) if len(sent) > 1 else sent[0]
            came.append(exchange(sent, bit, count))
        came = yield came
        for half in (0, 1):
            bit = orders[half][depth]
            pieces = split_rows(came[half], len(names[half]))
            held[half] = {
                m ^ bit: add_low(held[half][m ^ bit], x) for m, x in zip(names[half], pieces)
            }
    return jnp.concatenate([half[0] for half in held], axis=0)


def scatter_kernel(count, odd_ref, even_ref, out_ref, sums, came, near_sems, far_send, far_recv):
    me = lax.axis_index("ctx")
    dp = lax.axis_index("dp")
    orders = bit_orders(count)
    bits = orders[0] + [1]
    parts = count // 2
    rows = even_ref.shape[2]
    tile = min(32, rows)
    barrier = pltpu.get_barrier_semaphore()
    for bit in bits:
        pl.semaphore_signal(
            barrier, inc=1, device_id=(dp, me ^ bit), device_id_type=pl.DeviceIdType.MESH
        )
    pl.semaphore_wait(barrier, len(bits))
    first = sorted(range(parts), key=lambda n: -bin(n).count("1"))
    near = {}
    for n in first:
        near[n] = pltpu.make_async_remote_copy(
            src_ref=odd_ref.at[n],
            dst_ref=sums.at[n],
            send_sem=near_sems.at[0, n],
            recv_sem=near_sems.at[1, n],
            device_id=(dp, me ^ 1),
            device_id_type=pl.DeviceIdType.MESH,
        )
        near[n].start()

    def add(into, left, right):
        def body(step, carry):
            span = pl.ds(pl.multiple_of(step * tile, tile), tile)
            total = left[span, :].astype(full) + right[span, :].astype(full)
            into[span, :] = total.astype(into.dtype)
            return carry

        lax.fori_loop(0, rows // tile, body, 0)

    far = []
    used = [0, 0]

    def send(half, n, bit):
        place = used[half]
        used[half] += 1
        copy = pltpu.make_async_remote_copy(
            src_ref=sums.at[n, half],
            dst_ref=came.at[half, place],
            send_sem=far_send.at[half, place],
            recv_sem=far_recv.at[half, place],
            device_id=(dp, me ^ bit),
            device_id_type=pl.DeviceIdType.MESH,
        )
        copy.start()
        far.append(copy)
        return copy, place

    pending = [{}, {}]
    for n in first:
        near[n].wait_recv()
        for half in (0, 1):
            add(sums.at[n, half], sums.at[n, half], even_ref.at[n, half])
            bit = orders[half][0]
            if 2 * n & bit:
                pending[half][n] = send(half, n, bit)
    depth_count = len(orders[0])
    for depth in range(depth_count):
        later = [{}, {}]
        waiting = [(half, n) for k in range(parts) for half in (0, 1) for n in list(pending[half])[k : k + 1]]
        for half, n in waiting:
            copy, place = pending[half][n]
            keep = n ^ (orders[half][depth] >> 1)
            copy.wait_recv()
            if depth + 1 == depth_count:
                add(out_ref.at[half], sums.at[keep, half], came.at[half, place])
            else:
                add(sums.at[keep, half], sums.at[keep, half], came.at[half, place])
                bit = orders[half][depth + 1]
                if 2 * keep & bit:
                    later[half][keep] = send(half, keep, bit)
        pending = later
    for n in first:
        near[n].wait_send()
    for copy in far:
        copy.wait_send()


def scatter_now(odd, even, collective_id):
    count = lax.axis_size("ctx")
    parts = count // 2
    rows = odd.shape[0] // parts // 2
    shape = (parts, 2, rows, odd.shape[1])
    out = pl.pallas_call(
        functools.partial(scatter_kernel, count),
        in_specs=[pl.BlockSpec(memory_space=pl.ANY), pl.BlockSpec(memory_space=pltpu.VMEM)],
        out_specs=pl.BlockSpec(memory_space=pltpu.VMEM),
        out_shape=jax.ShapeDtypeStruct((2, rows, odd.shape[1]), full),
        scratch_shapes=[
            pltpu.VMEM(shape, low),
            pltpu.VMEM((2, parts - 1, rows, odd.shape[1]), low),
            pltpu.SemaphoreType.DMA((2, parts)),
            pltpu.SemaphoreType.DMA((2, parts - 1)),
            pltpu.SemaphoreType.DMA((2, parts - 1)),
        ],
        compiler_params=pltpu.CompilerParams(
            collective_id=collective_id, has_side_effects=True, vmem_limit_bytes=40 * 2**20
        ),
        cost_estimate=cost(90),
        name="scatter_rows",
    )(odd.reshape(shape), even.reshape(shape))
    return out.reshape(2 * rows, odd.shape[1])


def advance(steps, came):
    try:
        return (steps.send(came), None)
    except StopIteration as stop:
        return (None, stop.value)


def finish(steps, came):
    value = None
    while value is None:
        came, value = advance(steps, came)
    return value


def over_dp(grad, dim):
    return lax.psum_scatter(grad, "dp", scatter_dimension=dim, tiled=True)


def odd_first(step, count):
    return lax.rem(2 * step + 1, count + 1)


def swap_ctx(values):
    return lax.all_to_all(values, "ctx", split_axis=0, concat_axis=0, tiled=True)


def on_device(
    hidden_in,
    in_gain,
    w_query,
    b_query,
    w_key,
    b_key,
    w_value,
    b_value,
    w_out,
    ffn_gain,
    w_router,
    exp_gate,
    exp_up,
    exp_down,
    sh_gate,
    sh_up,
    sh_down,
    sh_mix,
    routes,
    priority,
    blocks,
    cotangent,
):
    both = ("dp", "ctx")
    ctx_count = lax.axis_size("ctx")
    ctx_index = lax.axis_index("ctx")
    dp_count = lax.axis_size("dp")
    dp_index = lax.axis_index("dp")
    tokens_low = hidden_in[0]
    tokens = tokens_low.astype(full)
    cot_low = cotangent[0]
    cot_full = cotangent[0].astype(full)
    tok_count = tokens.shape[0]
    group_len = tok_count * ctx_count
    shard = w_query.shape[0]
    experts_total = ctx_count * exp_gate.shape[0]
    capacity = 5 * tok_count * TOP_K // (4 * experts_total)
    repeat = max(1, ctx_count // HEADS)
    heads = max(1, HEADS // ctx_count)
    width = heads * HEAD_DIM
    head_sets = HEADS // heads

    def by_heads(weight):
        parts = weight.reshape(shard, head_sets, width).transpose(1, 0, 2)
        return jnp.repeat(parts, repeat, axis=0) if repeat > 1 else parts

    small = jnp.concatenate(
        [
            jnp.stack([in_gain, b_query, b_key, b_value, ffn_gain, sh_mix], axis=1),
            w_router,
        ],
        axis=1,
    )
    small_count = small.shape[1]
    small = jnp.pad(small, ((0, 0), (0, -small_count % HEAD_DIM)))
    qkv_parts = swap_ctx(
        jnp.concatenate(
            [
                by_heads(w_query),
                by_heads(w_key),
                by_heads(w_value),
                jnp.broadcast_to(small[None], (ctx_count, *small.shape)),
            ],
            axis=2,
        )
    )
    w_qkv = lax.all_gather(
        qkv_parts.reshape(ctx_count * shard, qkv_parts.shape[2]), "dp", axis=0, tiled=True
    )
    small_all = w_qkv[:, 3 * width : 3 * width + small_count].astype(full).T
    gain_one, gain_two, mix_row = small_all[0:1], small_all[4:5], small_all[5:6]
    mix_router = small_all[5:].astype(low)
    partners = jnp.arange(ctx_count, dtype=jnp.int32) ^ ctx_index
    origin = (dp_index - jnp.arange(dp_count, dtype=jnp.int32)) % dp_count
    out_around = jnp.stack(
        [w_out]
        + [
            lax.ppermute(w_out, "dp", [(i, (i + k) % dp_count) for i in range(dp_count)])
            for k in range(1, dp_count)
        ]
    )
    x_blocks, cot_all = gather_now([tokens_low, cot_low], None, 0, 145)
    cot_all = cot_all.reshape(group_len, D)
    out_mine = jnp.concatenate(
        [lax.dynamic_index_in_dim(out_around, origin[p], 0, False) for p in range(dp_count)], axis=0
    )
    (out_mine,), x_blocks = pin([out_mine], x_blocks)
    out_steps = gather_steps(out_mine)
    out_came = next(out_steps)
    shared_gate, shared_up, shared_down = (
        lax.all_gather(sh_gate.T, "dp", axis=0, tiled=True),
        lax.all_gather(sh_up.T, "dp", axis=0, tiled=True),
        lax.all_gather(sh_down, "dp", axis=0, tiled=True),
    )
    expert_gate, expert_up, expert_down = (
        lax.all_gather(exp_gate[0], "dp", axis=0, tiled=True),
        lax.all_gather(exp_up[0], "dp", axis=0, tiled=True),
        lax.all_gather(exp_down[0], "dp", axis=1, tiled=True),
    )

    route_ids = routes[0]
    flat_ids = route_ids.reshape(-1)
    order = priority[0, 0]
    earlier = (flat_ids[:, None] == flat_ids[None, :]) & (order[None, :] < order[:, None])
    ranks = jnp.sum(earlier.astype(jnp.int32), axis=1).reshape(route_ids.shape)
    expert_grid = jnp.arange(experts_total, dtype=jnp.int32)
    route_hits = route_ids[None, :, :] == expert_grid[:, None, None]
    code = jnp.sum(jnp.where(route_hits, ranks[None] + 1, 0), axis=2) - 1

    stored_to_place = blocks[0]
    block_count = stored_to_place.shape[0]
    block_grid = jnp.arange(block_count, dtype=jnp.int32)
    place_to_stored = jnp.sum(
        jnp.where(stored_to_place[None, :] == block_grid[:, None], block_grid[None, :], 0), axis=1
    )
    per_device = block_count // ctx_count
    near = partners * per_device
    stored_near = jnp.concatenate(
        [
            lax.dynamic_slice_in_dim(stored_to_place, near[m], per_device)
            for m in range(ctx_count)
        ]
    )
    place_to_near = (place_to_stored // per_device ^ ctx_index) * per_device + (
        place_to_stored % per_device
    )
    cosine_wide, sine_wide = rope_tables(group_len)
    my_heads = (ctx_index // repeat) * width
    scale_one = rms_scale(tokens)
    bias = lax.dynamic_slice_in_dim(small_all[1:4], my_heads, width, 1).reshape(1, 3 * width)
    normed_sorted, query, key, value = project(
        x_blocks, stored_near, gain_one, w_qkv, bias, cosine_wide, sine_wide
    )
    tiles = group_len // CONT
    direct = block_count == tiles
    at = place_to_stored if direct else jnp.arange(tiles, dtype=jnp.int32)
    out_came, query = pin(out_came, query)
    out_came, out_parts = advance(out_steps, out_came)
    attended_heads, lses, parts = [], [], []
    value_t = value.T
    for head in range(heads):
        one_head, lse = attention_forward(query, key, value_t, at, head)
        if head == 0:
            (*out_came, query), one_head = pin([*out_came, query], one_head)
            out_came, out_parts = advance(out_steps, out_came)
        if head == 1:
            (parts[0],), one_head = pin([parts[0]], one_head)
        attended_heads.append(one_head)
        lses.append(lse)
        stored_head = one_head if direct else take_blocks(one_head, stored_to_place)
        parts.append(swap_ctx(stored_head.reshape(ctx_count, tok_count, HEAD_DIM))[::repeat])
    if out_parts is None:
        out_came, parts[-1] = pin(out_came, parts[-1]) if heads == 1 else (out_came, parts[-1])
        out_parts = finish(out_steps, out_came)
    out_parts = out_parts.reshape(ctx_count, dp_count, shard, D)
    out_full = (
        jnp.stack(
            [lax.dynamic_index_in_dim(out_parts, partners[i], 0, False) for i in range(ctx_count)],
            axis=1,
        )
    ).reshape(D, D)
    attended_parts = jnp.stack(parts, axis=2).reshape(head_sets, tok_count, width)
    attended = attended_parts.transpose(1, 0, 2).reshape(tok_count, D)
    first_sum = tokens + dot(attended, out_full)
    scale_two = rms_scale(first_sum)
    normed_two = (first_sum * scale_two * gain_two).astype(low)
    logits = dot_nt(normed_two, mix_router)
    mix_mine = jax.nn.sigmoid(logits[:, 0:1])
    chosen = code.T >= 0
    masked = jnp.where(chosen, logits[:, 1:], masked_score)
    raised = jnp.where(chosen, jnp.exp(masked - jnp.max(masked, axis=1, keepdims=True)), 0.0)
    gates_mine = raised / jnp.sum(raised, axis=1, keepdims=True)
    narrow = jnp.concatenate([mix_mine.T, gates_mine.T, code.astype(full)], axis=0)
    narrow = jnp.pad(narrow, ((0, -narrow.shape[0] % 8), (0, 0)))
    all_normed, narrow_all = gather_now([normed_two], narrow, 1, 75)
    all_normed = all_normed.reshape(group_len, D)
    mix_all = narrow_all[:, 0].reshape(group_len, 1)
    gate_mine = lax.dynamic_index_in_dim(narrow_all, ctx_index + 1, 1, keepdims=False)
    code_mine = lax.dynamic_index_in_dim(
        narrow_all, ctx_index + 1 + experts_total, 1, keepdims=False
    ).astype(jnp.int32)
    code_mine = jnp.where(code_mine < capacity, code_mine, -1)
    slot_rows = -(-capacity // 32) * 32
    expert_rows, slot_grads, hidden_low, gate_grad, up_grad, gate_share, dx_routed, out_routed = (
        routed_expert(
            all_normed, cot_all, code_mine, gate_mine, expert_gate, expert_up, expert_down, slot_rows
        )
    )
    grad_egate = ein("crd,crf->df", expert_rows, gate_grad).astype(low)
    grad_eup = ein("crd,crf->df", expert_rows, up_grad).astype(low)
    dx_routed, grad_egate, grad_eup = lax.optimization_barrier((dx_routed, grad_egate, grad_eup))
    sum_egate, sum_eup = over_dp(grad_egate, 0), over_dp(grad_eup, 0)
    mix_cot, shared_low, shared_dg, shared_du, mix_share, dx_odd, dx_even, out_odd, out_even = (
        shared_expert(
            all_normed, cot_all, mix_all, shared_gate, shared_up, shared_down,
            dx_routed, out_routed, tok_count,
        )
    )
    dx_steps = scatter_steps(dx_odd, dx_even)
    came = next(dx_steps)
    grad_edown = ein("crf,crd->fd", hidden_low, slot_grads).astype(low)
    came, grad_edown, sum_egate, shared_low, shared_dg, shared_du = pin(
        came, grad_edown, sum_egate, shared_low, shared_dg, shared_du
    )
    sum_edown = over_dp(grad_edown, 1)
    came, dx_mine = advance(dx_steps, came)
    grad_sdown = ein("tf,td->fd", shared_low, mix_cot).astype(low)
    grad_sgate = ein("tf,td->fd", shared_dg, all_normed).astype(low)
    came, grad_sdown, grad_sgate, shared_du = pin(came, grad_sdown, grad_sgate, shared_du)
    sum_sdown, sum_sgate = over_dp(grad_sdown, 0), over_dp(grad_sgate, 0)
    came, dx_mine = advance(dx_steps, came)
    grad_sup = ein("tf,td->fd", shared_du, all_normed).astype(low)
    came, grad_sup = pin(came, grad_sup)
    sum_sup = over_dp(grad_sup, 0)
    dx_mine = finish(dx_steps, came).astype(full)

    shares = jnp.stack([gate_share[:, 0], mix_share.reshape(ctx_count, tok_count)], axis=1)
    shares = swap_ctx(jnp.take(shares, partners, axis=0))
    gate_shares = shares[:, 0].T
    mix_grad = jnp.sum(shares[:, 1], axis=0)[:, None] * (1.0 - mix_mine)
    logit_grad = gate_shares - gates_mine * jnp.sum(gate_shares, axis=1, keepdims=True)
    narrow_low = logit_grad.astype(low)
    grad_narrow = jnp.concatenate(
        [
            jnp.sum(mix_grad * normed_two.astype(full), axis=0, keepdims=True),
            ein("te,td->ed", narrow_low, normed_two),
        ],
        axis=0,
    )
    (out_odd,), dx_mine = pin([out_odd], dx_mine)
    add_steps = scatter_steps(out_odd, out_even)
    came = next(add_steps)
    normed_grad = dx_mine + mix_grad * mix_row + dot(narrow_low, mix_router[1:])
    norm_grad_two, grad_gain_two = norm_back(first_sum, scale_two, gain_two, normed_grad)
    first_grad = cot_full + norm_grad_two
    first_low = first_grad.astype(low)
    attended_grad = dot_nt(first_low, out_full).astype(low)
    grad_out = ein("td,te->de", attended, first_low).astype(low)

    upstream_parts = attended_grad.reshape(tok_count, head_sets, heads, HEAD_DIM)
    upstream_parts = [upstream_parts[:, :, head].transpose(1, 0, 2) for head in range(heads)]
    if repeat > 1:
        upstream_parts = [jnp.repeat(part, repeat, axis=0) for part in upstream_parts]
    came, upstream_parts[0], sum_eup = pin(came, upstream_parts[0], sum_eup)
    came, added = advance(add_steps, came)
    upstreams = [swap_ctx(part).reshape(group_len, HEAD_DIM) for part in upstream_parts]
    (grad_out,), upstreams[0] = pin([grad_out], upstreams[0])
    grad_out = grad_out.reshape(dp_count, ctx_count, shard, D)

    def out_rows_of(first):
        return jnp.concatenate(
            [
                lax.dynamic_index_in_dim(grad_out, partners[m], 1, False).reshape(-1, D)
                for m in range(first, ctx_count, 2)
            ],
            axis=0,
        )

    wout_steps = scatter_steps(out_rows_of(1), out_rows_of(0))
    wout_came = next(wout_steps)
    key_t = key.T
    head_grads = []
    for head in range(heads):
        upstream = upstreams[head] if direct else take_blocks(upstreams[head], place_to_stored)
        grads = attention_backward(
            query, upstream, attended_heads[head], lses[head], key, key_t, value,
            cosine_wide, sine_wide, at, head,
        )
        grads = list(grads)
        if head == 0:
            (*wout_came, upstreams[-1]), grads[0] = pin([*wout_came, upstreams[-1]], grads[0])
            wout_came, wout = advance(wout_steps, wout_came)
        head_grads.append(grads)
    came, last, sum_edown = pin(came, head_grads[-1][0], sum_edown)
    if wout is None:
        wout_came, last = pin(wout_came, last)
        wout_came, wout = advance(wout_steps, wout_came)
    head_grads[-1][0] = last
    came, added = advance(add_steps, came)
    qkv_grads = jnp.concatenate(
        [head_grads[head][kind] for kind in range(3) for head in range(heads)], axis=1
    )
    if repeat > 1:
        qkv_grads = jnp.where(ctx_index % repeat == 0, qkv_grads, jnp.zeros_like(qkv_grads))
    grad_qkv = ein("td,te->de", normed_sorted, qkv_grads).astype(low)
    bias_sums = jnp.sum(qkv_grads.astype(full), axis=0).reshape(3, width)
    grad_bias = lax.dynamic_update_slice_in_dim(
        jnp.zeros((3, D), full), bias_sums, my_heads, 1
    )
    grad_qkv, qkv_grads = lax.optimization_barrier((grad_qkv, qkv_grads))
    odd_one, even_one, gain_sums = unproject(
        qkv_grads, stored_near, w_qkv, normed_sorted, per_device
    )
    grad_gain_one = gain_sums[0] / gain_one[0]
    came, odd_one = pin(came, odd_one)
    added = finish(add_steps, came)
    layer_out = first_sum + added.astype(full)
    wout_came, odd_one = pin(wout_came, odd_one)
    wout = finish(wout_steps, wout_came)
    (wout,), odd_one, sum_sdown = pin([wout], odd_one, sum_sdown)
    qkv_rows = lax.psum_scatter(
        grad_qkv.reshape(dp_count, ctx_count, shard, 3 * width),
        "dp",
        scatter_dimension=0,
        tiled=True,
    )[0]
    wout_rows = lax.psum_scatter(
        wout.reshape(dp_count, shard, D), "dp", scatter_dimension=0, tiled=True
    )[0]
    dx_one = scatter_now(odd_one, even_one, 2)
    (sum_sgate, sum_sup, qkv_rows, wout_rows), dx_one = pin(
        [sum_sgate, sum_sup, qkv_rows, wout_rows], dx_one
    )
    norm_grad_one, _ = norm_back(tokens, scale_one, gain_one, dx_one)
    input_grad = first_grad + norm_grad_one

    qkv_mine = swap_ctx(qkv_rows)[::repeat].astype(full)
    qkv_mine = qkv_mine.reshape(head_sets, shard, 3, width).transpose(2, 1, 0, 3).reshape(3, shard, D)
    grad_wout = wout_rows.astype(full)
    small_grads = jnp.concatenate(
        [grad_gain_one[None], grad_bias, grad_gain_two[None], grad_narrow], axis=0
    )
    small_grads = small_grads.reshape(-1, dp_count, ctx_count, shard).transpose(2, 1, 0, 3)
    small_grads = jnp.sum(swap_ctx(small_grads), axis=0)
    small_grads = jnp.sum(
        lax.all_to_all(small_grads, "dp", split_axis=0, concat_axis=0, tiled=True), axis=0
    ).T

    return (
        layer_out.astype(low)[None],
        input_grad[None],
        small_grads[:, 0],
        qkv_mine[0],
        small_grads[:, 1],
        qkv_mine[1],
        small_grads[:, 2],
        qkv_mine[2],
        small_grads[:, 3],
        grad_wout,
        small_grads[:, 4],
        small_grads[:, 6:],
        sum_egate.astype(full)[None],
        sum_eup.astype(full)[None],
        sum_edown.astype(full)[None],
        sum_sgate.astype(full).T,
        sum_sup.astype(full).T,
        sum_sdown.astype(full),
        small_grads[:, 5],
    )


def solution(mesh):
    rows = P("dp", "ctx", None)
    flat = P(("dp", "ctx"))
    lines = P(("dp", "ctx"), None)
    columns = P(None, ("dp", "ctx"))
    deep = P("ctx", "dp", None)
    down = P("ctx", None, "dp")
    in_specs = (
        (rows, flat, lines, flat, lines, flat, lines, flat, lines, flat, lines)
        + (deep, deep, down, columns, columns, lines, flat)
        + (rows, rows, P("dp", None), rows)
    )
    out_specs = (
        (rows, rows, flat, lines, flat, lines, flat, lines, flat, lines, flat, lines)
        + (deep, deep, down, columns, columns, lines, flat)
    )
    return jax.shard_map(
        on_device, mesh=mesh, in_specs=in_specs, out_specs=out_specs, check_vma=False
    )
```

```python
import functools

import jax
import jax.numpy as jnp
import numpy as np
from jax import lax
from jax.experimental import pallas as pl
from jax.experimental.pallas import tpu as pltpu
from jax.sharding import PartitionSpec as P

D = 2048
HEADS = 16
HEAD_DIM = 128
TOP_K = 4
CONT = 256
PROMPT = 2048

rope_base = 1000000.0
epsilon = 1e-06
masked_score = -1e30
log2_e = 1.4426950408889634
low = jnp.bfloat16
full = jnp.float32


def dot(left, right):
    return jnp.dot(left, right, preferred_element_type=full)


def dot_nt(left, right):
    return lax.dot_general(left, right, (((1,), (1,)), ((), ())), preferred_element_type=full)


def ein(spec, left, right):
    return jnp.einsum(spec, left, right, preferred_element_type=full)


def rotate(values, cosine, sine):
    middle = values.shape[-1] // 2
    leading = values[..., :middle]
    trailing = values[..., middle:]
    return jnp.concatenate(
        [leading * cosine - trailing * sine, trailing * cosine + leading * sine], axis=-1
    )


def rope_tables(rows):
    places = np.arange(rows)
    turned = np.where(places < PROMPT, places, PROMPT + (places - PROMPT) % CONT)
    frequency = rope_base ** (-2.0 * np.arange(HEAD_DIM // 2, dtype=np.float64) / HEAD_DIM)
    angles = turned.astype(np.float64)[:, None] * frequency[None, :]
    cosine, sine = np.cos(angles), np.sin(angles)
    wide = np.concatenate([cosine, cosine], axis=1), np.concatenate([-sine, sine], axis=1)
    return tuple(jnp.asarray(table.astype(np.float32)) for table in wide)


def rms_scale(values):
    return lax.rsqrt(jnp.mean(values * values, axis=-1, keepdims=True) + epsilon)


def norm_back(values, scale_rows, gain_row, upstream):
    weighted = upstream * gain_row
    grad_gain = jnp.sum(upstream * values * scale_rows, axis=0)
    grad_values = scale_rows * weighted - values * scale_rows**3 * jnp.mean(
        weighted * values, axis=-1, keepdims=True
    )
    return (grad_values, grad_gain)


def silu_parts(values):
    sig_value = jax.nn.sigmoid(values)
    return (values * sig_value, sig_value * (1.0 + values * (1.0 - sig_value)))


def cost(microseconds):
    return pl.CostEstimate(
        flops=int(microseconds * 1.1e9),
        bytes_accessed=int(microseconds * 3.3e6),
        transcendentals=0,
    )


WIDE = 4


def attend_tiles(index, chunk, carry):
    whole = jnp.minimum(index, PROMPT // CONT)
    wide = whole // WIDE
    carry = lax.fori_loop(
        0, wide, lambda step, c: chunk(step * (WIDE * CONT), WIDE * CONT, False, c), carry
    )
    carry = lax.fori_loop(
        wide * WIDE, whole, lambda step, c: chunk(step * CONT, CONT, False, c), carry
    )
    return chunk(index * CONT, CONT, True, carry)


def turn(values, cosine, sine):
    half = HEAD_DIM // 2
    swapped = jnp.concatenate([values[:, half:], values[:, :half]], axis=1)
    return values * cosine + swapped * sine


def project_kernel(
    place_ref, x_ref, gain_ref, w_ref, bias_ref, cos_ref, sin_ref, normed_ref, q_ref, k_ref, v_ref
):
    values = x_ref[0].astype(full)
    scale = lax.rsqrt(jnp.mean(values * values, axis=1, keepdims=True) + epsilon)
    normed = (values * scale * gain_ref[...]).astype(low)
    normed_ref[...] = normed
    width = q_ref.shape[1]
    projected = dot(normed, w_ref[...]) + bias_ref[...]
    cosine, sine = cos_ref[...], sin_ref[...]
    for start in range(0, width, HEAD_DIM):
        for kind, out in ((0, q_ref), (1, k_ref)):
            column = kind * width + start
            head = projected[:, column : column + HEAD_DIM]
            out[:, start : start + HEAD_DIM] = turn(head, cosine, sine).astype(low)
    v_ref[...] = projected[:, 2 * width :].astype(low)


def project(x_blocks, places, gain, weight, bias, cosine, sine):
    count, rows, _ = x_blocks.shape
    width = bias.shape[1] // 3
    at_place = lambda g, place: (place[g], 0)
    whole = lambda g, place: (0, 0)
    tile = pl.BlockSpec((rows, width), at_place)
    head = jax.ShapeDtypeStruct((count * rows, width), low)
    return pl.pallas_call(
        project_kernel,
        grid_spec=pltpu.PrefetchScalarGridSpec(
            num_scalar_prefetch=1,
            grid=(count,),
            in_specs=[
                pl.BlockSpec((1, rows, D), lambda g, place: (g, 0, 0)),
                pl.BlockSpec((1, D), whole),
                pl.BlockSpec((D, 3 * width), whole),
                pl.BlockSpec((1, 3 * width), whole),
                pl.BlockSpec((rows, HEAD_DIM), at_place),
                pl.BlockSpec((rows, HEAD_DIM), at_place),
            ],
            out_specs=[pl.BlockSpec((rows, D), at_place), tile, tile, tile],
        ),
        out_shape=[jax.ShapeDtypeStruct((count * rows, D), low), head, head, head],
        compiler_params=pltpu.CompilerParams(vmem_limit_bytes=40 * 2**20),
        cost_estimate=cost(24),
        name="project",
    )(places, x_blocks, gain, weight, bias, cosine, sine)


def unproject_kernel(place_ref, grad_ref, w_ref, normed_ref, odd_ref, even_ref, gain_ref):
    step = pl.program_id(0)
    middle = pl.num_programs(0) // 2
    total = dot_nt(grad_ref[...], w_ref[...])
    gain_part = jnp.sum(total * normed_ref[...].astype(full), axis=0, keepdims=True)

    @pl.when(step == 0)
    def _():
        gain_ref[...] = jnp.zeros_like(gain_ref)

    gain_ref[...] += gain_part

    @pl.when(step < middle)
    def _():
        odd_ref[...] = total.astype(low)

    @pl.when(step >= middle)
    def _():
        even_ref[...] = total.astype(low)


def unproject(grads, places, weight, normed, per_device):
    count = places.shape[0]
    rows = grads.shape[0] // count
    width = grads.shape[1]
    middle = count // 2

    def at_place(g, place):
        block = odd_first(g // per_device, count // per_device) * per_device + g % per_device
        return (place[block], 0)

    shape = jax.ShapeDtypeStruct((middle * rows, D), low)
    return pl.pallas_call(
        unproject_kernel,
        grid_spec=pltpu.PrefetchScalarGridSpec(
            num_scalar_prefetch=1,
            grid=(count,),
            in_specs=[
                pl.BlockSpec((rows, width), at_place),
                pl.BlockSpec((D, width), lambda g, place: (0, 0)),
                pl.BlockSpec((rows, D), at_place),
            ],
            out_specs=[
                pl.BlockSpec((rows, D), lambda g, place: (jnp.minimum(g, middle - 1), 0)),
                pl.BlockSpec((rows, D), lambda g, place: (jnp.maximum(g - middle, 0), 0)),
                pl.BlockSpec((1, D), lambda g, place: (0, 0)),
            ],
        ),
        out_shape=[shape, shape, jax.ShapeDtypeStruct((1, D), full)],
        compiler_params=pltpu.CompilerParams(vmem_limit_bytes=40 * 2**20),
        cost_estimate=cost(20),
        name="unproject",
    )(places, grads, weight, normed)


def dot_tn(left, right):
    return lax.dot_general(left, right, (((0,), (0,)), ((), ())), preferred_element_type=full)


def expert_kernel(
    normed_ref, cot_ref, code_ref, gate_ref, wg_ref, wu_ref, wd_ref,
    rows_ref, sg_ref, act_ref, dg_ref, du_ref, share_ref, dx_ref, out_ref,
):
    slots = rows_ref.shape[1]
    tok = normed_ref.shape[0]
    hits = code_ref[0] == lax.broadcasted_iota(jnp.int32, (slots, tok), 0)
    table_full = jnp.where(hits, 1.0, 0.0)
    gated = jnp.where(hits, gate_ref[0], 0.0)
    table = table_full.astype(low)
    rows = dot(table, normed_ref[...]).astype(low)
    rows_ref[0] = rows
    slot_gate = jnp.sum(gated, axis=1, keepdims=True)
    slot_grad = (dot(table, cot_ref[...]) * slot_gate).astype(low)
    sg_ref[0] = slot_grad
    gate = dot(rows, wg_ref[...])
    up = dot(rows, wu_ref[...])
    hidden = dot_nt(slot_grad, wd_ref[...])
    silu, slope = silu_parts(gate)
    act_full = silu * up
    act = act_full.astype(low)
    act_ref[0] = act
    dg = (hidden * up * slope).astype(low)
    du = (hidden * silu).astype(low)
    dg_ref[0] = dg
    du_ref[0] = du
    slot_share = jnp.sum(hidden * act_full, axis=1, keepdims=True)
    share_ref[0] = jnp.sum(table_full * slot_share, axis=0, keepdims=True)
    slot_dx = (dot_nt(dg, wg_ref[...]) + dot_nt(du, wu_ref[...])).astype(low)
    dx_ref[...] = dot_tn(table, slot_dx).astype(low)
    expert_y = dot(act, wd_ref[...]).astype(low)
    out_ref[...] = dot_tn(gated.astype(low), expert_y).astype(low)


def routed_expert(all_normed, cot_all, code, gate, w_gate, w_up, w_down, slots):
    count, tok = code.shape
    ff = w_gate.shape[1]
    chunk = pl.BlockSpec((tok, D), lambda m: (m, 0))
    line = pl.BlockSpec((1, 1, tok), lambda m: (m, 0, 0))

    def fixed(array):
        return pl.BlockSpec(array.shape, lambda m: (0, 0), pipeline_mode=pl.Buffered(1))

    def per_slot(last):
        return pl.BlockSpec((1, slots, last), lambda m: (m, 0, 0))

    def shape(*dims, dtype=low):
        return jax.ShapeDtypeStruct(dims, dtype)

    return pl.pallas_call(
        expert_kernel,
        grid=(count,),
        in_specs=[chunk, chunk, line, line, fixed(w_gate), fixed(w_up), fixed(w_down)],
        out_specs=[per_slot(D), per_slot(D), per_slot(ff), per_slot(ff), per_slot(ff), line, chunk, chunk],
        out_shape=[
            shape(count, slots, D),
            shape(count, slots, D),
            shape(count, slots, ff),
            shape(count, slots, ff),
            shape(count, slots, ff),
            shape(count, 1, tok, dtype=full),
            shape(count * tok, D),
            shape(count * tok, D),
        ],
        compiler_params=pltpu.CompilerParams(vmem_limit_bytes=60 * 2**20),
        cost_estimate=cost(140),
        name="routed_expert",
    )(all_normed, cot_all, code[:, None, :], gate[:, None, :], w_gate, w_up, w_down)


def shared_kernel(
    normed_ref, cot_ref, mix_ref, wg_ref, wu_ref, wd_ref, dxe_ref, oute_ref,
    mixcot_ref, act_ref, dg_ref, du_ref, share_ref, dx_odd, dx_even, out_odd, out_even,
):
    step = pl.program_id(0)
    middle = pl.num_programs(0) // 2
    normed = normed_ref[...]
    mix = mix_ref[...]
    mix_cot = (mix * cot_ref[...].astype(full)).astype(low)
    mixcot_ref[...] = mix_cot
    gate = dot_nt(normed, wg_ref[...])
    up = dot_nt(normed, wu_ref[...])
    hidden = dot_nt(mix_cot, wd_ref[...])
    silu, slope = silu_parts(gate)
    act_full = silu * up
    act = act_full.astype(low)
    act_ref[...] = act
    dg = (hidden * up * slope).astype(low)
    du = (hidden * silu).astype(low)
    dg_ref[...] = dg
    du_ref[...] = du
    share_ref[...] = jnp.sum(hidden * act_full, axis=1, keepdims=True)
    dx = dot(dg, wg_ref[...]) + dot(du, wu_ref[...]) + dxe_ref[...].astype(full)
    out = mix * dot(act, wd_ref[...]) + oute_ref[...].astype(full)

    @pl.when(step < middle)
    def _():
        dx_odd[...] = dx.astype(low)
        out_odd[...] = out.astype(low)

    @pl.when(step >= middle)
    def _():
        dx_even[...] = dx.astype(low)
        out_even[...] = out.astype(low)


def shared_expert(all_normed, cot_all, mix, w_gate_t, w_up_t, w_down, dx_routed, out_routed, tok):
    rows = all_normed.shape[0]
    ff = w_down.shape[0]
    count = rows // tok
    middle = count // 2
    chunk = pl.BlockSpec((tok, D), lambda g: (odd_first(g, count), 0))
    narrow = pl.BlockSpec((tok, ff), lambda g: (odd_first(g, count), 0))
    column = pl.BlockSpec((tok, 1), lambda g: (odd_first(g, count), 0))
    odd = pl.BlockSpec((tok, D), lambda g: (jnp.minimum(g, middle - 1), 0))
    even = pl.BlockSpec((tok, D), lambda g: (jnp.maximum(g - middle, 0), 0))
    fixed = pl.BlockSpec((ff, D), lambda g: (0, 0), pipeline_mode=pl.Buffered(1))
    narrow_shape = jax.ShapeDtypeStruct((rows, ff), low)
    half_shape = jax.ShapeDtypeStruct((rows // 2, D), low)
    return pl.pallas_call(
        shared_kernel,
        grid=(count,),
        in_specs=[chunk, chunk, column, fixed, fixed, fixed, chunk, chunk],
        out_specs=[chunk, narrow, narrow, narrow, column, odd, even, odd, even],
        out_shape=[
            jax.ShapeDtypeStruct((rows, D), low),
            narrow_shape,
            narrow_shape,
            narrow_shape,
            jax.ShapeDtypeStruct((rows, 1), full),
            half_shape,
            half_shape,
            half_shape,
            half_shape,
        ],
        compiler_params=pltpu.CompilerParams(vmem_limit_bytes=60 * 2**20),
        cost_estimate=cost(103),
        name="shared_expert",
    )(all_normed, cot_all, mix, w_gate_t, w_up_t, w_down, dx_routed, out_routed)


def forward_kernel(at_ref, q_ref, k_ref, vt_ref, o_ref, lse_ref):
    index = pl.program_id(0)
    query = q_ref[...]
    score_scale = HEAD_DIM ** (-0.5) * log2_e

    def chunk(start, size, diagonal, carry):
        highest, total, acc = carry
        start = pl.multiple_of(start, CONT)
        scores = dot_nt(k_ref[pl.ds(start, size), :], query) * score_scale
        if diagonal:
            keys = lax.broadcasted_iota(jnp.int32, scores.shape, 0)
            queries = lax.broadcasted_iota(jnp.int32, scores.shape, 1)
            scores = jnp.where(keys <= queries, scores, masked_score)
        newest = jnp.maximum(highest, jnp.max(scores, axis=0, keepdims=True))
        weights = jnp.exp2(scores - newest)
        shrink = jnp.exp2(highest - newest)
        total = total * shrink + jnp.sum(weights, axis=0, keepdims=True)
        acc = acc * shrink + dot(vt_ref[:, pl.ds(start, size)], weights.astype(low))
        return (newest, total, acc)

    highest, total, acc = attend_tiles(
        index,
        chunk,
        (
            jnp.full((1, CONT), masked_score, full),
            jnp.zeros((1, CONT), full),
            jnp.zeros((HEAD_DIM, CONT), full),
        ),
    )
    o_ref[...] = (acc / total).T.astype(low)
    lse_ref[...] = highest + jnp.log2(total)


def attention_forward(query, key, value_t, at, head):
    rows = query.shape[0]
    return pl.pallas_call(
        forward_kernel,
        grid_spec=pltpu.PrefetchScalarGridSpec(
            num_scalar_prefetch=1,
            grid=(rows // CONT,),
            in_specs=[
                pl.BlockSpec((CONT, HEAD_DIM), lambda i, at: (i, head)),
                pl.BlockSpec((rows, HEAD_DIM), lambda i, at: (0, head)),
                pl.BlockSpec((HEAD_DIM, rows), lambda i, at: (head, 0)),
            ],
            out_specs=[
                pl.BlockSpec((CONT, HEAD_DIM), lambda i, at: (at[i], 0)),
                pl.BlockSpec((1, CONT), lambda i, at: (0, i)),
            ],
        ),
        out_shape=[
            jax.ShapeDtypeStruct((rows, HEAD_DIM), low),
            jax.ShapeDtypeStruct((1, rows), full),
        ],
        compiler_params=pltpu.CompilerParams(vmem_limit_bytes=32 * 2**20),
        cost_estimate=cost(30),
        name="attend_forward",
    )(at, query, key, value_t)


def backward_kernel(
    at_ref, q_ref, do_ref, o_ref, lse_ref, k_ref, kt_ref, v_ref, cos_ref, sin_ref,
    dq_ref, dk_ref, dv_ref, dk_sum, dv_sum,
):
    index = pl.program_id(0)
    query = q_ref[...]
    upstream = do_ref[...]
    lse = lse_ref[...]
    product = upstream.astype(full) * o_ref[...].astype(full)
    delta = jnp.sum(product.T, axis=0, keepdims=True)
    scale = HEAD_DIM ** (-0.5)
    span_now = pl.ds(pl.multiple_of(index * CONT, CONT), CONT)

    @pl.when(index == 0)
    def _():
        dk_sum[...] = jnp.zeros_like(dk_sum)
        dv_sum[...] = jnp.zeros_like(dv_sum)

    def chunk(start, size, diagonal, acc):
        start = pl.multiple_of(start, CONT)
        span = pl.ds(start, size)
        scores = dot_nt(k_ref[span, :], query) * (scale * log2_e) - lse
        if diagonal:
            keys = lax.broadcasted_iota(jnp.int32, scores.shape, 0)
            queries = lax.broadcasted_iota(jnp.int32, scores.shape, 1)
            scores = jnp.where(keys <= queries, scores, masked_score)
        probs = jnp.exp2(scores)
        prob_grad = dot_nt(v_ref[span, :], upstream)
        score_grad = (probs * (prob_grad - delta)).astype(low)
        dv_sum[span, :] += dot(probs.astype(low), upstream)
        dk_sum[span, :] += dot(score_grad, query)
        return acc + dot(kt_ref[:, span], score_grad)

    acc = attend_tiles(index, chunk, jnp.zeros((HEAD_DIM, CONT), full))
    dq_ref[...] = turn(acc.T * scale, cos_ref[span_now, :], -sin_ref[span_now, :]).astype(low)

    @pl.when(index == pl.num_programs(0) - 1)
    def _():
        def finish(step, carry):
            span = pl.ds(pl.multiple_of(step * CONT, CONT), CONT)
            dk_ref[span, :] = turn(
                dk_sum[span, :] * scale, cos_ref[span, :], -sin_ref[span, :]
            ).astype(low)
            dv_ref[span, :] = dv_sum[span, :].astype(low)
            return carry

        lax.fori_loop(0, pl.num_programs(0), finish, 0)


def attention_backward(query, upstream, attended, lse, key, key_t, value, cosine, sine, at, head):
    rows = query.shape[0]
    tile = pl.BlockSpec((CONT, HEAD_DIM), lambda i, at: (i, head))
    stored = pl.BlockSpec((CONT, HEAD_DIM), lambda i, at: (at[i], 0))
    whole = pl.BlockSpec((rows, HEAD_DIM), lambda i, at: (0, head))
    table = pl.BlockSpec((rows, HEAD_DIM), lambda i, at: (0, 0))
    grad = jax.ShapeDtypeStruct((rows, HEAD_DIM), low)
    return pl.pallas_call(
        backward_kernel,
        grid_spec=pltpu.PrefetchScalarGridSpec(
            num_scalar_prefetch=1,
            grid=(rows // CONT,),
            in_specs=[
                tile,
                stored,
                stored,
                pl.BlockSpec((1, CONT), lambda i, at: (0, i)),
                whole,
                pl.BlockSpec((HEAD_DIM, rows), lambda i, at: (head, 0)),
                whole,
                table,
                table,
            ],
            out_specs=[pl.BlockSpec((CONT, HEAD_DIM), lambda i, at: (i, 0)), table, table],
            scratch_shapes=[
                pltpu.VMEM((rows, HEAD_DIM), full),
                pltpu.VMEM((rows, HEAD_DIM), full),
            ],
        ),
        out_shape=[grad, grad, grad],
        compiler_params=pltpu.CompilerParams(vmem_limit_bytes=48 * 2**20),
        cost_estimate=cost(38),
        name="attend_backward",
    )(at, query, upstream, attended, lse, key, key_t, value, cosine, sine)


def take_blocks(rows, order):
    count = order.shape[0]
    blocked = rows.reshape(count, rows.shape[0] // count, *rows.shape[1:])
    return jnp.concatenate(
        [lax.dynamic_index_in_dim(blocked, order[i], 0, keepdims=False) for i in range(count)], axis=0
    )


def bit_orders(count):
    bits = [1 << i for i in range(1, count.bit_length() - 1)]
    return bits, bits[::-1]


def exchange(values, bit, count):
    return lax.ppermute(values, "ctx", [(i, i ^ bit) for i in range(count)])


def gather_plan(count):
    plan = []
    orders = bit_orders(count)
    held = [[0], [0]]
    for depth in range(len(orders[0])):
        sends = [[(half, m, orders[half][depth]) for m in held[half]] for half in (0, 1)]
        plan += [send for pair in zip(*sends) for send in pair]
        for half in (0, 1):
            held[half] = held[half] + [m ^ orders[half][depth] for m in held[half]]
    return plan, [(half, m, 1) for m in held[0] for half in (0, 1)]


def gather_kernel(count, big, with_small, *refs):
    ins = refs[: big + with_small]
    outs = refs[big + with_small : 2 * (big + with_small)]
    send_sems, recv_sems, own_sems = refs[2 * (big + with_small) :]
    me = lax.axis_index("ctx")
    dp = lax.axis_index("dp")
    bits = bit_orders(count)[0] + [1]
    rows = ins[0].shape[0] // 2
    barrier = pltpu.get_barrier_semaphore()
    for bit in bits:
        pl.semaphore_signal(
            barrier, inc=1, device_id=(dp, me ^ bit), device_id_type=pl.DeviceIdType.MESH
        )
    pl.semaphore_wait(barrier, len(bits))
    own, spots = [], []
    for a in range(big):
        for half in (0, 1):
            own.append(ins[a].at[pl.ds(half * rows, rows)])
            spots.append([outs[a].at[2 * m + half] for m in range(count)])
    if with_small:
        own.append(ins[big])
        spots.append([outs[big].at[m] for m in range(count)])
    local = [
        pltpu.make_async_copy(own[t], spots[t][0], own_sems.at[t]) for t in range(len(own))
    ]
    for copy in local:
        copy.start()
    copies = {}
    waited = set()

    def send(track, m, bit):
        if m and (track, m) not in waited:
            copies[(track, m)].wait_recv()
            waited.add((track, m))
        lands = track * count + (m ^ bit)
        copy = pltpu.make_async_remote_copy(
            src_ref=spots[track][m] if m else own[track],
            dst_ref=spots[track][m ^ bit],
            send_sem=send_sems.at[lands],
            recv_sem=recv_sems.at[lands],
            device_id=(dp, me ^ bit),
            device_id_type=pl.DeviceIdType.MESH,
        )
        copy.start()
        copies[(track, m ^ bit)] = copy

    plan_far, plan_near = gather_plan(count)
    far, near = [], []
    if with_small:
        far += [(2 * big, m, bit) for half, m, bit in plan_far if half == 0]
        near += [(2 * big, m, bit) for half, m, bit in plan_near if half == 0]
    for half, m, bit in plan_far:
        far += [(2 * a + half, m, bit) for a in range(big)]
    for half, m, bit in plan_near:
        near += [(2 * a + half, m, bit) for a in range(big)]
    done = set()
    for entry in far:
        send(*entry)
        for other in near:
            if other not in done and (other[1] == 0 or (other[0], other[1]) in waited):
                done.add(other)
                send(*other)
    for other in near:
        if other not in done:
            send(*other)
    for key, copy in copies.items():
        if key not in waited:
            copy.wait_recv()
    for copy in copies.values():
        copy.wait_send()
    for copy in local:
        copy.wait()


def gather_now(arrays, small, collective_id, microseconds):
    count = lax.axis_size("ctx")
    shapes = [
        jax.ShapeDtypeStruct((2 * count, x.shape[0] // 2, x.shape[1]), x.dtype) for x in arrays
    ]
    inputs = list(arrays)
    if small is not None:
        inputs.append(small)
        shapes.append(jax.ShapeDtypeStruct((count, *small.shape), small.dtype))
    tracks = len(arrays) + len(inputs)
    return pl.pallas_call(
        functools.partial(gather_kernel, count, len(arrays), len(inputs) - len(arrays)),
        in_specs=[pl.BlockSpec(memory_space=pl.ANY)] * len(shapes),
        out_specs=[pl.BlockSpec(memory_space=pltpu.HBM)] * len(arrays)
        + [pl.BlockSpec(memory_space=pl.ANY)] * (len(inputs) - len(arrays)),
        out_shape=shapes,
        scratch_shapes=[
            pltpu.SemaphoreType.DMA((tracks * count,)),
            pltpu.SemaphoreType.DMA((tracks * count,)),
            pltpu.SemaphoreType.DMA((tracks,)),
        ],
        compiler_params=pltpu.CompilerParams(
            collective_id=collective_id, has_side_effects=True, vmem_limit_bytes=58 * 2**20
        ),
        cost_estimate=cost(microseconds),
        name="gather_rows",
    )(*inputs)


def split_rows(values, parts):
    rows = values.shape[0] // parts
    return [values[i * rows : (i + 1) * rows] for i in range(parts)]


def pin(arrays, *others):
    held = lax.optimization_barrier((tuple(arrays), *others))
    return (list(held[0]), *held[1:])


def gather_steps(values):
    count = lax.axis_size("ctx")
    orders = bit_orders(count)
    names, held = [[0], [0]], [[piece] for piece in split_rows(values, 2)]
    for depth in range(len(orders[0])):
        came = []
        for half in (0, 1):
            sent = jnp.concatenate(held[half], axis=0) if depth else held[half][0]
            came.append(exchange(sent, orders[half][depth], count))
        came = yield came
        for half in (0, 1):
            held[half] = held[half] + split_rows(came[half], len(held[half]))
            names[half] = names[half] + [m ^ orders[half][depth] for m in names[half]]
    halves = [dict(zip(names[half], held[half])) for half in (0, 1)]
    own = jnp.stack(
        [jnp.concatenate([half[m] for half in halves], axis=0) for m in range(0, count, 2)]
    )
    (other,) = yield [exchange(own, 1, count)]
    return jnp.stack([own, other], axis=1).reshape(count * values.shape[0], *values.shape[1:])


def add_low(left, right):
    return (left.astype(full) + right.astype(full)).astype(low)


def scatter_steps(odd, even):
    count = lax.axis_size("ctx")
    parts = count // 2
    (came,) = yield [exchange(odd, 1, count)]
    pairs = list(zip(split_rows(even, parts), split_rows(came, parts)))
    orders = bit_orders(count)
    held = [
        {
            2 * n: add_low(split_rows(left, 2)[half], split_rows(right, 2)[half])
            for n, (left, right) in enumerate(pairs)
        }
        for half in (0, 1)
    ]
    for depth in range(len(orders[0])):
        names, came = [], []
        for half in (0, 1):
            bit = orders[half][depth]
            names.append([m for m in held[half] if m & bit])
            sent = [held[half][m] for m in names[half]]
            sent = jnp.concatenate(sent, axis=0) if len(sent) > 1 else sent[0]
            came.append(exchange(sent, bit, count))
        came = yield came
        for half in (0, 1):
            bit = orders[half][depth]
            pieces = split_rows(came[half], len(names[half]))
            held[half] = {
                m ^ bit: add_low(held[half][m ^ bit], x) for m, x in zip(names[half], pieces)
            }
    return jnp.concatenate([half[0] for half in held], axis=0)


def scatter_kernel(count, odd_ref, even_ref, out_ref, sums, came, near_sems, far_send, far_recv):
    me = lax.axis_index("ctx")
    dp = lax.axis_index("dp")
    orders = bit_orders(count)
    bits = orders[0] + [1]
    parts = count // 2
    rows = even_ref.shape[2]
    tile = min(32, rows)
    barrier = pltpu.get_barrier_semaphore()
    for bit in bits:
        pl.semaphore_signal(
            barrier, inc=1, device_id=(dp, me ^ bit), device_id_type=pl.DeviceIdType.MESH
        )
    pl.semaphore_wait(barrier, len(bits))
    first = sorted(range(parts), key=lambda n: -bin(n).count("1"))
    near = {}
    for n in first:
        near[n] = pltpu.make_async_remote_copy(
            src_ref=odd_ref.at[n],
            dst_ref=sums.at[n],
            send_sem=near_sems.at[0, n],
            recv_sem=near_sems.at[1, n],
            device_id=(dp, me ^ 1),
            device_id_type=pl.DeviceIdType.MESH,
        )
        near[n].start()

    def add(into, left, right):
        def body(step, carry):
            span = pl.ds(pl.multiple_of(step * tile, tile), tile)
            total = left[span, :].astype(full) + right[span, :].astype(full)
            into[span, :] = total.astype(into.dtype)
            return carry

        lax.fori_loop(0, rows // tile, body, 0)

    far = []
    used = [0, 0]

    def send(half, n, bit):
        place = used[half]
        used[half] += 1
        copy = pltpu.make_async_remote_copy(
            src_ref=sums.at[n, half],
            dst_ref=came.at[half, place],
            send_sem=far_send.at[half, place],
            recv_sem=far_recv.at[half, place],
            device_id=(dp, me ^ bit),
            device_id_type=pl.DeviceIdType.MESH,
        )
        copy.start()
        far.append(copy)
        return copy, place

    pending = [{}, {}]
    for n in first:
        near[n].wait_recv()
        for half in (0, 1):
            add(sums.at[n, half], sums.at[n, half], even_ref.at[n, half])
            bit = orders[half][0]
            if 2 * n & bit:
                pending[half][n] = send(half, n, bit)
    depth_count = len(orders[0])
    for depth in range(depth_count):
        later = [{}, {}]
        waiting = [(half, n) for k in range(parts) for half in (0, 1) for n in list(pending[half])[k : k + 1]]
        for half, n in waiting:
            copy, place = pending[half][n]
            keep = n ^ (orders[half][depth] >> 1)
            copy.wait_recv()
            if depth + 1 == depth_count:
                add(out_ref.at[half], sums.at[keep, half], came.at[half, place])
            else:
                add(sums.at[keep, half], sums.at[keep, half], came.at[half, place])
                bit = orders[half][depth + 1]
                if 2 * keep & bit:
                    later[half][keep] = send(half, keep, bit)
        pending = later
    for n in first:
        near[n].wait_send()
    for copy in far:
        copy.wait_send()


def scatter_now(odd, even, collective_id):
    count = lax.axis_size("ctx")
    parts = count // 2
    rows = odd.shape[0] // parts // 2
    shape = (parts, 2, rows, odd.shape[1])
    out = pl.pallas_call(
        functools.partial(scatter_kernel, count),
        in_specs=[pl.BlockSpec(memory_space=pl.ANY), pl.BlockSpec(memory_space=pltpu.VMEM)],
        out_specs=pl.BlockSpec(memory_space=pltpu.VMEM),
        out_shape=jax.ShapeDtypeStruct((2, rows, odd.shape[1]), full),
        scratch_shapes=[
            pltpu.VMEM(shape, low),
            pltpu.VMEM((2, parts - 1, rows, odd.shape[1]), low),
            pltpu.SemaphoreType.DMA((2, parts)),
            pltpu.SemaphoreType.DMA((2, parts - 1)),
            pltpu.SemaphoreType.DMA((2, parts - 1)),
        ],
        compiler_params=pltpu.CompilerParams(
            collective_id=collective_id, has_side_effects=True, vmem_limit_bytes=40 * 2**20
        ),
        cost_estimate=cost(90),
        name="scatter_rows",
    )(odd.reshape(shape), even.reshape(shape))
    return out.reshape(2 * rows, odd.shape[1])


def advance(steps, came):
    try:
        return (steps.send(came), None)
    except StopIteration as stop:
        return (None, stop.value)


def finish(steps, came):
    value = None
    while value is None:
        came, value = advance(steps, came)
    return value


def over_dp(grad, dim):
    return lax.psum_scatter(grad, "dp", scatter_dimension=dim, tiled=True)


def odd_first(step, count):
    return lax.rem(2 * step + 1, count + 1)


def swap_ctx(values):
    return lax.all_to_all(values, "ctx", split_axis=0, concat_axis=0, tiled=True)


def on_device(
    hidden_in,
    in_gain,
    w_query,
    b_query,
    w_key,
    b_key,
    w_value,
    b_value,
    w_out,
    ffn_gain,
    w_router,
    exp_gate,
    exp_up,
    exp_down,
    sh_gate,
    sh_up,
    sh_down,
    sh_mix,
    routes,
    priority,
    blocks,
    cotangent,
):
    both = ("dp", "ctx")
    ctx_count = lax.axis_size("ctx")
    ctx_index = lax.axis_index("ctx")
    dp_count = lax.axis_size("dp")
    dp_index = lax.axis_index("dp")
    tokens_low = hidden_in[0]
    tokens = tokens_low.astype(full)
    cot_low = cotangent[0]
    cot_full = cotangent[0].astype(full)
    tok_count = tokens.shape[0]
    group_len = tok_count * ctx_count
    shard = w_query.shape[0]
    experts_total = ctx_count * exp_gate.shape[0]
    capacity = 5 * tok_count * TOP_K // (4 * experts_total)
    repeat = max(1, ctx_count // HEADS)
    heads = max(1, HEADS // ctx_count)
    width = heads * HEAD_DIM
    head_sets = HEADS // heads

    def by_heads(weight):
        parts = weight.reshape(shard, head_sets, width).transpose(1, 0, 2)
        return jnp.repeat(parts, repeat, axis=0) if repeat > 1 else parts

    small = jnp.concatenate(
        [
            jnp.stack([in_gain, b_query, b_key, b_value, ffn_gain, sh_mix], axis=1),
            w_router,
        ],
        axis=1,
    )
    small_count = small.shape[1]
    small = jnp.pad(small, ((0, 0), (0, -small_count % HEAD_DIM)))
    qkv_parts = swap_ctx(
        jnp.concatenate(
            [
                by_heads(w_query),
                by_heads(w_key),
                by_heads(w_value),
                jnp.broadcast_to(small[None], (ctx_count, *small.shape)),
            ],
            axis=2,
        )
    )
    w_qkv = lax.all_gather(
        qkv_parts.reshape(ctx_count * shard, qkv_parts.shape[2]), "dp", axis=0, tiled=True
    )
    small_all = w_qkv[:, 3 * width : 3 * width + small_count].astype(full).T
    gain_one, gain_two, mix_row = small_all[0:1], small_all[4:5], small_all[5:6]
    mix_router = small_all[5:].astype(low)
    partners = jnp.arange(ctx_count, dtype=jnp.int32) ^ ctx_index
    out_around = jnp.stack(
        [w_out]
        + [
            lax.ppermute(w_out, "dp", [(i, (i + k) % dp_count) for i in range(dp_count)])
            for k in range(1, dp_count)
        ]
    )
    x_blocks, cot_all = gather_now([tokens_low, cot_low], None, 0, 145)
    cot_all = cot_all.reshape(group_len, D)
    out_mine = jnp.concatenate(
        [lax.dynamic_index_in_dim(out_around, (dp_index + dp_count - p) % dp_count, 0, False)
            for p in range(dp_count)], axis=0
    )
    (out_mine,), x_blocks = pin([out_mine], x_blocks)
    out_steps = gather_steps(out_mine)
    out_came = next(out_steps)
    shared_gate, shared_up, shared_down = (
        lax.all_gather(sh_gate.T, "dp", axis=0, tiled=True),
        lax.all_gather(sh_up.T, "dp", axis=0, tiled=True),
        lax.all_gather(sh_down, "dp", axis=0, tiled=True),
    )
    expert_gate, expert_up, expert_down = (
        lax.all_gather(exp_gate[0], "dp", axis=0, tiled=True),
        lax.all_gather(exp_up[0], "dp", axis=0, tiled=True),
        lax.all_gather(exp_down[0], "dp", axis=1, tiled=True),
    )

    route_ids = routes[0]
    flat_ids = route_ids.reshape(-1)
    order = priority[0, 0]
    earlier = (flat_ids[:, None] == flat_ids[None, :]) & (order[None, :] < order[:, None])
    ranks = jnp.sum(earlier.astype(jnp.int32), axis=1).reshape(route_ids.shape)
    expert_grid = jnp.arange(experts_total, dtype=jnp.int32)
    route_hits = route_ids[None, :, :] == expert_grid[:, None, None]
    code = jnp.sum(jnp.where(route_hits, ranks[None] + 1, 0), axis=2) - 1

    stored_to_place = blocks[0]
    block_count = stored_to_place.shape[0]
    block_grid = jnp.arange(block_count, dtype=jnp.int32)
    place_to_stored = jnp.sum(
        jnp.where(stored_to_place[None, :] == block_grid[:, None], block_grid[None, :], 0), axis=1
    )
    per_device = block_count // ctx_count
    near = (block_grid // per_device ^ ctx_index) * per_device + block_grid % per_device
    stored_near = jnp.sum(
        jnp.where(near[:, None] == block_grid[None, :], stored_to_place[None, :], 0), axis=1
    )
    cosine_wide, sine_wide = rope_tables(group_len)
    my_heads = (ctx_index // repeat) * width
    scale_one = rms_scale(tokens)
    bias = lax.dynamic_slice_in_dim(small_all[1:4], my_heads, width, 1).reshape(1, 3 * width)
    normed_sorted, query, key, value = project(
        x_blocks, stored_near, gain_one, w_qkv, bias, cosine_wide, sine_wide
    )
    tiles = group_len // CONT
    direct = block_count == tiles
    at = place_to_stored if direct else jnp.arange(tiles, dtype=jnp.int32)
    out_came, query = pin(out_came, query)
    out_came, out_parts = advance(out_steps, out_came)
    attended_heads, lses, parts = [], [], []
    value_t = value.T
    for head in range(heads):
        one_head, lse = attention_forward(query, key, value_t, at, head)
        if head == 0:
            (*out_came, query), one_head = pin([*out_came, query], one_head)
            out_came, out_parts = advance(out_steps, out_came)
        if head == 1:
            (parts[0],), one_head = pin([parts[0]], one_head)
        attended_heads.append(one_head)
        lses.append(lse)
        stored_head = one_head if direct else take_blocks(one_head, stored_to_place)
        parts.append(swap_ctx(stored_head.reshape(ctx_count, tok_count, HEAD_DIM))[::repeat])
    if out_parts is None:
        out_came, parts[-1] = pin(out_came, parts[-1]) if heads == 1 else (out_came, parts[-1])
        out_parts = finish(out_steps, out_came)
    out_parts = out_parts.reshape(ctx_count, dp_count, shard, D)
    out_full = (
        jnp.stack(
            [lax.dynamic_index_in_dim(out_parts, ctx_index ^ i, 0, False) for i in range(ctx_count)],
            axis=1,
        )
    ).reshape(D, D)
    parts, out_full = pin(parts, out_full)
    attended_parts = jnp.stack(parts, axis=2).reshape(head_sets, tok_count, width)
    attended = attended_parts.transpose(1, 0, 2).reshape(tok_count, D)
    first_sum = tokens + dot(attended, out_full)
    scale_two = rms_scale(first_sum)
    normed_two = (first_sum * scale_two * gain_two).astype(low)
    logits = dot_nt(normed_two, mix_router)
    mix_mine = jax.nn.sigmoid(logits[:, 0:1])
    chosen = code.T >= 0
    masked = jnp.where(chosen, logits[:, 1:], masked_score)
    raised = jnp.where(chosen, jnp.exp(masked - jnp.max(masked, axis=1, keepdims=True)), 0.0)
    gates_mine = raised / jnp.sum(raised, axis=1, keepdims=True)
    narrow = jnp.concatenate([mix_mine.T, gates_mine.T, code.astype(full)], axis=0)
    narrow = jnp.pad(narrow, ((0, -narrow.shape[0] % 8), (0, 0)))
    all_normed, narrow_all = gather_now([normed_two], narrow, 1, 75)
    all_normed = all_normed.reshape(group_len, D)
    mix_all = narrow_all[:, 0].reshape(group_len, 1)
    gate_mine = lax.dynamic_index_in_dim(narrow_all, ctx_index + 1, 1, keepdims=False)
    code_mine = lax.dynamic_index_in_dim(
        narrow_all, ctx_index + 1 + experts_total, 1, keepdims=False
    ).astype(jnp.int32)
    code_mine = jnp.where(code_mine < capacity, code_mine, -1)
    slot_rows = -(-capacity // 32) * 32
    expert_rows, slot_grads, hidden_low, gate_grad, up_grad, gate_share, dx_routed, out_routed = (
        routed_expert(
            all_normed, cot_all, code_mine, gate_mine, expert_gate, expert_up, expert_down, slot_rows
        )
    )
    grad_egate = ein("crd,crf->df", expert_rows, gate_grad).astype(low)
    grad_eup = ein("crd,crf->df", expert_rows, up_grad).astype(low)
    dx_routed, grad_egate, grad_eup = lax.optimization_barrier((dx_routed, grad_egate, grad_eup))
    sum_egate, sum_eup = over_dp(grad_egate, 0), over_dp(grad_eup, 0)
    mix_cot, shared_low, shared_dg, shared_du, mix_share, dx_odd, dx_even, out_odd, out_even = (
        shared_expert(
            all_normed, cot_all, mix_all, shared_gate, shared_up, shared_down,
            dx_routed, out_routed, tok_count,
        )
    )
    dx_steps = scatter_steps(dx_odd, dx_even)
    came = next(dx_steps)
    grad_edown = ein("crf,crd->fd", hidden_low, slot_grads).astype(low)
    came, grad_edown, sum_egate, shared_low, shared_dg, shared_du = pin(
        came, grad_edown, sum_egate, shared_low, shared_dg, shared_du
    )
    sum_edown = over_dp(grad_edown, 1)
    came, dx_mine = advance(dx_steps, came)
    grad_sdown = ein("tf,td->fd", shared_low, mix_cot).astype(low)
    grad_sgate = ein("tf,td->fd", shared_dg, all_normed).astype(low)
    came, grad_sdown, grad_sgate, shared_du = pin(came, grad_sdown, grad_sgate, shared_du)
    sum_sdown, sum_sgate = over_dp(grad_sdown, 0), over_dp(grad_sgate, 0)
    came, dx_mine = advance(dx_steps, came)
    grad_sup = ein("tf,td->fd", shared_du, all_normed).astype(low)
    came, grad_sup = pin(came, grad_sup)
    sum_sup = over_dp(grad_sup, 0)
    dx_mine = finish(dx_steps, came).astype(full)

    shares = jnp.stack([gate_share[:, 0], mix_share.reshape(ctx_count, tok_count)], axis=1)
    shares = swap_ctx(jnp.take(shares, partners, axis=0))
    gate_shares = shares[:, 0].T
    mix_grad = jnp.sum(shares[:, 1], axis=0)[:, None] * (1.0 - mix_mine)
    logit_grad = gate_shares - gates_mine * jnp.sum(gate_shares, axis=1, keepdims=True)
    narrow_low = logit_grad.astype(low)
    grad_narrow = jnp.concatenate(
        [
            jnp.sum(mix_grad * normed_two.astype(full), axis=0, keepdims=True),
            ein("te,td->ed", narrow_low, normed_two),
        ],
        axis=0,
    )
    (out_odd,), dx_mine = pin([out_odd], dx_mine)
    add_steps = scatter_steps(out_odd, out_even)
    came = next(add_steps)
    normed_grad = dx_mine + mix_grad * mix_row + dot(narrow_low, mix_router[1:])
    norm_grad_two, grad_gain_two = norm_back(first_sum, scale_two, gain_two, normed_grad)
    first_grad = cot_full + norm_grad_two
    first_low = first_grad.astype(low)
    attended_grad = dot_nt(first_low, out_full).astype(low)
    grad_out = ein("td,te->de", attended, first_low).astype(low)

    upstream_parts = attended_grad.reshape(tok_count, head_sets, heads, HEAD_DIM)
    upstream_parts = [upstream_parts[:, :, head].transpose(1, 0, 2) for head in range(heads)]
    if repeat > 1:
        upstream_parts = [jnp.repeat(part, repeat, axis=0) for part in upstream_parts]
    came, upstream_parts[0], sum_eup = pin(came, upstream_parts[0], sum_eup)
    came, added = advance(add_steps, came)
    upstreams = [swap_ctx(part).reshape(group_len, HEAD_DIM) for part in upstream_parts]
    (grad_out,), upstreams[0] = pin([grad_out], upstreams[0])
    grad_out = grad_out.reshape(dp_count, ctx_count, shard, D)

    def out_rows_of(first):
        return jnp.concatenate(
            [
                lax.dynamic_index_in_dim(grad_out, ctx_index ^ m, 1, False).reshape(-1, D)
                for m in range(first, ctx_count, 2)
            ],
            axis=0,
        )

    wout_steps = scatter_steps(out_rows_of(1), out_rows_of(0))
    wout_came = next(wout_steps)
    key_t = key.T
    head_grads = []
    for head in range(heads):
        upstream = upstreams[head] if direct else take_blocks(upstreams[head], place_to_stored)
        grads = attention_backward(
            query, upstream, attended_heads[head], lses[head], key, key_t, value,
            cosine_wide, sine_wide, at, head,
        )
        grads = list(grads)
        if head == 0:
            (*wout_came, upstreams[-1]), grads[0] = pin([*wout_came, upstreams[-1]], grads[0])
            wout_came, wout = advance(wout_steps, wout_came)
        head_grads.append(grads)
    came, last, sum_edown = pin(came, head_grads[-1][0], sum_edown)
    if wout is None:
        wout_came, last = pin(wout_came, last)
        wout_came, wout = advance(wout_steps, wout_came)
    head_grads[-1][0] = last
    came, added = advance(add_steps, came)
    qkv_grads = jnp.concatenate(
        [head_grads[head][kind] for kind in range(3) for head in range(heads)], axis=1
    )
    if repeat > 1:
        qkv_grads = jnp.where(ctx_index % repeat == 0, qkv_grads, jnp.zeros_like(qkv_grads))
    grad_qkv = ein("td,te->de", normed_sorted, qkv_grads).astype(low)
    bias_sums = jnp.sum(qkv_grads.astype(full), axis=0).reshape(3, width)
    grad_bias = lax.dynamic_update_slice_in_dim(
        jnp.zeros((3, D), full), bias_sums, my_heads, 1
    )
    grad_qkv, qkv_grads = lax.optimization_barrier((grad_qkv, qkv_grads))
    odd_one, even_one, gain_sums = unproject(
        qkv_grads, stored_near, w_qkv, normed_sorted, per_device
    )
    grad_gain_one = gain_sums[0] / gain_one[0]
    came, odd_one = pin(came, odd_one)
    added = finish(add_steps, came)
    layer_out = first_sum + added.astype(full)
    wout_came, odd_one = pin(wout_came, odd_one)
    wout = finish(wout_steps, wout_came)
    (wout,), odd_one, sum_sdown = pin([wout], odd_one, sum_sdown)
    qkv_rows = lax.psum_scatter(
        grad_qkv.reshape(dp_count, ctx_count, shard, 3 * width),
        "dp",
        scatter_dimension=0,
        tiled=True,
    )[0]
    wout_rows = lax.psum_scatter(
        wout.reshape(dp_count, shard, D), "dp", scatter_dimension=0, tiled=True
    )[0]
    dx_one = scatter_now(odd_one, even_one, 2)
    (sum_sgate, sum_sup, qkv_rows, wout_rows), dx_one = pin(
        [sum_sgate, sum_sup, qkv_rows, wout_rows], dx_one
    )
    norm_grad_one, _ = norm_back(tokens, scale_one, gain_one, dx_one)
    input_grad = first_grad + norm_grad_one

    qkv_mine = swap_ctx(qkv_rows)[::repeat].astype(full)
    qkv_mine = qkv_mine.reshape(head_sets, shard, 3, width).transpose(2, 1, 0, 3).reshape(3, shard, D)
    grad_wout = wout_rows.astype(full)
    small_grads = jnp.concatenate(
        [grad_gain_one[None], grad_bias, grad_gain_two[None], grad_narrow], axis=0
    )
    small_grads = small_grads.reshape(-1, dp_count, ctx_count, shard).transpose(2, 1, 0, 3)
    small_grads = jnp.sum(swap_ctx(small_grads), axis=0)
    small_grads = jnp.sum(
        lax.all_to_all(small_grads, "dp", split_axis=0, concat_axis=0, tiled=True), axis=0
    ).T

    return (
        layer_out.astype(low)[None],
        input_grad[None],
        small_grads[:, 0],
        qkv_mine[0],
        small_grads[:, 1],
        qkv_mine[1],
        small_grads[:, 2],
        qkv_mine[2],
        small_grads[:, 3],
        grad_wout,
        small_grads[:, 4],
        small_grads[:, 6:],
        sum_egate.astype(full)[None],
        sum_eup.astype(full)[None],
        sum_edown.astype(full)[None],
        sum_sgate.astype(full).T,
        sum_sup.astype(full).T,
        sum_sdown.astype(full),
        small_grads[:, 5],
    )


def solution(mesh):
    rows = P("dp", "ctx", None)
    flat = P(("dp", "ctx"))
    lines = P(("dp", "ctx"), None)
    columns = P(None, ("dp", "ctx"))
    deep = P("ctx", "dp", None)
    down = P("ctx", None, "dp")
    in_specs = (
        (rows, flat, lines, flat, lines, flat, lines, flat, lines, flat, lines)
        + (deep, deep, down, columns, columns, lines, flat)
        + (rows, rows, P("dp", None), rows)
    )
    out_specs = (
        (rows, rows, flat, lines, flat, lines, flat, lines, flat, lines, flat, lines)
        + (deep, deep, down, columns, columns, lines, flat)
    )
    return jax.shard_map(
        on_device, mesh=mesh, in_specs=in_specs, out_specs=out_specs, check_vma=False
    )
```

```python
import functools

import jax
import jax.numpy as jnp
import numpy as np
from jax import lax
from jax.experimental import pallas as pl
from jax.experimental.pallas import tpu as pltpu
from jax.sharding import PartitionSpec as P

D = 2048
HEADS = 16
HEAD_DIM = 128
TOP_K = 4
CONT = 256
PROMPT = 2048

rope_base = 1000000.0
epsilon = 1e-06
masked_score = -1e30
log2_e = 1.4426950408889634
low = jnp.bfloat16
full = jnp.float32


def dot(left, right):
    return jnp.dot(left, right, preferred_element_type=full)


def dot_nt(left, right):
    return lax.dot_general(left, right, (((1,), (1,)), ((), ())), preferred_element_type=full)


def ein(spec, left, right):
    return jnp.einsum(spec, left, right, preferred_element_type=full)


def rotate(values, cosine, sine):
    middle = values.shape[-1] // 2
    leading = values[..., :middle]
    trailing = values[..., middle:]
    return jnp.concatenate(
        [leading * cosine - trailing * sine, trailing * cosine + leading * sine], axis=-1
    )


def rope_tables(rows):
    places = np.arange(rows)
    turned = np.where(places < PROMPT, places, PROMPT + (places - PROMPT) % CONT)
    frequency = rope_base ** (-2.0 * np.arange(HEAD_DIM // 2, dtype=np.float64) / HEAD_DIM)
    angles = turned.astype(np.float64)[:, None] * frequency[None, :]
    cosine, sine = np.cos(angles), np.sin(angles)
    wide = np.concatenate([cosine, cosine], axis=1), np.concatenate([-sine, sine], axis=1)
    return tuple(jnp.asarray(table.astype(np.float32)) for table in wide)


def rms_scale(values):
    return lax.rsqrt(jnp.mean(values * values, axis=-1, keepdims=True) + epsilon)


def norm_back(values, scale_rows, gain_row, upstream):
    weighted = upstream * gain_row
    grad_gain = jnp.sum(upstream * values * scale_rows, axis=0)
    grad_values = scale_rows * weighted - values * scale_rows**3 * jnp.mean(
        weighted * values, axis=-1, keepdims=True
    )
    return (grad_values, grad_gain)


def silu_parts(values):
    sig_value = jax.nn.sigmoid(values)
    return (values * sig_value, sig_value * (1.0 + values * (1.0 - sig_value)))


def cost(microseconds):
    return pl.CostEstimate(
        flops=int(microseconds * 1.1e9),
        bytes_accessed=int(microseconds * 3.3e6),
        transcendentals=0,
    )


WIDE = 4


def attend_tiles(index, chunk, carry):
    whole = jnp.minimum(index, PROMPT // CONT)
    wide = whole // WIDE
    carry = lax.fori_loop(
        0, wide, lambda step, c: chunk(step * (WIDE * CONT), WIDE * CONT, False, c), carry
    )
    carry = lax.fori_loop(
        wide * WIDE, whole, lambda step, c: chunk(step * CONT, CONT, False, c), carry
    )
    return chunk(index * CONT, CONT, True, carry)


def turn(values, cosine, sine):
    half = HEAD_DIM // 2
    swapped = jnp.concatenate([values[:, half:], values[:, :half]], axis=1)
    return values * cosine + swapped * sine


def project_kernel(
    place_ref, x_ref, gain_ref, w_ref, bias_ref, cos_ref, sin_ref, normed_ref, q_ref, k_ref, v_ref
):
    values = x_ref[0].astype(full)
    scale = lax.rsqrt(jnp.mean(values * values, axis=1, keepdims=True) + epsilon)
    normed = (values * scale * gain_ref[...]).astype(low)
    normed_ref[...] = normed
    width = q_ref.shape[1]
    projected = dot(normed, w_ref[...]) + bias_ref[...]
    cosine, sine = cos_ref[...], sin_ref[...]
    for start in range(0, width, HEAD_DIM):
        for kind, out in ((0, q_ref), (1, k_ref)):
            column = kind * width + start
            head = projected[:, column : column + HEAD_DIM]
            out[:, start : start + HEAD_DIM] = turn(head, cosine, sine).astype(low)
    v_ref[...] = projected[:, 2 * width :].astype(low)


def project(x_blocks, places, gain, weight, bias, cosine, sine):
    count, rows, _ = x_blocks.shape
    width = bias.shape[1] // 3
    at_place = lambda g, place: (place[g], 0)
    whole = lambda g, place: (0, 0)
    tile = pl.BlockSpec((rows, width), at_place)
    head = jax.ShapeDtypeStruct((count * rows, width), low)
    return pl.pallas_call(
        project_kernel,
        grid_spec=pltpu.PrefetchScalarGridSpec(
            num_scalar_prefetch=1,
            grid=(count,),
            in_specs=[
                pl.BlockSpec((1, rows, D), lambda g, place: (g, 0, 0)),
                pl.BlockSpec((1, D), whole),
                pl.BlockSpec((D, 3 * width), whole),
                pl.BlockSpec((1, 3 * width), whole),
                pl.BlockSpec((rows, HEAD_DIM), at_place),
                pl.BlockSpec((rows, HEAD_DIM), at_place),
            ],
            out_specs=[pl.BlockSpec((rows, D), at_place), tile, tile, tile],
        ),
        out_shape=[jax.ShapeDtypeStruct((count * rows, D), low), head, head, head],
        compiler_params=pltpu.CompilerParams(vmem_limit_bytes=40 * 2**20),
        cost_estimate=cost(24),
        name="project",
    )(places, x_blocks, gain, weight, bias, cosine, sine)


def unproject_kernel(place_ref, grad_ref, w_ref, normed_ref, odd_ref, even_ref, gain_ref):
    step = pl.program_id(0)
    middle = pl.num_programs(0) // 2
    total = dot_nt(grad_ref[...], w_ref[...])
    gain_part = jnp.sum(total * normed_ref[...].astype(full), axis=0, keepdims=True)

    @pl.when(step == 0)
    def _():
        gain_ref[...] = jnp.zeros_like(gain_ref)

    gain_ref[...] += gain_part

    @pl.when(step < middle)
    def _():
        odd_ref[...] = total.astype(low)

    @pl.when(step >= middle)
    def _():
        even_ref[...] = total.astype(low)


def unproject(grads, places, weight, normed, per_device):
    count = places.shape[0]
    rows = grads.shape[0] // count
    width = grads.shape[1]
    middle = count // 2

    def at_place(g, place):
        block = odd_first(g // per_device, count // per_device) * per_device + g % per_device
        return (place[block], 0)

    shape = jax.ShapeDtypeStruct((middle * rows, D), low)
    return pl.pallas_call(
        unproject_kernel,
        grid_spec=pltpu.PrefetchScalarGridSpec(
            num_scalar_prefetch=1,
            grid=(count,),
            in_specs=[
                pl.BlockSpec((rows, width), at_place),
                pl.BlockSpec((D, width), lambda g, place: (0, 0)),
                pl.BlockSpec((rows, D), at_place),
            ],
            out_specs=[
                pl.BlockSpec((rows, D), lambda g, place: (jnp.minimum(g, middle - 1), 0)),
                pl.BlockSpec((rows, D), lambda g, place: (jnp.maximum(g - middle, 0), 0)),
                pl.BlockSpec((1, D), lambda g, place: (0, 0)),
            ],
        ),
        out_shape=[shape, shape, jax.ShapeDtypeStruct((1, D), full)],
        compiler_params=pltpu.CompilerParams(vmem_limit_bytes=40 * 2**20),
        cost_estimate=cost(20),
        name="unproject",
    )(places, grads, weight, normed)


def dot_tn(left, right):
    return lax.dot_general(left, right, (((0,), (0,)), ((), ())), preferred_element_type=full)


def expert_kernel(
    normed_ref, cot_ref, code_ref, gate_ref, wg_ref, wu_ref, wd_ref,
    rows_ref, sg_ref, act_ref, dg_ref, du_ref, share_ref, dx_ref, out_ref,
):
    slots = rows_ref.shape[1]
    tok = normed_ref.shape[0]
    hits = code_ref[0] == lax.broadcasted_iota(jnp.int32, (slots, tok), 0)
    table_full = jnp.where(hits, 1.0, 0.0)
    gated = jnp.where(hits, gate_ref[0], 0.0)
    table = table_full.astype(low)
    rows = dot(table, normed_ref[...]).astype(low)
    rows_ref[0] = rows
    slot_gate = jnp.sum(gated, axis=1, keepdims=True)
    slot_grad = (dot(table, cot_ref[...]) * slot_gate).astype(low)
    sg_ref[0] = slot_grad
    gate = dot(rows, wg_ref[...])
    up = dot(rows, wu_ref[...])
    hidden = dot_nt(slot_grad, wd_ref[...])
    silu, slope = silu_parts(gate)
    act_full = silu * up
    act = act_full.astype(low)
    act_ref[0] = act
    dg = (hidden * up * slope).astype(low)
    du = (hidden * silu).astype(low)
    dg_ref[0] = dg
    du_ref[0] = du
    slot_share = jnp.sum(hidden * act_full, axis=1, keepdims=True)
    share_ref[0] = jnp.sum(table_full * slot_share, axis=0, keepdims=True)
    slot_dx = (dot_nt(dg, wg_ref[...]) + dot_nt(du, wu_ref[...])).astype(low)
    dx_ref[...] = dot_tn(table, slot_dx).astype(low)
    expert_y = dot(act, wd_ref[...]).astype(low)
    out_ref[...] = dot_tn(gated.astype(low), expert_y).astype(low)


def routed_expert(all_normed, cot_all, code, gate, w_gate, w_up, w_down, slots):
    count, tok = code.shape
    ff = w_gate.shape[1]
    chunk = pl.BlockSpec((tok, D), lambda m: (m, 0))
    line = pl.BlockSpec((1, 1, tok), lambda m: (m, 0, 0))

    def fixed(array):
        return pl.BlockSpec(array.shape, lambda m: (0, 0), pipeline_mode=pl.Buffered(1))

    def per_slot(last):
        return pl.BlockSpec((1, slots, last), lambda m: (m, 0, 0))

    def shape(*dims, dtype=low):
        return jax.ShapeDtypeStruct(dims, dtype)

    return pl.pallas_call(
        expert_kernel,
        grid=(count,),
        in_specs=[chunk, chunk, line, line, fixed(w_gate), fixed(w_up), fixed(w_down)],
        out_specs=[per_slot(D), per_slot(D), per_slot(ff), per_slot(ff), per_slot(ff), line, chunk, chunk],
        out_shape=[
            shape(count, slots, D),
            shape(count, slots, D),
            shape(count, slots, ff),
            shape(count, slots, ff),
            shape(count, slots, ff),
            shape(count, 1, tok, dtype=full),
            shape(count * tok, D),
            shape(count * tok, D),
        ],
        compiler_params=pltpu.CompilerParams(vmem_limit_bytes=60 * 2**20),
        cost_estimate=cost(140),
        name="routed_expert",
    )(all_normed, cot_all, code[:, None, :], gate[:, None, :], w_gate, w_up, w_down)


def shared_kernel(
    normed_ref, cot_ref, mix_ref, wg_ref, wu_ref, wd_ref, dxe_ref, oute_ref,
    mixcot_ref, act_ref, dg_ref, du_ref, share_ref, dx_odd, dx_even, out_odd, out_even,
):
    step = pl.program_id(0)
    middle = pl.num_programs(0) // 2
    normed = normed_ref[...]
    mix = mix_ref[...]
    mix_cot = (mix * cot_ref[...].astype(full)).astype(low)
    mixcot_ref[...] = mix_cot
    gate = dot_nt(normed, wg_ref[...])
    up = dot_nt(normed, wu_ref[...])
    hidden = dot_nt(mix_cot, wd_ref[...])
    silu, slope = silu_parts(gate)
    act_full = silu * up
    act = act_full.astype(low)
    act_ref[...] = act
    dg = (hidden * up * slope).astype(low)
    du = (hidden * silu).astype(low)
    dg_ref[...] = dg
    du_ref[...] = du
    share_ref[...] = jnp.sum(hidden * act_full, axis=1, keepdims=True)
    dx = dot(dg, wg_ref[...]) + dot(du, wu_ref[...]) + dxe_ref[...].astype(full)
    out = mix * dot(act, wd_ref[...]) + oute_ref[...].astype(full)

    @pl.when(step < middle)
    def _():
        dx_odd[...] = dx.astype(low)
        out_odd[...] = out.astype(low)

    @pl.when(step >= middle)
    def _():
        dx_even[...] = dx.astype(low)
        out_even[...] = out.astype(low)


def shared_expert(all_normed, cot_all, mix, w_gate_t, w_up_t, w_down, dx_routed, out_routed, tok):
    rows = all_normed.shape[0]
    ff = w_down.shape[0]
    count = rows // tok
    middle = count // 2
    chunk = pl.BlockSpec((tok, D), lambda g: (odd_first(g, count), 0))
    narrow = pl.BlockSpec((tok, ff), lambda g: (odd_first(g, count), 0))
    column = pl.BlockSpec((tok, 1), lambda g: (odd_first(g, count), 0))
    odd = pl.BlockSpec((tok, D), lambda g: (jnp.minimum(g, middle - 1), 0))
    even = pl.BlockSpec((tok, D), lambda g: (jnp.maximum(g - middle, 0), 0))
    fixed = pl.BlockSpec((ff, D), lambda g: (0, 0), pipeline_mode=pl.Buffered(1))
    narrow_shape = jax.ShapeDtypeStruct((rows, ff), low)
    half_shape = jax.ShapeDtypeStruct((rows // 2, D), low)
    return pl.pallas_call(
        shared_kernel,
        grid=(count,),
        in_specs=[chunk, chunk, column, fixed, fixed, fixed, chunk, chunk],
        out_specs=[chunk, narrow, narrow, narrow, column, odd, even, odd, even],
        out_shape=[
            jax.ShapeDtypeStruct((rows, D), low),
            narrow_shape,
            narrow_shape,
            narrow_shape,
            jax.ShapeDtypeStruct((rows, 1), full),
            half_shape,
            half_shape,
            half_shape,
            half_shape,
        ],
        compiler_params=pltpu.CompilerParams(vmem_limit_bytes=60 * 2**20),
        cost_estimate=cost(103),
        name="shared_expert",
    )(all_normed, cot_all, mix, w_gate_t, w_up_t, w_down, dx_routed, out_routed)


def forward_kernel(at_ref, q_ref, k_ref, vt_ref, o_ref, lse_ref):
    index = pl.program_id(0)
    query = q_ref[...]
    score_scale = HEAD_DIM ** (-0.5) * log2_e

    def chunk(start, size, diagonal, carry):
        highest, total, acc = carry
        start = pl.multiple_of(start, CONT)
        scores = dot_nt(k_ref[pl.ds(start, size), :], query) * score_scale
        if diagonal:
            keys = lax.broadcasted_iota(jnp.int32, scores.shape, 0)
            queries = lax.broadcasted_iota(jnp.int32, scores.shape, 1)
            scores = jnp.where(keys <= queries, scores, masked_score)
        newest = jnp.maximum(highest, jnp.max(scores, axis=0, keepdims=True))
        weights = jnp.exp2(scores - newest)
        shrink = jnp.exp2(highest - newest)
        total = total * shrink + jnp.sum(weights, axis=0, keepdims=True)
        acc = acc * shrink + dot(vt_ref[:, pl.ds(start, size)], weights.astype(low))
        return (newest, total, acc)

    highest, total, acc = attend_tiles(
        index,
        chunk,
        (
            jnp.full((1, CONT), masked_score, full),
            jnp.zeros((1, CONT), full),
            jnp.zeros((HEAD_DIM, CONT), full),
        ),
    )
    o_ref[...] = (acc / total).T.astype(low)
    lse_ref[...] = highest + jnp.log2(total)


def attention_forward(query, key, value_t, at, head):
    rows = query.shape[0]
    return pl.pallas_call(
        forward_kernel,
        grid_spec=pltpu.PrefetchScalarGridSpec(
            num_scalar_prefetch=1,
            grid=(rows // CONT,),
            in_specs=[
                pl.BlockSpec((CONT, HEAD_DIM), lambda i, at: (i, head)),
                pl.BlockSpec((rows, HEAD_DIM), lambda i, at: (0, head)),
                pl.BlockSpec((HEAD_DIM, rows), lambda i, at: (head, 0)),
            ],
            out_specs=[
                pl.BlockSpec((CONT, HEAD_DIM), lambda i, at: (at[i], 0)),
                pl.BlockSpec((1, CONT), lambda i, at: (0, i)),
            ],
        ),
        out_shape=[
            jax.ShapeDtypeStruct((rows, HEAD_DIM), low),
            jax.ShapeDtypeStruct((1, rows), full),
        ],
        compiler_params=pltpu.CompilerParams(vmem_limit_bytes=32 * 2**20),
        cost_estimate=cost(30),
        name="attend_forward",
    )(at, query, key, value_t)


def backward_kernel(
    at_ref, q_ref, do_ref, o_ref, lse_ref, k_ref, kt_ref, v_ref, cos_ref, sin_ref,
    dq_ref, dk_ref, dv_ref, dk_sum, dv_sum,
):
    index = pl.program_id(0)
    query = q_ref[...]
    upstream = do_ref[...]
    lse = lse_ref[...]
    product = upstream.astype(full) * o_ref[...].astype(full)
    delta = jnp.sum(product.T, axis=0, keepdims=True)
    scale = HEAD_DIM ** (-0.5)
    span_now = pl.ds(pl.multiple_of(index * CONT, CONT), CONT)

    @pl.when(index == 0)
    def _():
        dk_sum[...] = jnp.zeros_like(dk_sum)
        dv_sum[...] = jnp.zeros_like(dv_sum)

    def chunk(start, size, diagonal, acc):
        start = pl.multiple_of(start, CONT)
        span = pl.ds(start, size)
        scores = dot_nt(k_ref[span, :], query) * (scale * log2_e) - lse
        if diagonal:
            keys = lax.broadcasted_iota(jnp.int32, scores.shape, 0)
            queries = lax.broadcasted_iota(jnp.int32, scores.shape, 1)
            scores = jnp.where(keys <= queries, scores, masked_score)
        probs = jnp.exp2(scores)
        prob_grad = dot_nt(v_ref[span, :], upstream)
        score_grad = (probs * (prob_grad - delta)).astype(low)
        dv_sum[span, :] += dot(probs.astype(low), upstream)
        dk_sum[span, :] += dot(score_grad, query)
        return acc + dot(kt_ref[:, span], score_grad)

    acc = attend_tiles(index, chunk, jnp.zeros((HEAD_DIM, CONT), full))
    dq_ref[...] = turn(acc.T * scale, cos_ref[span_now, :], -sin_ref[span_now, :]).astype(low)

    @pl.when(index == pl.num_programs(0) - 1)
    def _():
        def finish(step, carry):
            span = pl.ds(pl.multiple_of(step * CONT, CONT), CONT)
            dk_ref[span, :] = turn(
                dk_sum[span, :] * scale, cos_ref[span, :], -sin_ref[span, :]
            ).astype(low)
            dv_ref[span, :] = dv_sum[span, :].astype(low)
            return carry

        lax.fori_loop(0, pl.num_programs(0), finish, 0)


def attention_backward(query, upstream, attended, lse, key, key_t, value, cosine, sine, at, head):
    rows = query.shape[0]
    tile = pl.BlockSpec((CONT, HEAD_DIM), lambda i, at: (i, head))
    stored = pl.BlockSpec((CONT, HEAD_DIM), lambda i, at: (at[i], 0))
    whole = pl.BlockSpec((rows, HEAD_DIM), lambda i, at: (0, head))
    table = pl.BlockSpec((rows, HEAD_DIM), lambda i, at: (0, 0))
    grad = jax.ShapeDtypeStruct((rows, HEAD_DIM), low)
    return pl.pallas_call(
        backward_kernel,
        grid_spec=pltpu.PrefetchScalarGridSpec(
            num_scalar_prefetch=1,
            grid=(rows // CONT,),
            in_specs=[
                tile,
                stored,
                stored,
                pl.BlockSpec((1, CONT), lambda i, at: (0, i)),
                whole,
                pl.BlockSpec((HEAD_DIM, rows), lambda i, at: (head, 0)),
                whole,
                table,
                table,
            ],
            out_specs=[pl.BlockSpec((CONT, HEAD_DIM), lambda i, at: (i, 0)), table, table],
            scratch_shapes=[
                pltpu.VMEM((rows, HEAD_DIM), full),
                pltpu.VMEM((rows, HEAD_DIM), full),
            ],
        ),
        out_shape=[grad, grad, grad],
        compiler_params=pltpu.CompilerParams(vmem_limit_bytes=48 * 2**20),
        cost_estimate=cost(38),
        name="attend_backward",
    )(at, query, upstream, attended, lse, key, key_t, value, cosine, sine)


def take_blocks(rows, order):
    count = order.shape[0]
    blocked = rows.reshape(count, rows.shape[0] // count, *rows.shape[1:])
    return jnp.concatenate(
        [lax.dynamic_index_in_dim(blocked, order[i], 0, keepdims=False) for i in range(count)], axis=0
    )


def bit_orders(count):
    bits = [1 << i for i in range(1, count.bit_length() - 1)]
    return bits, bits[::-1]


def exchange(values, bit, count):
    return lax.ppermute(values, "ctx", [(i, i ^ bit) for i in range(count)])


def gather_plan(count):
    plan = []
    orders = bit_orders(count)
    held = [[0], [0]]
    for depth in range(len(orders[0])):
        sends = [[(half, m, orders[half][depth]) for m in held[half]] for half in (0, 1)]
        plan += [send for pair in zip(*sends) for send in pair]
        for half in (0, 1):
            held[half] = held[half] + [m ^ orders[half][depth] for m in held[half]]
    return plan, [(half, m, 1) for m in held[0] for half in (0, 1)]


def gather_kernel(count, big, with_small, *refs):
    ins = refs[: big + with_small]
    outs = refs[big + with_small : 2 * (big + with_small)]
    send_sems, recv_sems, own_sems = refs[2 * (big + with_small) :]
    me = lax.axis_index("ctx")
    dp = lax.axis_index("dp")
    bits = bit_orders(count)[0] + [1]
    rows = ins[0].shape[0] // 2
    barrier = pltpu.get_barrier_semaphore()
    for bit in bits:
        pl.semaphore_signal(
            barrier, inc=1, device_id=(dp, me ^ bit), device_id_type=pl.DeviceIdType.MESH
        )
    pl.semaphore_wait(barrier, len(bits))
    own, spots = [], []
    for a in range(big):
        for half in (0, 1):
            own.append(ins[a].at[pl.ds(half * rows, rows)])
            spots.append([outs[a].at[2 * m + half] for m in range(count)])
    if with_small:
        own.append(ins[big])
        spots.append([outs[big].at[m] for m in range(count)])
    local = [
        pltpu.make_async_copy(own[t], spots[t][0], own_sems.at[t]) for t in range(len(own))
    ]
    for copy in local:
        copy.start()
    copies = {}
    waited = set()

    def send(track, m, bit):
        if m and (track, m) not in waited:
            copies[(track, m)].wait_recv()
            waited.add((track, m))
        lands = track * count + (m ^ bit)
        copy = pltpu.make_async_remote_copy(
            src_ref=spots[track][m] if m else own[track],
            dst_ref=spots[track][m ^ bit],
            send_sem=send_sems.at[lands],
            recv_sem=recv_sems.at[lands],
            device_id=(dp, me ^ bit),
            device_id_type=pl.DeviceIdType.MESH,
        )
        copy.start()
        copies[(track, m ^ bit)] = copy

    plan_far, plan_near = gather_plan(count)
    far, near = [], []
    if with_small:
        far += [(2 * big, m, bit) for half, m, bit in plan_far if half == 0]
        near += [(2 * big, m, bit) for half, m, bit in plan_near if half == 0]
    for half, m, bit in plan_far:
        far += [(2 * a + half, m, bit) for a in range(big)]
    for half, m, bit in plan_near:
        near += [(2 * a + half, m, bit) for a in range(big)]
    done = set()
    for entry in far:
        send(*entry)
        for other in near:
            if other not in done and (other[1] == 0 or (other[0], other[1]) in waited):
                done.add(other)
                send(*other)
    for other in near:
        if other not in done:
            send(*other)
    for key, copy in copies.items():
        if key not in waited:
            copy.wait_recv()
    for copy in copies.values():
        copy.wait_send()
    for copy in local:
        copy.wait()


def gather_now(arrays, small, collective_id, microseconds):
    count = lax.axis_size("ctx")
    shapes = [
        jax.ShapeDtypeStruct((2 * count, x.shape[0] // 2, x.shape[1]), x.dtype) for x in arrays
    ]
    inputs = list(arrays)
    if small is not None:
        inputs.append(small)
        shapes.append(jax.ShapeDtypeStruct((count, *small.shape), small.dtype))
    tracks = len(arrays) + len(inputs)
    return pl.pallas_call(
        functools.partial(gather_kernel, count, len(arrays), len(inputs) - len(arrays)),
        in_specs=[pl.BlockSpec(memory_space=pl.ANY)] * len(shapes),
        out_specs=[pl.BlockSpec(memory_space=pltpu.HBM)] * len(arrays)
        + [pl.BlockSpec(memory_space=pl.ANY)] * (len(inputs) - len(arrays)),
        out_shape=shapes,
        scratch_shapes=[
            pltpu.SemaphoreType.DMA((tracks * count,)),
            pltpu.SemaphoreType.DMA((tracks * count,)),
            pltpu.SemaphoreType.DMA((tracks,)),
        ],
        compiler_params=pltpu.CompilerParams(
            collective_id=collective_id, has_side_effects=True, vmem_limit_bytes=58 * 2**20
        ),
        cost_estimate=cost(microseconds),
        name="gather_rows",
    )(*inputs)


def split_rows(values, parts):
    rows = values.shape[0] // parts
    return [values[i * rows : (i + 1) * rows] for i in range(parts)]


def pin(arrays, *others):
    held = lax.optimization_barrier((tuple(arrays), *others))
    return (list(held[0]), *held[1:])


def gather_steps(values):
    count = lax.axis_size("ctx")
    orders = bit_orders(count)
    names, held = [[0], [0]], [[piece] for piece in split_rows(values, 2)]
    for depth in range(len(orders[0])):
        came = []
        for half in (0, 1):
            sent = jnp.concatenate(held[half], axis=0) if depth else held[half][0]
            came.append(exchange(sent, orders[half][depth], count))
        came = yield came
        for half in (0, 1):
            held[half] = held[half] + split_rows(came[half], len(held[half]))
            names[half] = names[half] + [m ^ orders[half][depth] for m in names[half]]
    halves = [dict(zip(names[half], held[half])) for half in (0, 1)]
    own = jnp.stack(
        [jnp.concatenate([half[m] for half in halves], axis=0) for m in range(0, count, 2)]
    )
    (other,) = yield [exchange(own, 1, count)]
    return jnp.stack([own, other], axis=1).reshape(count * values.shape[0], *values.shape[1:])


def add_low(left, right):
    return (left.astype(full) + right.astype(full)).astype(low)


def scatter_steps(odd, even):
    count = lax.axis_size("ctx")
    parts = count // 2
    (came,) = yield [exchange(odd, 1, count)]
    pairs = list(zip(split_rows(even, parts), split_rows(came, parts)))
    orders = bit_orders(count)
    held = [
        {
            2 * n: add_low(split_rows(left, 2)[half], split_rows(right, 2)[half])
            for n, (left, right) in enumerate(pairs)
        }
        for half in (0, 1)
    ]
    for depth in range(len(orders[0])):
        names, came = [], []
        for half in (0, 1):
            bit = orders[half][depth]
            names.append([m for m in held[half] if m & bit])
            sent = [held[half][m] for m in names[half]]
            sent = jnp.concatenate(sent, axis=0) if len(sent) > 1 else sent[0]
            came.append(exchange(sent, bit, count))
        came = yield came
        for half in (0, 1):
            bit = orders[half][depth]
            pieces = split_rows(came[half], len(names[half]))
            held[half] = {
                m ^ bit: add_low(held[half][m ^ bit], x) for m, x in zip(names[half], pieces)
            }
    return jnp.concatenate([half[0] for half in held], axis=0)


def scatter_kernel(count, odd_ref, even_ref, out_ref, sums, came, near_sems, far_send, far_recv):
    me = lax.axis_index("ctx")
    dp = lax.axis_index("dp")
    orders = bit_orders(count)
    bits = orders[0] + [1]
    parts = count // 2
    rows = even_ref.shape[2]
    tile = min(32, rows)
    barrier = pltpu.get_barrier_semaphore()
    for bit in bits:
        pl.semaphore_signal(
            barrier, inc=1, device_id=(dp, me ^ bit), device_id_type=pl.DeviceIdType.MESH
        )
    pl.semaphore_wait(barrier, len(bits))
    first = sorted(range(parts), key=lambda n: -bin(n).count("1"))
    near = {}
    for n in first:
        near[n] = pltpu.make_async_remote_copy(
            src_ref=odd_ref.at[n],
            dst_ref=sums.at[n],
            send_sem=near_sems.at[0, n],
            recv_sem=near_sems.at[1, n],
            device_id=(dp, me ^ 1),
            device_id_type=pl.DeviceIdType.MESH,
        )
        near[n].start()

    def add(into, left, right):
        def body(step, carry):
            span = pl.ds(pl.multiple_of(step * tile, tile), tile)
            total = left[span, :].astype(full) + right[span, :].astype(full)
            into[span, :] = total.astype(into.dtype)
            return carry

        lax.fori_loop(0, rows // tile, body, 0)

    far = []
    used = [0, 0]

    def send(half, n, bit):
        place = used[half]
        used[half] += 1
        copy = pltpu.make_async_remote_copy(
            src_ref=sums.at[n, half],
            dst_ref=came.at[half, place],
            send_sem=far_send.at[half, place],
            recv_sem=far_recv.at[half, place],
            device_id=(dp, me ^ bit),
            device_id_type=pl.DeviceIdType.MESH,
        )
        copy.start()
        far.append(copy)
        return copy, place

    pending = [{}, {}]
    for n in first:
        near[n].wait_recv()
        for half in (0, 1):
            add(sums.at[n, half], sums.at[n, half], even_ref.at[n, half])
            bit = orders[half][0]
            if 2 * n & bit:
                pending[half][n] = send(half, n, bit)
    depth_count = len(orders[0])
    for depth in range(depth_count):
        later = [{}, {}]
        waiting = [(half, n) for k in range(parts) for half in (0, 1) for n in list(pending[half])[k : k + 1]]
        for half, n in waiting:
            copy, place = pending[half][n]
            keep = n ^ (orders[half][depth] >> 1)
            copy.wait_recv()
            if depth + 1 == depth_count:
                add(out_ref.at[half], sums.at[keep, half], came.at[half, place])
            else:
                add(sums.at[keep, half], sums.at[keep, half], came.at[half, place])
                bit = orders[half][depth + 1]
                if 2 * keep & bit:
                    later[half][keep] = send(half, keep, bit)
        pending = later
    for n in first:
        near[n].wait_send()
    for copy in far:
        copy.wait_send()


def scatter_now(odd, even, collective_id):
    count = lax.axis_size("ctx")
    parts = count // 2
    rows = odd.shape[0] // parts // 2
    shape = (parts, 2, rows, odd.shape[1])
    out = pl.pallas_call(
        functools.partial(scatter_kernel, count),
        in_specs=[pl.BlockSpec(memory_space=pl.ANY), pl.BlockSpec(memory_space=pltpu.VMEM)],
        out_specs=pl.BlockSpec(memory_space=pltpu.VMEM),
        out_shape=jax.ShapeDtypeStruct((2, rows, odd.shape[1]), full),
        scratch_shapes=[
            pltpu.VMEM(shape, low),
            pltpu.VMEM((2, parts - 1, rows, odd.shape[1]), low),
            pltpu.SemaphoreType.DMA((2, parts)),
            pltpu.SemaphoreType.DMA((2, parts - 1)),
            pltpu.SemaphoreType.DMA((2, parts - 1)),
        ],
        compiler_params=pltpu.CompilerParams(
            collective_id=collective_id, has_side_effects=True, vmem_limit_bytes=40 * 2**20
        ),
        cost_estimate=cost(90),
        name="scatter_rows",
    )(odd.reshape(shape), even.reshape(shape))
    return out.reshape(2 * rows, odd.shape[1])


def advance(steps, came):
    try:
        return (steps.send(came), None)
    except StopIteration as stop:
        return (None, stop.value)


def finish(steps, came):
    value = None
    while value is None:
        came, value = advance(steps, came)
    return value


def over_dp(grad, dim):
    return lax.psum_scatter(grad, "dp", scatter_dimension=dim, tiled=True)


def odd_first(step, count):
    return lax.rem(2 * step + 1, count + 1)


def swap_ctx(values):
    return lax.all_to_all(values, "ctx", split_axis=0, concat_axis=0, tiled=True)


def on_device(
    hidden_in,
    in_gain,
    w_query,
    b_query,
    w_key,
    b_key,
    w_value,
    b_value,
    w_out,
    ffn_gain,
    w_router,
    exp_gate,
    exp_up,
    exp_down,
    sh_gate,
    sh_up,
    sh_down,
    sh_mix,
    routes,
    priority,
    blocks,
    cotangent,
):
    both = ("dp", "ctx")
    ctx_count = lax.axis_size("ctx")
    ctx_index = lax.axis_index("ctx")
    dp_count = lax.axis_size("dp")
    dp_index = lax.axis_index("dp")
    tokens_low = hidden_in[0]
    tokens = tokens_low.astype(full)
    cot_low = cotangent[0]
    cot_full = cotangent[0].astype(full)
    tok_count = tokens.shape[0]
    group_len = tok_count * ctx_count
    shard = w_query.shape[0]
    experts_total = ctx_count * exp_gate.shape[0]
    capacity = 5 * tok_count * TOP_K // (4 * experts_total)
    repeat = max(1, ctx_count // HEADS)
    heads = max(1, HEADS // ctx_count)
    width = heads * HEAD_DIM
    head_sets = HEADS // heads

    def by_heads(weight):
        parts = weight.reshape(shard, head_sets, width).transpose(1, 0, 2)
        return jnp.repeat(parts, repeat, axis=0) if repeat > 1 else parts

    small = jnp.concatenate(
        [
            jnp.stack([in_gain, b_query, b_key, b_value, ffn_gain, sh_mix], axis=1),
            w_router,
        ],
        axis=1,
    )
    small_count = small.shape[1]
    small = jnp.pad(small, ((0, 0), (0, -small_count % HEAD_DIM)))
    qkv_parts = swap_ctx(
        jnp.concatenate(
            [
                by_heads(w_query),
                by_heads(w_key),
                by_heads(w_value),
                jnp.broadcast_to(small[None], (ctx_count, *small.shape)),
            ],
            axis=2,
        )
    )
    w_qkv = lax.all_gather(
        qkv_parts.reshape(ctx_count * shard, qkv_parts.shape[2]), "dp", axis=0, tiled=True
    )
    small_all = w_qkv[:, 3 * width : 3 * width + small_count].astype(full).T
    gain_one, gain_two, mix_row = small_all[0:1], small_all[4:5], small_all[5:6]
    mix_router = small_all[5:].astype(low)
    partners = jnp.arange(ctx_count, dtype=jnp.int32) ^ ctx_index
    out_around = jnp.stack(
        [w_out]
        + [
            lax.ppermute(w_out, "dp", [(i, (i + k) % dp_count) for i in range(dp_count)])
            for k in range(1, dp_count)
        ]
    )
    x_blocks, cot_all = gather_now([tokens_low, cot_low], None, 0, 145)
    cot_all = cot_all.reshape(group_len, D)
    out_mine = jnp.concatenate(
        [lax.dynamic_index_in_dim(out_around, (dp_index + dp_count - p) % dp_count, 0, False)
            for p in range(dp_count)], axis=0
    )
    (out_mine,), x_blocks = pin([out_mine], x_blocks)
    out_steps = gather_steps(out_mine)
    out_came = next(out_steps)
    shared_gate, shared_up, shared_down = (
        lax.all_gather(sh_gate.T, "dp", axis=0, tiled=True),
        lax.all_gather(sh_up.T, "dp", axis=0, tiled=True),
        lax.all_gather(sh_down, "dp", axis=0, tiled=True),
    )
    expert_gate, expert_up, expert_down = (
        lax.all_gather(exp_gate[0], "dp", axis=0, tiled=True),
        lax.all_gather(exp_up[0], "dp", axis=0, tiled=True),
        lax.all_gather(exp_down[0], "dp", axis=1, tiled=True),
    )

    route_ids = routes[0]
    flat_ids = route_ids.reshape(-1)
    order = priority[0, 0]
    earlier = (flat_ids[:, None] == flat_ids[None, :]) & (order[None, :] < order[:, None])
    ranks = jnp.sum(earlier.astype(jnp.int32), axis=1).reshape(route_ids.shape)
    expert_grid = jnp.arange(experts_total, dtype=jnp.int32)
    route_hits = route_ids[None, :, :] == expert_grid[:, None, None]
    code = jnp.sum(jnp.where(route_hits, ranks[None] + 1, 0), axis=2) - 1

    stored_to_place = blocks[0]
    block_count = stored_to_place.shape[0]
    block_grid = jnp.arange(block_count, dtype=jnp.int32)
    place_to_stored = jnp.sum(
        jnp.where(stored_to_place[None, :] == block_grid[:, None], block_grid[None, :], 0), axis=1
    )
    per_device = block_count // ctx_count
    near = (block_grid // per_device ^ ctx_index) * per_device + block_grid % per_device
    stored_near = jnp.sum(
        jnp.where(near[:, None] == block_grid[None, :], stored_to_place[None, :], 0), axis=1
    )
    cosine_wide, sine_wide = rope_tables(group_len)
    my_heads = (ctx_index // repeat) * width
    scale_one = rms_scale(tokens)
    bias = lax.dynamic_slice_in_dim(small_all[1:4], my_heads, width, 1).reshape(1, 3 * width)
    normed_sorted, query, key, value = project(
        x_blocks, stored_near, gain_one, w_qkv, bias, cosine_wide, sine_wide
    )
    tiles = group_len // CONT
    direct = block_count == tiles
    at = place_to_stored if direct else jnp.arange(tiles, dtype=jnp.int32)
    out_came, query = pin(out_came, query)
    out_came, out_parts = advance(out_steps, out_came)
    attended_heads, lses, parts = [], [], []
    value_t = value.T
    for head in range(heads):
        one_head, lse = attention_forward(query, key, value_t, at, head)
        if head == 0:
            (*out_came, query), one_head = pin([*out_came, query], one_head)
            out_came, out_parts = advance(out_steps, out_came)
        if head == 1:
            (parts[0],), one_head = pin([parts[0]], one_head)
        attended_heads.append(one_head)
        lses.append(lse)
        stored_head = one_head if direct else take_blocks(one_head, stored_to_place)
        parts.append(swap_ctx(stored_head.reshape(ctx_count, tok_count, HEAD_DIM))[::repeat])
    if out_parts is None:
        out_came, parts[-1] = pin(out_came, parts[-1]) if heads == 1 else (out_came, parts[-1])
        out_parts = finish(out_steps, out_came)
    out_parts = out_parts.reshape(ctx_count, dp_count, shard, D)
    out_full = (
        jnp.stack(
            [lax.dynamic_index_in_dim(out_parts, ctx_index ^ i, 0, False) for i in range(ctx_count)],
            axis=1,
        )
    ).reshape(D, D)
    parts, out_full = pin(parts, out_full)
    attended_parts = jnp.stack(parts, axis=2).reshape(head_sets, tok_count, width)
    attended = attended_parts.transpose(1, 0, 2).reshape(tok_count, D)
    first_sum = tokens + dot(attended, out_full)
    scale_two = rms_scale(first_sum)
    normed_two = (first_sum * scale_two * gain_two).astype(low)
    logits = dot_nt(normed_two, mix_router)
    mix_mine = jax.nn.sigmoid(logits[:, 0:1])
    chosen = code.T >= 0
    masked = jnp.where(chosen, logits[:, 1:], masked_score)
    raised = jnp.where(chosen, jnp.exp(masked - jnp.max(masked, axis=1, keepdims=True)), 0.0)
    gates_mine = raised / jnp.sum(raised, axis=1, keepdims=True)
    narrow = jnp.concatenate([mix_mine.T, gates_mine.T, code.astype(full)], axis=0)
    narrow = jnp.pad(narrow, ((0, -narrow.shape[0] % 8), (0, 0)))
    all_normed, narrow_all = gather_now([normed_two], narrow, 1, 75)
    all_normed = all_normed.reshape(group_len, D)
    mix_all = narrow_all[:, 0].reshape(group_len, 1)
    gate_mine = lax.dynamic_index_in_dim(narrow_all, ctx_index + 1, 1, keepdims=False)
    code_mine = lax.dynamic_index_in_dim(
        narrow_all, ctx_index + 1 + experts_total, 1, keepdims=False
    ).astype(jnp.int32)
    code_mine = jnp.where(code_mine < capacity, code_mine, -1)
    slot_rows = -(-capacity // 32) * 32
    expert_rows, slot_grads, hidden_low, gate_grad, up_grad, gate_share, dx_routed, out_routed = (
        routed_expert(
            all_normed, cot_all, code_mine, gate_mine, expert_gate, expert_up, expert_down, slot_rows
        )
    )
    grad_egate = ein("crd,crf->df", expert_rows, gate_grad).astype(low)
    grad_egate, up_grad = lax.optimization_barrier((grad_egate, up_grad))
    grad_eup = ein("crd,crf->df", expert_rows, up_grad).astype(low)
    sum_egate = over_dp(grad_egate, 0)
    dx_routed, grad_eup = lax.optimization_barrier((dx_routed, grad_eup))
    sum_eup = over_dp(grad_eup, 0)
    mix_cot, shared_low, shared_dg, shared_du, mix_share, dx_odd, dx_even, out_odd, out_even = (
        shared_expert(
            all_normed, cot_all, mix_all, shared_gate, shared_up, shared_down,
            dx_routed, out_routed, tok_count,
        )
    )
    dx_steps = scatter_steps(dx_odd, dx_even)
    came = next(dx_steps)
    grad_edown = ein("crf,crd->fd", hidden_low, slot_grads).astype(low)
    came, grad_edown, sum_egate, shared_low, shared_dg, shared_du = pin(
        came, grad_edown, sum_egate, shared_low, shared_dg, shared_du
    )
    sum_edown = over_dp(grad_edown, 1)
    came, dx_mine = advance(dx_steps, came)
    grad_sdown = ein("tf,td->fd", shared_low, mix_cot).astype(low)
    grad_sgate = ein("tf,td->fd", shared_dg, all_normed).astype(low)
    came, grad_sdown, grad_sgate, shared_du = pin(came, grad_sdown, grad_sgate, shared_du)
    sum_sdown, sum_sgate = over_dp(grad_sdown, 0), over_dp(grad_sgate, 0)
    came, dx_mine = advance(dx_steps, came)
    grad_sup = ein("tf,td->fd", shared_du, all_normed).astype(low)
    came, grad_sup = pin(came, grad_sup)
    sum_sup = over_dp(grad_sup, 0)
    dx_mine = finish(dx_steps, came).astype(full)

    shares = jnp.stack([gate_share[:, 0], mix_share.reshape(ctx_count, tok_count)], axis=1)
    shares = swap_ctx(jnp.take(shares, partners, axis=0))
    gate_shares = shares[:, 0].T
    mix_grad = jnp.sum(shares[:, 1], axis=0)[:, None] * (1.0 - mix_mine)
    logit_grad = gate_shares - gates_mine * jnp.sum(gate_shares, axis=1, keepdims=True)
    narrow_low = logit_grad.astype(low)
    grad_narrow = jnp.concatenate(
        [
            jnp.sum(mix_grad * normed_two.astype(full), axis=0, keepdims=True),
            ein("te,td->ed", narrow_low, normed_two),
        ],
        axis=0,
    )
    (out_odd,), dx_mine = pin([out_odd], dx_mine)
    add_steps = scatter_steps(out_odd, out_even)
    came = next(add_steps)
    normed_grad = dx_mine + mix_grad * mix_row + dot(narrow_low, mix_router[1:])
    norm_grad_two, grad_gain_two = norm_back(first_sum, scale_two, gain_two, normed_grad)
    first_grad = cot_full + norm_grad_two
    first_low = first_grad.astype(low)
    attended_grad = dot_nt(first_low, out_full).astype(low)
    grad_out = ein("td,te->de", attended, first_low).astype(low)

    upstream_parts = attended_grad.reshape(tok_count, head_sets, heads, HEAD_DIM)
    upstream_parts = [upstream_parts[:, :, head].transpose(1, 0, 2) for head in range(heads)]
    if repeat > 1:
        upstream_parts = [jnp.repeat(part, repeat, axis=0) for part in upstream_parts]
    came, upstream_parts[0], sum_eup = pin(came, upstream_parts[0], sum_eup)
    came, added = advance(add_steps, came)
    upstreams = [swap_ctx(part).reshape(group_len, HEAD_DIM) for part in upstream_parts]
    (grad_out,), upstreams[0] = pin([grad_out], upstreams[0])
    grad_out = grad_out.reshape(dp_count, ctx_count, shard, D)

    def out_rows_of(first):
        return jnp.concatenate(
            [
                lax.dynamic_index_in_dim(grad_out, ctx_index ^ m, 1, False).reshape(-1, D)
                for m in range(first, ctx_count, 2)
            ],
            axis=0,
        )

    wout_steps = scatter_steps(out_rows_of(1), out_rows_of(0))
    wout_came = next(wout_steps)
    key_t = key.T
    head_grads = []
    for head in range(heads):
        upstream = upstreams[head] if direct else take_blocks(upstreams[head], place_to_stored)
        grads = attention_backward(
            query, upstream, attended_heads[head], lses[head], key, key_t, value,
            cosine_wide, sine_wide, at, head,
        )
        grads = list(grads)
        if head == 0:
            (*wout_came, upstreams[-1]), grads[0] = pin([*wout_came, upstreams[-1]], grads[0])
            wout_came, wout = advance(wout_steps, wout_came)
        head_grads.append(grads)
    last = head_grads[-1][0]
    if wout is None:
        wout_came, last = pin(wout_came, last)
        wout_came, wout = advance(wout_steps, wout_came)
    came, last, sum_edown = pin(came, last, sum_edown)
    head_grads[-1][0] = last
    came, added = advance(add_steps, came)
    qkv_grads = jnp.concatenate(
        [head_grads[head][kind] for kind in range(3) for head in range(heads)], axis=1
    )
    if repeat > 1:
        qkv_grads = jnp.where(ctx_index % repeat == 0, qkv_grads, jnp.zeros_like(qkv_grads))
    grad_qkv = ein("td,te->de", normed_sorted, qkv_grads).astype(low)
    bias_sums = jnp.sum(qkv_grads.astype(full), axis=0).reshape(3, width)
    grad_bias = lax.dynamic_update_slice_in_dim(
        jnp.zeros((3, D), full), bias_sums, my_heads, 1
    )
    grad_qkv, qkv_grads = lax.optimization_barrier((grad_qkv, qkv_grads))
    odd_one, even_one, gain_sums = unproject(
        qkv_grads, stored_near, w_qkv, normed_sorted, per_device
    )
    grad_gain_one = gain_sums[0] / gain_one[0]
    came, odd_one = pin(came, odd_one)
    added = finish(add_steps, came)
    layer_out = first_sum + added.astype(full)
    wout_came, odd_one = pin(wout_came, odd_one)
    wout = finish(wout_steps, wout_came)
    (wout,), odd_one, sum_sdown = pin([wout], odd_one, sum_sdown)
    qkv_rows = lax.psum_scatter(
        grad_qkv.reshape(dp_count, ctx_count, shard, 3 * width),
        "dp",
        scatter_dimension=0,
        tiled=True,
    )[0]
    wout_rows = lax.psum_scatter(
        wout.reshape(dp_count, shard, D), "dp", scatter_dimension=0, tiled=True
    )[0]
    dx_one = scatter_now(odd_one, even_one, 2)
    (sum_sgate, sum_sup, qkv_rows, wout_rows), dx_one = pin(
        [sum_sgate, sum_sup, qkv_rows, wout_rows], dx_one
    )
    norm_grad_one, _ = norm_back(tokens, scale_one, gain_one, dx_one)
    input_grad = first_grad + norm_grad_one

    qkv_mine = swap_ctx(qkv_rows)[::repeat].astype(full)
    qkv_mine = qkv_mine.reshape(head_sets, shard, 3, width).transpose(2, 1, 0, 3).reshape(3, shard, D)
    grad_wout = wout_rows.astype(full)
    small_grads = jnp.concatenate(
        [grad_gain_one[None], grad_bias, grad_gain_two[None], grad_narrow], axis=0
    )
    small_grads = small_grads.reshape(-1, dp_count, ctx_count, shard).transpose(2, 1, 0, 3)
    small_grads = jnp.sum(swap_ctx(small_grads), axis=0)
    small_grads = jnp.sum(
        lax.all_to_all(small_grads, "dp", split_axis=0, concat_axis=0, tiled=True), axis=0
    ).T

    return (
        layer_out.astype(low)[None],
        input_grad[None],
        small_grads[:, 0],
        qkv_mine[0],
        small_grads[:, 1],
        qkv_mine[1],
        small_grads[:, 2],
        qkv_mine[2],
        small_grads[:, 3],
        grad_wout,
        small_grads[:, 4],
        small_grads[:, 6:],
        sum_egate.astype(full)[None],
        sum_eup.astype(full)[None],
        sum_edown.astype(full)[None],
        sum_sgate.astype(full).T,
        sum_sup.astype(full).T,
        sum_sdown.astype(full),
        small_grads[:, 5],
    )


def solution(mesh):
    rows = P("dp", "ctx", None)
    flat = P(("dp", "ctx"))
    lines = P(("dp", "ctx"), None)
    columns = P(None, ("dp", "ctx"))
    deep = P("ctx", "dp", None)
    down = P("ctx", None, "dp")
    in_specs = (
        (rows, flat, lines, flat, lines, flat, lines, flat, lines, flat, lines)
        + (deep, deep, down, columns, columns, lines, flat)
        + (rows, rows, P("dp", None), rows)
    )
    out_specs = (
        (rows, rows, flat, lines, flat, lines, flat, lines, flat, lines, flat, lines)
        + (deep, deep, down, columns, columns, lines, flat)
    )
    return jax.shard_map(
        on_device, mesh=mesh, in_specs=in_specs, out_specs=out_specs, check_vma=False
    )
```
